128 devices in a mesh: gx: 8 (over x, core), gy: 16 (over z, y).
Axes of the slice: x: 4, y: 4, z: 4, core: 2. Of those that a mesh axis runs over, the one named last changes fastest.
Arguments:
- grad_cells: float32 [3, 32, 128, 2048], P(None, None, 'gx', 'gy'), may hold values from -6 to 6
- grad_segs: float32 [3, 131072], P(None, ('gx', 'gy')), may hold values from -6 to 6
- cell_diag: float32 [3, 3, 32, 128, 2048], P(None, None, None, 'gx', 'gy'), may hold values from -1.2 to 8, as said below
- cell_off: float32 [6, 3, 3, 32, 128, 2048], P(None, None, None, None, 'gx', 'gy'), may hold values from -1.2 to 1.2
- seg_diag: float32 [3, 3, 131072], P(None, None, ('gx', 'gy')), may hold values from -1.2 to 8, as said below
- seg_chain: float32 [2, 3, 3, 131072], P(None, None, None, ('gx', 'gy')), may hold values from -1.8 to 1.8
- seg_len: int32 [4096], P(('gx', 'gy')), may hold values from 8 to 32
- perf_device: int32 [524288, 1], P(('gx', 'gy')), may hold values from 0 to 127; in each aligned block of 4096 rows (0 to 4095, 4096 to 8191, ...) at most 64 rows name the same one
- perf_local: int32 [524288], P(('gx', 'gy')), may hold values from 0 to 65535
- perf_seg: int32 [524288], P(('gx', 'gy')), may hold values from 0 to 1023, as said below
- perf_blocks: float32 [2, 3, 3, 524288], P(None, None, None, ('gx', 'gy')), may hold values from -2.4 to 2.4
Outputs:
- adjoint_cells: float32 [3, 32, 128, 2048], P(None, None, 'gx', 'gy')
- adjoint_segs: float32 [3, 131072], P(None, ('gx', 'gy'))
- residual_cells: float32 [3, 32, 128, 2048], P(None, None, 'gx', 'gy')
- residual_segs: float32 [3, 131072], P(None, ('gx', 'gy'))
The draws below stay inside these ranges and needn't reach their ends.
Inputs may be any that keep to these rules, and one draw needn't show every extreme that they name: `perf_device`: in the rows of one device (aligned blocks of 4096 rows) no device index appears more than 64 times. `perf_seg`: perforation r names slot w * 32 + k of device r // 4096, where w is one of that device's wells and k is below that well's seg_len. `cell_diag`: diagonal entries lie in 4 to 8, the others in -1.2 to 1.2. `seg_diag`: diagonal entries lie in 4 to 8, the others in -1.2 to 1.2.
All inputs are finite; a program needn't handle non-finite values.
Results may differ from the reference program's by a relative error of at most 0.0003.
Values sent between devices are 32-bit elements; how exact they have to be, the bound alone decides.
A program may use at most 256 MiB of HBM per device.

```python
import math
import jax
import jax.numpy as jnp
import numpy as np

CX = 16
CY = 128
NZ = 32
WELL_DEV = 32
SEG_MAX = 32
PERF_DEV = 4096
ITERS = 2
NX = 128
NY = 2048
CELLS_DEV = 65536
SEGS_DEV = 1024
WELLS = 4096
SEGS = 131072
PERFS = 524288
CAP = 64
N_GX = 8
N_GY = 16
DEVICES = 128


def dominant(uniform_draw):
    identity = (jnp.arange(3)[:, None] == jnp.arange(3)[None, :]).reshape((3, 3) + (1,) * (uniform_draw.ndim - 2))
    return jnp.where(identity, 4.0 + 4.0 * uniform_draw, -1.2 + 2.4 * uniform_draw).astype(jnp.float32)


def well_lengths(key):
    drawn = jax.random.randint(key, (WELLS,), SEG_MAX // 4, SEG_MAX + 1)
    position = jnp.arange(WELLS)
    drawn = jnp.where(position == 0, SEG_MAX // 4, drawn)
    drawn = jnp.where(position == WELL_DEV - 1, SEG_MAX, drawn)
    return drawn.astype(jnp.int32)


def draw_cell_diag(key, part):
    key = jax.random.fold_in(key, 11)
    uniform_draw = jax.random.uniform(key, (3, 3, NZ, NX, NY), jnp.float32)
    return dominant(uniform_draw)


def draw_seg_diag(key, part):
    key = jax.random.fold_in(key, 13)
    uniform_draw = jax.random.uniform(key, (3, 3, SEGS), jnp.float32)
    return dominant(uniform_draw)


def draw_seg_len(key, part):
    return well_lengths(key)


def draw_perf_seg(key, part):
    lengths = well_lengths(key)
    key = jax.random.fold_in(key, 17)
    first_key, second_key = jax.random.split(key)
    well_local = jax.random.randint(first_key, (PERFS,), 0, WELL_DEV)
    row_index = jnp.arange(PERFS)
    within = row_index % PERF_DEV
    device_index = row_index // PERF_DEV
    topmost = (within == 0) & (device_index == 0)
    well_local = jnp.where(topmost, WELL_DEV - 1, jnp.where(within == 1, 0, well_local))
    well_global = device_index * WELL_DEV + well_local
    spread = jax.random.randint(second_key, (PERFS,), 0, 1 << 20)
    along = spread % lengths[well_global]
    along = jnp.where(topmost, SEG_MAX - 1, jnp.where(within == 1, 0, along))
    return (well_local * SEG_MAX + along).astype(jnp.int32)


def set_ends(array, own_key, low, largest):
    spot = [jax.random.randint(jax.random.fold_in(own_key, axis), (), 0, length) for axis, length in enumerate(array.shape)]
    main_axis = array.shape.index(max(array.shape))
    neighbour = spot[:main_axis] + [(spot[main_axis] + 1) % array.shape[main_axis]] + spot[main_axis + 1:]
    return array.at[tuple(spot)].set(low).at[tuple(neighbour)].set(largest)


def block_scale(stream_key, dims, shards, low, top_value):
    def one(dim, parts):
        heights = jax.random.uniform(jax.random.fold_in(jax.random.fold_in(stream_key, 6), dim), (parts,), jnp.float32, low / len(shards), top_value / len(shards))
        return jnp.repeat(jnp.exp(heights), dims[dim] // parts).reshape((-1,) + (1,) * (len(dims) - dim - 1))

    gain = one(*shards[0])
    for cut in shards[1:]:
        gain = gain * one(*cut)
    return gain


def assign_block(rng, own, number, rows, number_of, top, bound, lean):
    sequence = jax.random.permutation(rng, number_of)
    packed, ordinary = portions_of(number_of, rows * top, bound, lean, True), portions_of(number_of, rows * top, bound, lean, False)
    places = jnp.arange(number_of)

    def named(tallies, rotation):
        used = int((tallies > 0).sum())
        fixed = max(1, used // 4)
        moved = fixed + (places - fixed + rotation * (used - fixed)) % max(1, number_of - fixed)
        return jnp.zeros((number_of,), jnp.int32).at[sequence[jnp.where(places < fixed, places, moved)]].set(jnp.asarray(tallies, jnp.int32))

    tallies = jnp.where(number % 4 == 0, named(packed, number // 4), named(ordinary, number - number // 4 - 1))
    mixed = jax.random.permutation(jax.random.fold_in(own, 3), number_of)
    source_of, sink = mixed[0:number_of // 2 * 2:2], mixed[1:number_of // 2 * 2:2]
    slack = jnp.minimum(tallies[source_of] - 1, bound - tallies[sink]) // 2
    slack = jnp.where((source_of == sequence[0]) | (sink == sequence[0]) | (tallies[sink] == 0), 0, jnp.maximum(slack, 0))
    moved = jax.random.randint(jax.random.fold_in(own, 4), (number_of // 2,), 0, 1 << 20) % (slack + 1)
    tallies = tallies.at[source_of].add(-moved).at[sink].add(moved)
    items = jnp.searchsorted(jnp.cumsum(tallies), jnp.arange(rows * top), side="right").astype(jnp.int32)
    listing = items.reshape(top, rows).T
    listing = listing[jax.random.permutation(jax.random.fold_in(own, 1), rows)]
    rotation = jax.random.randint(jax.random.fold_in(own, 2), (rows, 1), 0, top)
    return jnp.take_along_axis(listing, (jnp.arange(top)[None, :] + rotation) % top, axis=1)


def portions_of(count, total, most, skew, full):
    loads = [(1 << 20) // math.isqrt(standing ** skew) + 1 for standing in range(1, count + 1)]
    largest = most if full else min(most, max(-(-total // count), total * loads[0] // sum(loads)))
    least = 1 if total - largest >= count - 1 else 0
    given, spare = [largest] + [least] * (count - 1), total - largest - least * (count - 1)
    while spare > 0:
        movable = [i for i in range(1, count) if given[i] < largest] or [i for i in range(1, count) if given[i] < most]
        mass, budget = sum([loads[i] for i in movable]), spare
        for i in movable:
            addition = min(most - given[i], max(1, budget * loads[i] // mass), spare)
            given[i] = given[i] + addition
            spare = spare - addition
    return np.array(given)


def centred(stream_key, extent, deviation, reach, pieces=(), kind=jnp.bfloat16):
    factor_of = block_scale(stream_key, extent, pieces, -0.22, 0.18) if pieces else 1.0
    array = jax.random.normal(stream_key, extent, jnp.float32) * deviation * factor_of
    return jnp.minimum(jnp.maximum(array, -reach), reach).astype(kind)


def setup_inputs(seed: int = 0) -> dict:
    splits = jax.random.split(jax.random.key(seed), 12)
    grad_cells = centred(splits[0], (3, NZ, NX, NY), 1.0, 6.0, ((2, 8), (3, 16)), jnp.float32)
    grad_segs = centred(splits[1], (3, SEGS), 1.0, 6.0, ((1, 128),), jnp.float32)
    cell_diag = draw_cell_diag(jax.random.fold_in(splits[11], 71), 0)
    cell_off = centred(splits[3], (6, 3, 3, NZ, NX, NY), 0.2, 1.2, ((4, 8), (5, 16)), jnp.float32)
    seg_diag = draw_seg_diag(jax.random.fold_in(splits[11], 71), 0)
    seg_chain = centred(splits[5], (2, 3, 3, SEGS), 0.3, 1.8, ((3, 128),), jnp.float32)
    seg_len = draw_seg_len(jax.random.fold_in(splits[11], 71), 0)
    perf_device_keys = jax.random.split(jax.random.fold_in(splits[7], 1), PERFS // PERF_DEV)
    perf_device_turns = jax.random.permutation(jax.random.fold_in(splits[7], 3), PERFS // PERF_DEV)
    perf_device = jax.vmap(lambda own, number: assign_block(jax.random.fold_in(splits[7], 2), own, number, PERF_DEV, DEVICES, 1, CAP, 2))(perf_device_keys, perf_device_turns).reshape((PERFS, 1))
    perf_local = set_ends(jax.random.randint(splits[8], (PERFS,), 0, CELLS_DEV), jax.random.fold_in(splits[8], 1), 0, CELLS_DEV - 1).astype(jnp.int32)
    perf_seg = draw_perf_seg(jax.random.fold_in(splits[11], 71), 0)
    perf_blocks = centred(splits[10], (2, 3, 3, PERFS), 0.4, 2.4, ((3, 128),), jnp.float32)
    return {"grad_cells": grad_cells, "grad_segs": grad_segs, "cell_diag": cell_diag, "cell_off": cell_off, "seg_diag": seg_diag, "seg_chain": seg_chain, "seg_len": seg_len, "perf_device": perf_device, "perf_local": perf_local, "perf_seg": perf_seg, "perf_blocks": perf_blocks}


def apply_transpose(blocks, vector):
    return jnp.sum(blocks * vector[:, None], axis=0)


def inverse_transpose(matrix):
    cofactor = [[matrix[(i + 1) % 3, (j + 1) % 3] * matrix[(i + 2) % 3, (j + 2) % 3]
                 - matrix[(i + 1) % 3, (j + 2) % 3] * matrix[(i + 2) % 3, (j + 1) % 3]
                 for j in range(3)] for i in range(3)]
    determinant = matrix[0, 0] * cofactor[0][0] + matrix[0, 1] * cofactor[0][1] + matrix[0, 2] * cofactor[0][2]
    return jnp.stack([jnp.stack(row_list) for row_list in cofactor]) / determinant


def apply_inverse(inverse, vector):
    return jnp.sum(inverse * vector[None], axis=1)


def cell_couple(adjoint, cell_diag, cell_off):
    result = apply_transpose(cell_diag, adjoint)
    moved = [apply_transpose(cell_off[direction], adjoint) for direction in range(6)]
    result = result.at[:, :, 1:, :].add(moved[0][:, :, :-1, :])
    result = result.at[:, :, :-1, :].add(moved[1][:, :, 1:, :])
    result = result.at[:, :, :, 1:].add(moved[2][:, :, :, :-1])
    result = result.at[:, :, :, :-1].add(moved[3][:, :, :, 1:])
    result = result.at[:, 1:].add(moved[4][:, :-1])
    result = result.at[:, :-1].add(moved[5][:, 1:])
    return result


def segment_couple(adjoint, seg_diag, seg_chain, well_count, seg_slots):
    result = apply_transpose(seg_diag, adjoint).reshape(3, well_count, seg_slots)
    lower = apply_transpose(seg_chain[0], adjoint).reshape(3, well_count, seg_slots)
    upper = apply_transpose(seg_chain[1], adjoint).reshape(3, well_count, seg_slots)
    result = result.at[:, :, :-1].add(lower[:, :, 1:])
    result = result.at[:, :, 1:].add(upper[:, :, :-1])
    return result.reshape(3, -1)


def to_blocks(field):
    return field.reshape(3, NZ, N_GX, CX, N_GY, CY).transpose(0, 2, 4, 1, 3, 5).reshape(3, -1)


def from_blocks(flat):
    return flat.reshape(3, N_GX, N_GY, NZ, CX, CY).transpose(0, 3, 1, 4, 2, 5).reshape(3, NZ, NX, NY)


def reference(grad_cells, grad_segs, cell_diag, cell_off, seg_diag, seg_chain, seg_len, perf_device, perf_local, perf_seg, perf_blocks):
    active = (jnp.arange(SEG_MAX, dtype=jnp.int32)[None, :] < seg_len[:, None]).reshape(-1).astype(jnp.float32)
    cell_ids = (perf_device[:, 0] * CELLS_DEV + perf_local).astype(jnp.int32)
    seg_ids = ((jnp.arange(PERFS, dtype=jnp.int32) // PERF_DEV) * SEGS_DEV + perf_seg).astype(jnp.int32)
    cell_inverse = inverse_transpose(cell_diag)
    seg_inverse = inverse_transpose(seg_diag)

    def couple(cells, segs):
        cell_out = to_blocks(cell_couple(cells, cell_diag, cell_off))
        seg_out = segment_couple(segs, seg_diag, seg_chain, WELLS, SEG_MAX)
        cell_out = cell_out.at[:, cell_ids].add(apply_transpose(perf_blocks[0], segs[:, seg_ids]))
        seg_out = seg_out.at[:, seg_ids].add(apply_transpose(perf_blocks[1], to_blocks(cells)[:, cell_ids]))
        return from_blocks(cell_out), seg_out

    adjoint_cells = apply_inverse(cell_inverse, grad_cells)
    adjoint_segs = active * apply_inverse(seg_inverse, grad_segs)
    for sweep in range(ITERS - 1):
        image_cells, image_segs = couple(adjoint_cells, adjoint_segs)
        adjoint_cells = adjoint_cells + apply_inverse(cell_inverse, grad_cells - image_cells)
        adjoint_segs = adjoint_segs + active * apply_inverse(seg_inverse, grad_segs - image_segs)
    image_cells, image_segs = couple(adjoint_cells, adjoint_segs)
    residual_cells = grad_cells - image_cells
    residual_segs = active * (grad_segs - image_segs)
    return adjoint_cells, adjoint_segs, residual_cells, residual_segs
```

```python
import jax
import jax.numpy as jnp
from jax import lax
from jax.experimental import pallas as pl
from jax.experimental.pallas import tpu as pltpu
from jax.sharding import PartitionSpec as P

MESH = pl.DeviceIdType.MESH
F32 = jnp.float32
BF16 = jnp.bfloat16
NT = (((1,), (1,)), ((), ()))
GX = 8
GY = 16
ND = GX * GY
NZ = 32
CX = 16
CY = 128
ROWS = NZ * CX
SEGS = 1024
SEG_MAX = 32
PERFS = 4096
KLO = 32
KHI = 2
WIDE = KHI * ND
SLOTS = KLO * WIDE
BUCKETS = 4
BROWS = ROWS // BUCKETS
CHUNK = 512
CHUNKS = SLOTS // CHUNK + BUCKETS
CROWS = 24
VMEM = pl.BlockSpec(memory_space=pltpu.VMEM)
ANY = pl.BlockSpec(memory_space=pl.ANY)


def rounded(x):
    return x.astype(BF16).astype(F32)


def halves(x):
    high = rounded(x)
    return high, x - high


def iota(shape, dim):
    return lax.broadcasted_iota(jnp.int32, shape, dim)


def one_hot(count, row, kind):
    hit = iota((count, row.shape[1]), 0) == row
    return hit.astype(F32).astype(kind)


def inverse_rows(matrix):
    cofactor = [
        [
            matrix[(i + 1) % 3][(j + 1) % 3] * matrix[(i + 2) % 3][(j + 2) % 3]
            - matrix[(i + 1) % 3][(j + 2) % 3] * matrix[(i + 2) % 3][(j + 1) % 3]
            for j in range(3)
        ]
        for i in range(3)
    ]
    determinant = (
        matrix[0][0] * cofactor[0][0]
        + matrix[0][1] * cofactor[0][1]
        + matrix[0][2] * cofactor[0][2]
    )
    return cofactor, 1.0 / determinant


def solve_rows(matrix, vector):
    cofactor, scale = inverse_rows(matrix)
    return [
        (cofactor[i][0] * vector[0] + cofactor[i][1] * vector[1] + cofactor[i][2] * vector[2])
        * scale
        for i in range(3)
    ]


def transposed_rows(matrix, vector):
    return [
        matrix[0][i] * vector[0] + matrix[1][i] * vector[1] + matrix[2][i] * vector[2]
        for i in range(3)
    ]


def seg_rows(ref):
    return [ref[j : j + 1, :] for j in range(3)]


def seg_matrix(ref):
    return [[ref[i, j : j + 1, :] for j in range(3)] for i in range(3)]


def active_row(seg_len_ref):
    lanes = iota((32, SEGS), 1)
    mine = (lanes // SEG_MAX) == iota((32, SEGS), 0)
    below = (lanes % SEG_MAX) < seg_len_ref[...]
    return jnp.sum(jnp.where(mine & below, 1.0, 0.0), axis=0, keepdims=True)


def seg_gather(values, seg_slots, lane_hot_ref, table_ref, out_ref):
    for c in range(3):
        high, low = halves(values[c])
        for h in range(8):
            table_ref[c * 8 + h : c * 8 + h + 1, 0:128] = high[:, 128 * h : 128 * (h + 1)]
            table_ref[c * 8 + h : c * 8 + h + 1, 128:256] = low[:, 128 * h : 128 * (h + 1)]
    table = table_ref[...].astype(BF16)

    def body(k, _):
        lanes = pl.ds(pl.multiple_of(k * WIDE, WIDE), WIDE)
        hot = lane_hot_ref[:, lanes]
        found = jnp.dot(table[:, :128], hot, preferred_element_type=F32) + jnp.dot(
            table[:, 128:], hot, preferred_element_type=F32
        )
        high = seg_slots[pl.ds(k, 1), :].astype(jnp.int32) >> 7
        pick = (iota((8, WIDE), 0) == high).astype(F32)
        for c in range(3):
            out_ref[pl.ds(c * KLO + k, 1), :] = jnp.sum(
                found[8 * c : 8 * c + 8] * pick, axis=0, keepdims=True
            )
        return 0

    lax.fori_loop(0, KLO, body, 0, unroll=4)


def seg_scatter(values_ref, seg_slots, lane_hot_ref, table_ref):
    def body(k, total):
        lanes = pl.ds(pl.multiple_of(k * WIDE, WIDE), WIDE)
        hot = lane_hot_ref[:, lanes]
        high = seg_slots[pl.ds(k, 1), :].astype(jnp.int32) >> 7
        pick = (iota((8, WIDE), 0) == high).astype(F32)
        left = []
        for c in range(3):
            left += [pick * part for part in halves(values_ref[pl.ds(c * KLO + k, 1), :])]
        return total + lax.dot_general(
            jnp.concatenate(left, axis=0).astype(BF16), hot, NT, preferred_element_type=F32
        )

    total = lax.fori_loop(0, KLO, body, jnp.zeros((48, 128), F32), unroll=4)
    rows = []
    for c in range(3):
        table_ref[0:8, 0:128] = total[16 * c : 16 * c + 8] + total[16 * c + 8 : 16 * c + 16]
        rows.append(
            jnp.concatenate([table_ref[h : h + 1, 0:128] for h in range(8)], axis=1)
        )
    return rows


def lane_hots(seg_slots, lane_hot_ref):
    def body(k, _):
        lanes = pl.ds(pl.multiple_of(k * WIDE, WIDE), WIDE)
        low = seg_slots[pl.ds(k, 1), :].astype(jnp.int32) & 127
        lane_hot_ref[:, lanes] = one_hot(128, low, BF16)
        return 0

    lax.fori_loop(0, KLO, body, 0, unroll=4)


def slot_terms(blocks, number, rows_ref, start):
    vector = [rows_ref[start + c * KLO : start + (c + 1) * KLO, :] for c in range(3)]
    out = []
    for i in range(3):
        total = None
        for j in range(3):
            at = (number * 9 + j * 3 + i) * KLO
            term = blocks[at : at + KLO, :] * vector[j]
            total = term if total is None else total + term
        out.append(total)
    return out


def everyone(act):
    gx = lax.axis_index("gx")
    gy = lax.axis_index("gy")
    me = gx * GY + gy

    def body(i, _):
        other = lax.rem(me + i, ND)
        act(other, (other // GY, lax.rem(other, GY)))
        return 0

    lax.fori_loop(1, ND, body, 0)


def greet():
    barrier = pltpu.get_barrier_semaphore()
    everyone(
        lambda other, place: pl.semaphore_signal(
            barrier, inc=1, device_id=place, device_id_type=MESH
        )
    )


def greeted():
    pl.semaphore_wait(pltpu.get_barrier_semaphore(), ND - 1)


class Exchange:
    def __init__(self, source, target, send_sem, recv_sem, own_sem):
        self.source, self.target = source, target
        self.send_sem, self.recv_sem, self.own_sem = send_sem, recv_sem, own_sem
        self.me = lax.axis_index("gx") * GY + lax.axis_index("gy")

    def own(self):
        return pltpu.make_async_copy(
            self.source.at[self.me], self.target.at[self.me], self.own_sem
        )

    def whole(self):
        return pltpu.make_async_remote_copy(
            src_ref=self.source.at[pl.ds(0, ND - 1)],
            dst_ref=self.target.at[pl.ds(0, ND - 1)],
            send_sem=self.send_sem,
            recv_sem=self.recv_sem,
            device_id=(lax.axis_index("gx"), lax.axis_index("gy")),
            device_id_type=MESH,
        )

    def start(self):
        self.own().start()
        everyone(
            lambda other, place: pltpu.make_async_remote_copy(
                src_ref=self.source.at[other],
                dst_ref=self.target.at[self.me],
                send_sem=self.send_sem,
                recv_sem=self.recv_sem,
                device_id=place,
                device_id_type=MESH,
            ).start()
        )

    def wait_recv(self):
        self.own().wait()
        self.whole().wait_recv()

    def wait_send(self):
        self.whole().wait_send()


class Halo:
    def __init__(self, x_out, x_in, y_out, y_in, send_sem, recv_sem):
        gx = lax.axis_index("gx")
        gy = lax.axis_index("gy")
        places = [
            (lax.rem(gx + 1, GX), gy),
            (lax.rem(gx + GX - 1, GX), gy),
            (gx, lax.rem(gy + 1, GY)),
            (gx, lax.rem(gy + GY - 1, GY)),
        ]
        pairs = [(x_out, x_in, 0), (x_out, x_in, 1), (y_out, y_in, 0), (y_out, y_in, 1)]
        self.copies = [
            pltpu.make_async_remote_copy(
                src_ref=a.at[n],
                dst_ref=b.at[n],
                send_sem=send_sem.at[at],
                recv_sem=recv_sem.at[at],
                device_id=place,
                device_id_type=MESH,
            )
            for at, ((a, b, n), place) in enumerate(zip(pairs, places))
        ]
        self.x_out, self.x_in, self.y_out, self.y_in = x_out, x_in, y_out, y_in

    def start(self):
        for copy in self.copies:
            copy.start()

    def wait_recv(self):
        for copy in self.copies:
            copy.wait_recv()

    def wait_send(self):
        for copy in self.copies:
            copy.wait_send()


def stencil(adjoint, diag_ref, off_ref, image_ref, halo, column_ref):
    for c in range(3):
        image_ref[c] = jnp.zeros((NZ + 2, CX, CY), F32)
    rows = iota((CX, CY), 0)
    lanes = iota((CX, CY), 1)

    def body(z, _):
        a = adjoint(z)
        own = transposed_rows([[diag_ref[j, i, z] for i in range(3)] for j in range(3)], a)
        moved = [
            transposed_rows([[off_ref[e, j, i, z] for i in range(3)] for j in range(3)], a)
            for e in range(6)
        ]
        columns = jnp.zeros((CX, CY), F32)
        for c in range(3):
            total = own[c]
            halo.x_out[0, c, pl.ds(z, 1), :] = moved[0][c][CX - 1 : CX]
            halo.x_out[1, c, pl.ds(z, 1), :] = moved[1][c][0:1]
            total += jnp.where(rows == 0, 0.0, pltpu.roll(moved[0][c], 1, 0))
            total += jnp.where(rows == CX - 1, 0.0, pltpu.roll(moved[1][c], CX - 1, 0))
            total += jnp.where(lanes == 0, 0.0, pltpu.roll(moved[2][c], 1, 1))
            total += jnp.where(lanes == CY - 1, 0.0, pltpu.roll(moved[3][c], CY - 1, 1))
            columns = jnp.where(lanes == c, pltpu.roll(moved[2][c], 1 + c, 1), columns)
            columns = jnp.where(lanes == 8 + c, pltpu.roll(moved[3][c], 8 + c, 1), columns)
            image_ref[c, z + 1] += total
            image_ref[c, z + 2] += moved[4][c]
            image_ref[c, z] += moved[5][c]
        column_ref[pl.ds(pl.multiple_of(z * CX, CX), CX), :] = columns
        return 0

    lax.fori_loop(0, NZ, body, 0, unroll=2)
    turned = column_ref[...].T
    halo.y_out[0] = turned[0:8]
    halo.y_out[1] = turned[8:16]
    halo.start()


def add_rims(image_ref, halo, column_ref):
    gx = lax.axis_index("gx")
    gy = lax.axis_index("gy")
    first_x = jnp.where(gx > 0, 1.0, 0.0)
    last_x = jnp.where(gx < GX - 1, 1.0, 0.0)
    first_y = jnp.where(gy > 0, 1.0, 0.0)
    last_y = jnp.where(gy < GY - 1, 1.0, 0.0)
    came = jnp.concatenate(
        [halo.y_in[0] * first_y, halo.y_in[1] * last_y, jnp.zeros((CY - 16, ROWS), F32)], axis=0
    )
    column_ref[...] = came.T
    rows = iota((CX, CY), 0)
    lanes = iota((CX, CY), 1)

    def body(z, _):
        columns = column_ref[pl.ds(pl.multiple_of(z * CX, CX), CX), :]
        for c in range(3):
            low = halo.x_in[0, c, pl.ds(z, 1), :] * first_x
            high = halo.x_in[1, c, pl.ds(z, 1), :] * last_x
            total = jnp.where(rows == 0, low, 0.0) + jnp.where(rows == CX - 1, high, 0.0)
            left = columns if c == 0 else pltpu.roll(columns, CY - c, 1)
            total += jnp.where(lanes == 0, left, 0.0)
            right = pltpu.roll(columns, CY - 1 - 8 - c, 1)
            total += jnp.where(lanes == CY - 1, right, 0.0)
            image_ref[c, z + 1] += total
        return 0

    lax.fori_loop(0, NZ, body, 0, unroll=2)


def rank_and_place(device_ref, x_ref, work_ref, total_ref):
    above = (iota((256, 256), 0) < iota((256, 256), 1)).astype(F32).astype(BF16)
    ones = jnp.ones((256, 256), BF16)
    carry = jnp.zeros((ND, 256), F32)
    for j in range(PERFS // 512):
        ranks = []
        for half in range(2):
            target = device_ref[:, 512 * j + 256 * half : 512 * j + 256 * (half + 1)]
            hit = one_hot(ND, target, F32)
            hit16 = hit.astype(BF16)
            before = jnp.dot(hit16, above, preferred_element_type=F32) + carry
            carry = carry + jnp.dot(hit16, ones, preferred_element_type=F32)
            ranks.append(jnp.sum(before * hit, axis=0, keepdims=True))
        rank = jnp.concatenate(ranks, axis=1).astype(jnp.int32)
        target = device_ref[:, 512 * j : 512 * (j + 1)]
        column_hot = one_hot(WIDE, target + ND * (rank >> 5), BF16)
        row_hot = one_hot(KLO, rank & (KLO - 1), F32)
        x = x_ref[:, 512 * j : 512 * (j + 1)]
        high, low = halves(x)
        for q in range(20):
            at = slice(q * KLO, (q + 1) * KLO)
            work_ref[0, at, :] = (row_hot * high[q : q + 1]).astype(BF16)
            work_ref[1, at, :] = (row_hot * low[q : q + 1]).astype(BF16)
        part = lax.dot_general(work_ref[0], column_hot, NT, preferred_element_type=F32)
        part += lax.dot_general(work_ref[1], column_hot, NT, preferred_element_type=F32)
        if j == 0:
            total_ref[...] = part
        else:
            total_ref[...] += part


def cells_at(ref, z):
    return [ref[c, z] for c in range(3)]


def first_kernel(
    grad_cells, grad_segs, diag, off, seg_diag, seg_len, device, local, seg, blocks,
    came, slots_out, adjoint_out, rest_out, adjoint_segs_out,
    x, work, slots, lane_hot, table, push, message, off_here, image,
    x_out, x_in, y_out, y_in, column,
    off_sem, send_sem, recv_sem, own_sem, halo_send, halo_recv,
):
    load = pltpu.make_async_copy(off, off_here, off_sem)
    load.start()
    greet()
    exchange = Exchange(message, came, send_sem, recv_sem, own_sem)
    halo = Halo(x_out, x_in, y_out, y_in, halo_send, halo_recv)
    x[0:1, :] = (local[...] + 1).astype(F32)
    x[1:2, :] = seg[...].astype(F32)
    for b in range(2):
        for j in range(3):
            at = 2 + 9 * b + 3 * j
            x[at : at + 3, :] = blocks[b, j]
    rank_and_place(device, x, work, slots)
    active = active_row(seg_len)
    adjoint_segs = [
        active * row for row in solve_rows(seg_matrix(seg_diag), seg_rows(grad_segs))
    ]
    for c in range(3):
        adjoint_segs_out[c : c + 1, :] = adjoint_segs[c]
    seg_slots = slots.at[pl.ds(KLO, KLO)]
    lane_hots(seg_slots, lane_hot)
    seg_gather(adjoint_segs, seg_slots, lane_hot, table, push)
    terms = slot_terms(slots.at[pl.ds(2 * KLO, 18 * KLO)], 0, push, 0)
    packed = jnp.concatenate([slots[0:KLO, :]] + terms, axis=0)
    for h in range(KHI):
        message[:, h, :] = packed[:, ND * h : ND * (h + 1)].T
    greeted()
    exchange.start()
    slots_out[...] = slots[KLO:, :]

    def begin(z, _):
        a = solve_rows(
            [[diag[i, j, z] for j in range(3)] for i in range(3)], cells_at(grad_cells, z)
        )
        for c in range(3):
            adjoint_out[c, z] = a[c]
        return 0

    lax.fori_loop(0, NZ, begin, 0, unroll=2)
    load.wait()
    stencil(lambda z: cells_at(adjoint_out, z), diag, off_here, image, halo, column)
    halo.wait_recv()
    add_rims(image, halo, column)
    for c in range(3):
        rest_out[c] = grad_cells[c] - image[c, 1 : NZ + 1]
    exchange.wait_recv()
    exchange.wait_send()
    halo.wait_send()


def place_slots(index, place_ref, starts):
    row = (index - 1) >> 7
    parts = []
    for b in range(BUCKETS):
        parts.append(((index > 0) & ((row // BROWS) == b)).astype(F32))
    hit = jnp.concatenate(parts, axis=0)
    hit16 = hit.astype(BF16)
    above = (iota((WIDE, WIDE), 0) < iota((WIDE, WIDE), 1)).astype(F32).astype(BF16)
    within = jnp.dot(hit16, above, preferred_element_type=F32)
    totals = jnp.dot(hit16, jnp.ones((WIDE, WIDE), BF16), preferred_element_type=F32)
    r0 = iota((BUCKETS * KLO, BUCKETS * KLO), 0)
    r1 = iota((BUCKETS * KLO, BUCKETS * KLO), 1)
    lower = ((r1 < r0) & ((r1 // KLO) == (r0 // KLO))).astype(F32).astype(BF16)
    earlier = jnp.dot(lower, totals.astype(BF16), preferred_element_type=F32)
    before = within + earlier
    place = jnp.full((KLO, WIDE), -1.0, F32)
    for b in range(BUCKETS):
        at = slice(b * KLO, (b + 1) * KLO)
        base = (starts[b] * CHUNK).astype(F32)
        place = jnp.where(hit[at] > 0, before[at] + base, place)
    place_ref[...] = place.astype(jnp.int32)


def bucket_starts(index):
    row = (index - 1) >> 7
    starts = [jnp.int32(0)]
    for b in range(BUCKETS):
        held = ((index > 0) & ((row // BROWS) == b)).astype(jnp.int32)
        count = jnp.sum(held)
        starts.append(starts[-1] + (count + CHUNK - 1) // CHUNK)
    return starts


def place_hots(place_ref, lane_ref, chunk_ref):
    def body(k, _):
        lanes = pl.ds(pl.multiple_of(k * WIDE, WIDE), WIDE)
        place = place_ref[pl.ds(k, 1), :]
        lane_ref[:, lanes] = one_hot(CHUNK, place & (CHUNK - 1), BF16)
        chunk_ref[:, lanes] = one_hot(CROWS, place >> 9, F32)
        return 0

    lax.fori_loop(0, KLO, body, 0, unroll=2)


def to_places(rows_ref, starts, lane_ref, chunk_ref, out_ref):
    count = len(starts)

    def body(k, _):
        lanes = pl.ds(pl.multiple_of(k * 4 * WIDE, 4 * WIDE), 4 * WIDE)
        chunk = chunk_ref[:, lanes]
        lane = lane_ref[:, lanes]
        left = [[], []]
        for q in range(count):
            value = jnp.concatenate(
                [rows_ref[pl.ds(starts[q] + 4 * k + n, 1), :] for n in range(4)], axis=1
            )
            for p, part in enumerate(halves(value)):
                left[p].append(chunk * part)
        part = lax.dot_general(
            jnp.concatenate(left[0], axis=0).astype(BF16), lane, NT, preferred_element_type=F32
        )
        part += lax.dot_general(
            jnp.concatenate(left[1], axis=0).astype(BF16), lane, NT, preferred_element_type=F32
        )
        out_ref[...] += part
        return 0

    out_ref[...] = jnp.zeros_like(out_ref)
    lax.fori_loop(0, KLO // 4, body, 0)


def from_places(rows_ref, count, lane_ref, chunk_ref, out_ref, starts):
    high, low = halves(rows_ref[...])
    high = high.astype(BF16)
    low = low.astype(BF16)

    def body(k, _):
        lanes = pl.ds(pl.multiple_of(k * 2 * WIDE, 2 * WIDE), 2 * WIDE)
        lane = lane_ref[:, lanes]
        chunk = chunk_ref[:, lanes]
        found = jnp.dot(high, lane, preferred_element_type=F32)
        found += jnp.dot(low, lane, preferred_element_type=F32)
        for q in range(count):
            value = jnp.sum(found[q * CROWS : (q + 1) * CROWS] * chunk, axis=0, keepdims=True)
            for n in range(2):
                out_ref[pl.ds(starts[q] + 2 * k + n, 1), :] = value[:, WIDE * n : WIDE * (n + 1)]
        return 0

    lax.fori_loop(0, KLO // 2, body, 0)


def turn_cells(cells, turned_ref):
    for c in range(3):
        for b in range(BUCKETS):
            block = cells(c, b).T
            high, low = halves(block)
            at = slice(c * CY, (c + 1) * CY)
            turned_ref[b, at, 0:BROWS] = high.astype(BF16)
            turned_ref[b, at, BROWS : 2 * BROWS] = low.astype(BF16)


def chunk_hots(index_ref, j, b):
    index = index_ref[pl.ds(j, 1), :].astype(jnp.int32) - 1
    row = one_hot(BROWS, (index >> 7) - BROWS * b, BF16)
    lane = one_hot(CY, index & 127, F32)
    return row, lane


def gather_chunk(turned, row, lane, out_ref, start, j):
    found = jnp.dot(turned, jnp.concatenate([row, row], axis=0), preferred_element_type=F32)
    for c in range(3):
        out_ref[pl.ds(start + c * CROWS + j, 1), :] = jnp.sum(
            found[c * CY : (c + 1) * CY] * lane, axis=0, keepdims=True
        )


def scatter_chunk(values_ref, start, j, row, lane, total_ref, b):
    high, low = [], []
    for c in range(3):
        one, two = halves(values_ref[pl.ds(start + c * CROWS + j, 1), :])
        high.append(lane * one)
        low.append(lane * two)
    part = lax.dot_general(
        row, jnp.concatenate(high, axis=0).astype(BF16), NT, preferred_element_type=F32
    )
    part += lax.dot_general(
        row, jnp.concatenate(low, axis=0).astype(BF16), NT, preferred_element_type=F32
    )
    total_ref[b] += part


def unpack(came, rows_ref, comps):
    for h in range(KHI):
        rows_ref[0 : comps * KLO, ND * h : ND * (h + 1)] = came[:, h, :].T[0 : comps * KLO]


def second_kernel(
    came, diag, adjoint, rest,
    adjoint_out, message, lane_out, chunk_out, index_out, starts_out,
    rows, place, lane_hot, chunk_hot, ordered, turned, scattered, pulled, pulls,
):
    unpack(came, rows, 4)
    index = rows[0:KLO, :].astype(jnp.int32)
    starts = bucket_starts(index)
    place_slots(index, place, starts)
    place_hots(place, lane_hot, chunk_hot)
    to_places(rows, [q * KLO for q in range(4)], lane_hot, chunk_hot, ordered)
    turn_cells(
        lambda c, b: adjoint[c, 8 * b : 8 * b + 8].reshape(BROWS, CY),
        turned,
    )
    scattered[...] = jnp.zeros_like(scattered)
    pulled[...] = jnp.zeros_like(pulled)
    index_rows = ordered.at[pl.ds(0, CROWS)]
    for b in range(BUCKETS):
        def first(j, _):
            row, lane = chunk_hots(index_rows, j, b)
            gather_chunk(turned[b], row, lane, pulled, 0, j)
            scatter_chunk(ordered, CROWS, j, row, lane, scattered, b)
            return 0

        lax.fori_loop(starts[b], starts[b + 1], first, 0)
    for b in range(BUCKETS):
        def update(n, _):
            z = 8 * b + n
            at = pl.ds(pl.multiple_of(n * CX, CX), CX)
            left = [
                rest[c, z] - scattered[b, at, c * CY : (c + 1) * CY] for c in range(3)
            ]
            step = solve_rows([[diag[i, j, z] for j in range(3)] for i in range(3)], left)
            for c in range(3):
                adjoint_out[c, z] = adjoint[c, z] + step[c]
            return 0

        lax.fori_loop(0, 8, update, 0, unroll=2)
    turn_cells(
        lambda c, b: adjoint_out[c, 8 * b : 8 * b + 8].reshape(BROWS, CY),
        turned,
    )
    for b in range(BUCKETS):
        def second(j, _):
            row, lane = chunk_hots(index_rows, j, b)
            gather_chunk(turned[b], row, lane, pulled, 3 * CROWS, j)
            return 0

        lax.fori_loop(starts[b], starts[b + 1], second, 0)
    pulls[...] = jnp.zeros_like(pulls)
    from_places(
        pulled, 6, lane_hot, chunk_hot, pulls, [q * KLO + (q // 3) * KLO for q in range(6)]
    )
    for h in range(KHI):
        for n in range(2):
            message[:, 2 * h + n, :] = pulls[ND * n : ND * (n + 1), ND * h : ND * (h + 1)].T
    lane_out[...] = lane_hot[...]
    chunk_out[...] = chunk_hot[...]
    index_out[...] = ordered[0:CROWS, :]
    for b in range(BUCKETS + 1):
        starts_out[b] = starts[b]


def seg_image(adjoint, diag, chain, scattered):
    position = iota((1, SEGS), 1) % SEG_MAX
    own = transposed_rows(seg_matrix(diag), adjoint)
    lower = transposed_rows(seg_matrix(chain.at[0]), adjoint)
    upper = transposed_rows(seg_matrix(chain.at[1]), adjoint)
    out = []
    for c in range(3):
        total = own[c] + scattered[c]
        total += jnp.where(position == SEG_MAX - 1, 0.0, pltpu.roll(lower[c], SEGS - 1, 1))
        total += jnp.where(position == 0, 0.0, pltpu.roll(upper[c], 1, 1))
        out.append(total)
    return out


def third_kernel(
    message, grad_cells, adjoint, diag, off,
    grad_segs, adjoint_segs, seg_diag, seg_chain, seg_len, slots,
    came, rest_out, adjoint_segs_out, residual_segs_out,
    pulls_in, push_message, pulls, terms, lane_hot, table, push, off_here, image,
    x_out, x_in, y_out, y_in, column,
    off_sem, send_sem, recv_sem, own_sem, halo_send, halo_recv,
):
    load = pltpu.make_async_copy(off, off_here, off_sem)
    load.start()
    greet()
    pull_exchange = Exchange(message, pulls_in, send_sem.at[0], recv_sem.at[0], own_sem.at[0])
    push_exchange = Exchange(
        push_message, came, send_sem.at[1], recv_sem.at[1], own_sem.at[1]
    )
    halo = Halo(x_out, x_in, y_out, y_in, halo_send, halo_recv)
    seg_slots = slots.at[pl.ds(0, KLO)]
    blocks = slots.at[pl.ds(KLO, 18 * KLO)]
    lane_hots(seg_slots, lane_hot)
    greeted()
    pull_exchange.start()
    load.wait()
    stencil(lambda z: cells_at(adjoint, z), diag, off_here, image, halo, column)
    active = active_row(seg_len)
    grad = seg_rows(grad_segs)
    matrix = seg_matrix(seg_diag)
    before = seg_rows(adjoint_segs)
    pull_exchange.wait_recv()
    for h in range(KHI):
        for n in range(2):
            pulls[ND * n : ND * (n + 1), ND * h : ND * (h + 1)] = pulls_in[:, 2 * h + n, :].T
    for c, term in enumerate(slot_terms(blocks, 1, pulls, 0)):
        terms[c * KLO : (c + 1) * KLO, :] = term
    scattered = seg_scatter(terms, seg_slots, lane_hot, table)
    seen = seg_image(before, seg_diag, seg_chain, scattered)
    step = solve_rows(matrix, [grad[c] - seen[c] for c in range(3)])
    after = [before[c] + active * step[c] for c in range(3)]
    for c in range(3):
        adjoint_segs_out[c : c + 1, :] = after[c]
    seg_gather(after, seg_slots, lane_hot, table, push)
    packed = jnp.concatenate(
        slot_terms(blocks, 0, push, 0) + [jnp.zeros((KLO, WIDE), F32)], axis=0
    )
    for h in range(KHI):
        push_message[:, h, :] = packed[:, ND * h : ND * (h + 1)].T
    push_exchange.start()
    for c, term in enumerate(slot_terms(blocks, 1, pulls, ND)):
        terms[c * KLO : (c + 1) * KLO, :] = term
    scattered = seg_scatter(terms, seg_slots, lane_hot, table)
    seen = seg_image(after, seg_diag, seg_chain, scattered)
    for c in range(3):
        residual_segs_out[c : c + 1, :] = active * (grad[c] - seen[c])
    halo.wait_recv()
    add_rims(image, halo, column)
    for c in range(3):
        rest_out[c] = grad_cells[c] - image[c, 1 : NZ + 1]
    push_exchange.wait_recv()
    pull_exchange.wait_send()
    push_exchange.wait_send()
    halo.wait_send()


def fourth_kernel(
    starts, came, rest, lane_hot, chunk_hot, index_rows, adjoint_segs, residual_segs,
    residual_out, adjoint_segs_out, residual_segs_out,
    rows, ordered, scattered,
):
    adjoint_segs_out[...] = adjoint_segs[...]
    residual_segs_out[...] = residual_segs[...]
    unpack(came, rows, 3)
    to_places(rows, [q * KLO for q in range(3)], lane_hot, chunk_hot, ordered)
    scattered[...] = jnp.zeros_like(scattered)
    for b in range(BUCKETS):
        def body(j, _):
            row, lane = chunk_hots(index_rows, j, b)
            scatter_chunk(ordered, 0, j, row, lane, scattered, b)
            return 0

        lax.fori_loop(starts[b], starts[b + 1], body, 0)
    for b in range(BUCKETS):
        for c in range(3):
            at = slice(8 * b, 8 * b + 8)
            residual_out[c, at] = rest[c, at] - scattered[b, :, c * CY : (c + 1) * CY].reshape(
                8, CX, CY
            )


def shape(*dims, kind=F32):
    return jax.ShapeDtypeStruct(dims, kind)


def vmem(*dims, kind=F32):
    return pltpu.VMEM(dims, kind)


def rim_scratch():
    return [
        vmem(2, 3, NZ, CY),
        vmem(2, 3, NZ, CY),
        vmem(2, 8, ROWS),
        vmem(2, 8, ROWS),
        vmem(ROWS, CY),
    ]


def call(kernel, outs, ins, scratch, number, in_specs=None, limit=58 << 20):
    params = dict(vmem_limit_bytes=limit)
    if number is not None:
        params.update(collective_id=number, has_side_effects=True)
    return pl.pallas_call(
        kernel,
        out_shape=outs,
        in_specs=in_specs or [VMEM] * len(ins),
        out_specs=[VMEM] * len(outs) if not isinstance(outs[-1], tuple) else None,
        scratch_shapes=scratch,
        compiler_params=pltpu.CompilerParams(**params),
        name=kernel.__name__,
    )(*ins)


def shards(
    grad_cells, grad_segs, cell_diag, cell_off, seg_diag, seg_chain, seg_len,
    perf_device, perf_local, perf_seg, perf_blocks,
):
    dma = pltpu.SemaphoreType.DMA
    lens = seg_len.reshape(32, 1)
    cells = shape(3, NZ, CX, CY)
    segs = shape(3, SEGS)
    came, slots, adjoint, rest, adjoint_segs = call(
        first_kernel,
        [shape(ND, KHI, ND), shape(19 * KLO, WIDE), cells, cells, segs],
        [
            grad_cells, grad_segs, cell_diag, cell_off, seg_diag, lens,
            perf_device.reshape(1, PERFS), perf_local.reshape(1, PERFS),
            perf_seg.reshape(1, PERFS), perf_blocks,
        ],
        [
            vmem(24, PERFS),
            vmem(2, 20 * KLO, 512, kind=BF16),
            vmem(20 * KLO, WIDE),
            vmem(128, SLOTS, kind=BF16),
            vmem(24, 256),
            vmem(3 * KLO, WIDE),
            vmem(ND, KHI, ND),
            vmem(6, 3, 3, NZ, CX, CY),
            vmem(3, NZ + 2, CX, CY),
        ]
        + rim_scratch()
        + [dma, dma, dma, dma, dma((4,)), dma((4,))],
        0,
        [VMEM] * 3 + [ANY] + [VMEM] * 6,
    )
    adjoint, message, lane_hot, chunk_hot, index_rows, starts = pl.pallas_call(
        second_kernel,
        out_shape=[
            cells, shape(ND, 4, ND), shape(CHUNK, SLOTS, kind=BF16), shape(CROWS, SLOTS),
            shape(CROWS, CHUNK), shape(8, kind=jnp.int32),
        ],
        in_specs=[VMEM] * 4,
        out_specs=[VMEM] * 5 + [pl.BlockSpec(memory_space=pltpu.SMEM)],
        scratch_shapes=[
            vmem(4 * KLO, WIDE),
            vmem(KLO, WIDE, kind=jnp.int32),
            vmem(CHUNK, SLOTS, kind=BF16),
            vmem(CROWS, SLOTS),
            vmem(4 * CROWS, CHUNK),
            vmem(BUCKETS, 3 * CY, 2 * BROWS, kind=BF16),
            vmem(BUCKETS, BROWS, 3 * CY),
            vmem(6 * CROWS, CHUNK),
            vmem(8 * KLO, WIDE),
        ],
        compiler_params=pltpu.CompilerParams(vmem_limit_bytes=58 << 20),
        name="second_kernel",
    )(came, cell_diag, adjoint, rest)
    came, rest, adjoint_segs, residual_segs = call(
        third_kernel,
        [shape(ND, KHI, ND), cells, segs, segs],
        [
            message, grad_cells, adjoint, cell_diag, cell_off,
            grad_segs, adjoint_segs, seg_diag, seg_chain, lens, slots,
        ],
        [
            vmem(ND, 4, ND),
            vmem(ND, KHI, ND),
            vmem(8 * KLO, WIDE),
            vmem(3 * KLO, WIDE),
            vmem(128, SLOTS, kind=BF16),
            vmem(24, 256),
            vmem(3 * KLO, WIDE),
            vmem(6, 3, 3, NZ, CX, CY),
            vmem(3, NZ + 2, CX, CY),
        ]
        + rim_scratch()
        + [dma, dma((2,)), dma((2,)), dma((2,)), dma((4,)), dma((4,))],
        1,
        [VMEM] * 4 + [ANY] + [VMEM] * 6,
    )
    residual, adjoint_segs, residual_segs = call(
        fourth_kernel,
        [cells, segs, segs],
        [starts, came, rest, lane_hot, chunk_hot, index_rows, adjoint_segs, residual_segs],
        [
            vmem(3 * KLO, WIDE),
            vmem(3 * CROWS, CHUNK),
            vmem(BUCKETS, BROWS, 3 * CY),
        ],
        None,
        [pl.BlockSpec(memory_space=pltpu.SMEM)] + [VMEM] * 7,
    )
    return adjoint, adjoint_segs, residual, residual_segs


def solution(mesh):
    in_specs = (
        P(None, None, "gx", "gy"),
        P(None, ("gx", "gy")),
        P(None, None, None, "gx", "gy"),
        P(None, None, None, None, "gx", "gy"),
        P(None, None, ("gx", "gy")),
        P(None, None, None, ("gx", "gy")),
        P(("gx", "gy")),
        P(("gx", "gy"), None),
        P(("gx", "gy")),
        P(("gx", "gy")),
        P(None, None, None, ("gx", "gy")),
    )
    out_specs = (
        P(None, None, "gx", "gy"),
        P(None, ("gx", "gy")),
        P(None, None, "gx", "gy"),
        P(None, ("gx", "gy")),
    )
    return jax.shard_map(shards, mesh=mesh, in_specs=in_specs, out_specs=out_specs, check_vma=False)
```

```python
import jax
import jax.numpy as jnp
from jax import lax
from jax.experimental import pallas as pl
from jax.experimental.pallas import tpu as pltpu
from jax.sharding import PartitionSpec as P

MESH = pl.DeviceIdType.MESH
F32 = jnp.float32
BF16 = jnp.bfloat16
NT = (((1,), (1,)), ((), ()))
GX = 8
GY = 16
ND = GX * GY
NZ = 32
CX = 16
CY = 128
ROWS = NZ * CX
SEGS = 1024
SEG_MAX = 32
PERFS = 4096
KLO = 32
KHI = 2
WIDE = KHI * ND
SLOTS = KLO * WIDE
BUCKETS = 4
BROWS = ROWS // BUCKETS
CHUNK = 512
LANES = 256
CROWS = 40
SPARE = CROWS * LANES // CHUNK - 1
VMEM = pl.BlockSpec(memory_space=pltpu.VMEM)
ANY = pl.BlockSpec(memory_space=pl.ANY)


def rounded(x):
    return x.astype(BF16).astype(F32)


def halves(x):
    high = rounded(x)
    return high, x - high


def iota(shape, dim):
    return lax.broadcasted_iota(jnp.int32, shape, dim)


def one_hot(count, row, kind):
    hit = iota((count, row.shape[1]), 0) == row
    return hit.astype(F32).astype(kind)


def inverse_rows(matrix):
    cofactor = [
        [
            matrix[(i + 1) % 3][(j + 1) % 3] * matrix[(i + 2) % 3][(j + 2) % 3]
            - matrix[(i + 1) % 3][(j + 2) % 3] * matrix[(i + 2) % 3][(j + 1) % 3]
            for j in range(3)
        ]
        for i in range(3)
    ]
    determinant = (
        matrix[0][0] * cofactor[0][0]
        + matrix[0][1] * cofactor[0][1]
        + matrix[0][2] * cofactor[0][2]
    )
    return cofactor, 1.0 / determinant


def solve_rows(matrix, vector):
    cofactor, scale = inverse_rows(matrix)
    return [
        (cofactor[i][0] * vector[0] + cofactor[i][1] * vector[1] + cofactor[i][2] * vector[2])
        * scale
        for i in range(3)
    ]


def transposed_rows(matrix, vector):
    return [
        matrix[0][i] * vector[0] + matrix[1][i] * vector[1] + matrix[2][i] * vector[2]
        for i in range(3)
    ]


def seg_rows(ref):
    return [ref[j : j + 1, :] for j in range(3)]


def seg_matrix(ref):
    return [[ref[i, j : j + 1, :] for j in range(3)] for i in range(3)]


def active_row(seg_len_ref):
    square = iota((32, 32), 0) == iota((32, 32), 1)
    lens = jnp.sum(jnp.where(square, seg_len_ref[...].astype(F32), 0.0), axis=1, keepdims=True)
    lanes = iota((32, SEGS), 1)
    mine = (lanes // SEG_MAX) == iota((32, SEGS), 0)
    below = (lanes % SEG_MAX).astype(F32) < lens
    return jnp.sum(jnp.where(mine & below, 1.0, 0.0), axis=0, keepdims=True)


def four_rows(ref, start, k):
    return jnp.concatenate([ref[pl.ds(start + 4 * k + n, 1), :] for n in range(4)], axis=1)


def put_four_rows(ref, start, k, value):
    for n in range(4):
        ref[pl.ds(start + 4 * k + n, 1), :] = value[:, WIDE * n : WIDE * (n + 1)]


def four_lanes(k):
    return pl.ds(pl.multiple_of(k * 4 * WIDE, 4 * WIDE), 4 * WIDE)


def seg_gather(values, seg_slots, lane_hot_ref, table_ref, out_ref):
    for c in range(3):
        for p, part in enumerate(halves(values[c])):
            for h in range(8):
                at = p * 24 + c * 8 + h
                table_ref[at : at + 1, :] = part[:, 128 * h : 128 * (h + 1)]
    table = table_ref[...].astype(BF16)

    def body(k, _):
        found = jnp.dot(table, lane_hot_ref[:, four_lanes(k)], preferred_element_type=F32)
        found = found[:24] + found[24:]
        high = four_rows(seg_slots, 0, k).astype(jnp.int32) >> 7
        pick = (iota((8, 4 * WIDE), 0) == high).astype(F32)
        for c in range(3):
            value = jnp.sum(found[8 * c : 8 * c + 8] * pick, axis=0, keepdims=True)
            put_four_rows(out_ref, c * KLO, k, value)
        return 0

    lax.fori_loop(0, KLO // 4, body, 0, unroll=2)


def seg_scatter(values_ref, seg_slots, lane_hot_ref, table_ref):
    def body(k, total):
        high = four_rows(seg_slots, 0, k).astype(jnp.int32) >> 7
        pick = (iota((8, 4 * WIDE), 0) == high).astype(F32)
        right = []
        for c in range(3):
            right += [pick * part for part in halves(four_rows(values_ref, c * KLO, k))]
        return total + lax.dot_general(
            lane_hot_ref[:, four_lanes(k)],
            jnp.concatenate(right, axis=0).astype(BF16),
            NT,
            preferred_element_type=F32,
        )

    total = lax.fori_loop(0, KLO // 4, body, jnp.zeros((128, 48), F32), unroll=2)
    turned = jnp.concatenate([total, jnp.zeros((128, 80), F32)], axis=1).T
    rows = []
    for c in range(3):
        table_ref[0:8, :] = turned[16 * c : 16 * c + 8] + turned[16 * c + 8 : 16 * c + 16]
        rows.append(jnp.concatenate([table_ref[h : h + 1, :] for h in range(8)], axis=1))
    return rows


def lane_hots(seg_slots, lane_hot_ref):
    def body(k, _):
        low = four_rows(seg_slots, 0, k).astype(jnp.int32) & 127
        lane_hot_ref[:, four_lanes(k)] = one_hot(128, low, BF16)
        return 0

    lax.fori_loop(0, KLO // 4, body, 0)


def slot_terms(blocks, rows_ref, start):
    vector = [rows_ref[start + c * KLO : start + (c + 1) * KLO, :] for c in range(3)]
    out = []
    for i in range(3):
        total = None
        for j in range(3):
            at = (j * 3 + i) * KLO
            term = blocks[at : at + KLO, :] * vector[j]
            total = term if total is None else total + term
        out.append(total)
    return out


def everyone(act):
    gx = lax.axis_index("gx")
    gy = lax.axis_index("gy")
    me = gx * GY + gy

    def body(i, _):
        other = lax.rem(me + i, ND)
        act(other, (other // GY, lax.rem(other, GY)))
        return 0

    lax.fori_loop(1, ND, body, 0)


def greet():
    barrier = pltpu.get_barrier_semaphore()
    everyone(
        lambda other, place: pl.semaphore_signal(
            barrier, inc=1, device_id=place, device_id_type=MESH
        )
    )


def greeted():
    pl.semaphore_wait(pltpu.get_barrier_semaphore(), ND - 1)


class Exchange:
    def __init__(self, source, target, send_sem, recv_sem, own_sem):
        self.source, self.target = source, target
        self.send_sem, self.recv_sem, self.own_sem = send_sem, recv_sem, own_sem
        self.me = lax.axis_index("gx") * GY + lax.axis_index("gy")

    def own(self):
        return pltpu.make_async_copy(
            self.source.at[self.me], self.target.at[self.me], self.own_sem
        )

    def whole(self):
        return pltpu.make_async_remote_copy(
            src_ref=self.source.at[pl.ds(0, ND - 1)],
            dst_ref=self.target.at[pl.ds(0, ND - 1)],
            send_sem=self.send_sem,
            recv_sem=self.recv_sem,
            device_id=(lax.axis_index("gx"), lax.axis_index("gy")),
            device_id_type=MESH,
        )

    def start(self):
        self.own().start()
        everyone(
            lambda other, place: pltpu.make_async_remote_copy(
                src_ref=self.source.at[other],
                dst_ref=self.target.at[self.me],
                send_sem=self.send_sem,
                recv_sem=self.recv_sem,
                device_id=place,
                device_id_type=MESH,
            ).start()
        )

    def wait_recv(self):
        self.own().wait()
        self.whole().wait_recv()

    def wait_send(self):
        self.whole().wait_send()


class Halo:
    def __init__(self, x_out, x_in, y_out, y_in, send_sem, recv_sem):
        gx = lax.axis_index("gx")
        gy = lax.axis_index("gy")
        places = [
            (lax.rem(gx + 1, GX), gy),
            (lax.rem(gx + GX - 1, GX), gy),
            (gx, lax.rem(gy + 1, GY)),
            (gx, lax.rem(gy + GY - 1, GY)),
        ]
        pairs = [(x_out, x_in, 0), (x_out, x_in, 1), (y_out, y_in, 0), (y_out, y_in, 1)]
        self.copies = [
            pltpu.make_async_remote_copy(
                src_ref=a.at[n],
                dst_ref=b.at[n],
                send_sem=send_sem.at[at],
                recv_sem=recv_sem.at[at],
                device_id=place,
                device_id_type=MESH,
            )
            for at, ((a, b, n), place) in enumerate(zip(pairs, places))
        ]
        self.x_out, self.x_in, self.y_out, self.y_in = x_out, x_in, y_out, y_in

    def start(self):
        for copy in self.copies:
            copy.start()

    def wait_recv(self):
        for copy in self.copies:
            copy.wait_recv()

    def wait_send(self):
        for copy in self.copies:
            copy.wait_send()


def stencil(adjoint, diag_ref, off_ref, image_ref, halo, column_ref):
    for c in range(3):
        image_ref[c] = jnp.zeros((NZ + 2, CX, CY), F32)
    rows = iota((CX, CY), 0)
    lanes = iota((CX, CY), 1)

    def body(z, _):
        a = adjoint(z)
        own = transposed_rows([[diag_ref[j, i, z] for i in range(3)] for j in range(3)], a)
        moved = [
            transposed_rows([[off_ref[e, j, i, z] for i in range(3)] for j in range(3)], a)
            for e in range(6)
        ]
        columns = jnp.zeros((CX, CY), F32)
        for c in range(3):
            total = own[c]
            halo.x_out[0, c, pl.ds(z, 1), :] = moved[0][c][CX - 1 : CX]
            halo.x_out[1, c, pl.ds(z, 1), :] = moved[1][c][0:1]
            total += jnp.where(rows == 0, 0.0, pltpu.roll(moved[0][c], 1, 0))
            total += jnp.where(rows == CX - 1, 0.0, pltpu.roll(moved[1][c], CX - 1, 0))
            total += jnp.where(lanes == 0, 0.0, pltpu.roll(moved[2][c], 1, 1))
            total += jnp.where(lanes == CY - 1, 0.0, pltpu.roll(moved[3][c], CY - 1, 1))
            columns = jnp.where(lanes == c, pltpu.roll(moved[2][c], 1 + c, 1), columns)
            columns = jnp.where(lanes == 8 + c, pltpu.roll(moved[3][c], 8 + c, 1), columns)
            image_ref[c, z + 1] += total
            image_ref[c, z + 2] += moved[4][c]
            image_ref[c, z] += moved[5][c]
        column_ref[pl.ds(pl.multiple_of(z * CX, CX), CX), :] = columns
        return 0

    lax.fori_loop(0, NZ, body, 0, unroll=2)
    turned = column_ref[...].T
    halo.y_out[0] = turned[0:8]
    halo.y_out[1] = turned[8:16]
    halo.start()


def add_rims(image_ref, halo, column_ref):
    gx = lax.axis_index("gx")
    gy = lax.axis_index("gy")
    first_x = jnp.where(gx > 0, 1.0, 0.0)
    last_x = jnp.where(gx < GX - 1, 1.0, 0.0)
    first_y = jnp.where(gy > 0, 1.0, 0.0)
    last_y = jnp.where(gy < GY - 1, 1.0, 0.0)
    came = jnp.concatenate(
        [halo.y_in[0] * first_y, halo.y_in[1] * last_y, jnp.zeros((CY - 16, ROWS), F32)], axis=0
    )
    column_ref[...] = came.T
    rows = iota((CX, CY), 0)
    lanes = iota((CX, CY), 1)

    def body(z, _):
        columns = column_ref[pl.ds(pl.multiple_of(z * CX, CX), CX), :]
        for c in range(3):
            low = halo.x_in[0, c, pl.ds(z, 1), :] * first_x
            high = halo.x_in[1, c, pl.ds(z, 1), :] * last_x
            total = jnp.where(rows == 0, low, 0.0) + jnp.where(rows == CX - 1, high, 0.0)
            left = columns if c == 0 else pltpu.roll(columns, CY - c, 1)
            total += jnp.where(lanes == 0, left, 0.0)
            right = pltpu.roll(columns, CY - 1 - 8 - c, 1)
            total += jnp.where(lanes == CY - 1, right, 0.0)
            image_ref[c, z + 1] += total
        return 0

    lax.fori_loop(0, NZ, body, 0, unroll=2)


def rank_rows(device_ref, column_ref, row_ref):
    above = (iota((256, 256), 0) < iota((256, 256), 1)).astype(F32).astype(BF16)
    ones = jnp.ones((256, 256), BF16)
    carry = jnp.zeros((ND, 256), F32)
    for j in range(PERFS // 256):
        at = slice(256 * j, 256 * (j + 1))
        target = device_ref[:, at]
        hit = one_hot(ND, target, F32)
        hit16 = hit.astype(BF16)
        before = jnp.dot(hit16, above, preferred_element_type=F32) + carry
        carry = carry + jnp.dot(hit16, ones, preferred_element_type=F32)
        rank = jnp.sum(before * hit, axis=0, keepdims=True).astype(jnp.int32)
        column_ref[:, at] = one_hot(WIDE, target + ND * (rank >> 5), BF16)
        row_ref[:, at] = one_hot(KLO, rank & (KLO - 1), F32)


def place_rows(row, count, column_ref, row_ref, work_ref, total_ref, out_ref):
    size = count * KLO
    for j in range(PERFS // 512):
        at = slice(512 * j, 512 * (j + 1))
        row_hot = row_ref[:, at]
        for q in range(count):
            for p, part in enumerate(halves(row(q, at))):
                put = p * size + q * KLO
                work_ref[put : put + KLO, :] = (row_hot * part).astype(BF16)
        part = lax.dot_general(
            work_ref[0 : 2 * size, :], column_ref[:, at], NT, preferred_element_type=F32
        )
        if j == 0:
            total_ref[0 : 2 * size, :] = part
        else:
            total_ref[0 : 2 * size, :] += part
    out_ref[...] = total_ref[0:size, :] + total_ref[size : 2 * size, :]


def cells_at(ref, z):
    return [ref[c, z] for c in range(3)]


def first_kernel(
    grad_cells, grad_segs, diag, off, seg_diag, seg_len, device, local, seg, blocks,
    came, seg_slots, push_blocks, pull_blocks, adjoint_out, rest_out, adjoint_segs_out,
    column_hot, row_hot, work, total, slots, lane_hot, table, push, message,
    off_here, diag_here, grad_here, image,
    x_out, x_in, y_out, y_in, column,
    load_sem, send_sem, recv_sem, own_sem, halo_send, halo_recv,
):
    loads = [
        pltpu.make_async_copy(a, b, load_sem.at[n])
        for n, (a, b) in enumerate(
            [(diag, diag_here), (grad_cells, grad_here), (off, off_here)]
        )
    ]
    for load in loads:
        load.start()
    greet()
    exchange = Exchange(message, came, send_sem, recv_sem, own_sem)
    halo = Halo(x_out, x_in, y_out, y_in, halo_send, halo_recv)
    rank_rows(device, column_hot, row_hot)

    def first_rows(q, at):
        if q == 0:
            return (local[:, at] + 1).astype(F32)
        if q == 1:
            return seg[:, at].astype(F32)
        return blocks[(q - 2) // 3, (q - 2) % 3, 0:1, at]

    place_rows(first_rows, 11, column_hot, row_hot, work, total, slots)
    active = active_row(seg_len)
    adjoint_segs = [
        active * row for row in solve_rows(seg_matrix(seg_diag), seg_rows(grad_segs))
    ]
    for c in range(3):
        adjoint_segs_out[c : c + 1, :] = adjoint_segs[c]
    seg_slots[...] = slots[KLO : 2 * KLO, :]
    push_blocks[...] = slots[2 * KLO :, :]
    lane_hots(seg_slots, lane_hot)
    seg_gather(adjoint_segs, seg_slots, lane_hot, table, push)
    terms = slot_terms(push_blocks, push, 0)
    packed = jnp.concatenate([slots[0:KLO, :]] + terms, axis=0)
    for h in range(KHI):
        message[:, h, :] = packed[:, ND * h : ND * (h + 1)].T
    greeted()
    exchange.start()
    loads[0].wait()
    loads[1].wait()

    def begin(z, _):
        a = solve_rows(
            [[diag_here[i, j, z] for j in range(3)] for i in range(3)], cells_at(grad_here, z)
        )
        for c in range(3):
            adjoint_out[c, z] = a[c]
        return 0

    lax.fori_loop(0, NZ, begin, 0, unroll=2)
    loads[2].wait()
    stencil(lambda z: cells_at(adjoint_out, z), diag_here, off_here, image, halo, column)
    place_rows(
        lambda q, at: blocks[q // 3, q % 3, 1:2, at],
        9, column_hot, row_hot, work, total, pull_blocks,
    )
    halo.wait_recv()
    add_rims(image, halo, column)
    for c in range(3):
        rest_out[c] = grad_here[c] - image[c, 1 : NZ + 1]
    exchange.wait_recv()
    exchange.wait_send()
    halo.wait_send()


def place_slots(index, place_ref, starts):
    row = (index - 1) >> 7
    parts = []
    for b in range(BUCKETS):
        parts.append(((index > 0) & ((row // BROWS) == b)).astype(F32))
    hit = jnp.concatenate(parts, axis=0)
    hit16 = hit.astype(BF16)
    above = (iota((WIDE, WIDE), 0) < iota((WIDE, WIDE), 1)).astype(F32).astype(BF16)
    within = jnp.dot(hit16, above, preferred_element_type=F32)
    totals = jnp.dot(hit16, jnp.ones((WIDE, WIDE), BF16), preferred_element_type=F32)
    r0 = iota((BUCKETS * KLO, BUCKETS * KLO), 0)
    r1 = iota((BUCKETS * KLO, BUCKETS * KLO), 1)
    lower = ((r1 < r0) & ((r1 // KLO) == (r0 // KLO))).astype(F32).astype(BF16)
    earlier = jnp.dot(lower, totals.astype(BF16), preferred_element_type=F32)
    before = within + earlier
    place = jnp.full((KLO, WIDE), -1.0, F32)
    for b in range(BUCKETS):
        at = slice(b * KLO, (b + 1) * KLO)
        base = (starts[b] * CHUNK).astype(F32)
        place = jnp.where(hit[at] > 0, before[at] + base, place)
    place_ref[...] = place.astype(jnp.int32)


def bucket_starts(index):
    row = (index - 1) >> 7
    starts = [jnp.int32(0)]
    for b in range(BUCKETS):
        held = ((index > 0) & ((row // BROWS) == b)).astype(jnp.int32)
        count = jnp.sum(held)
        starts.append(starts[-1] + (count + CHUNK - 1) // CHUNK)
    return starts


def place_hots(place_ref, lane_ref, chunk_ref):
    def body(k, _):
        place = four_rows(place_ref, 0, k)
        lane_ref[:, four_lanes(k)] = one_hot(LANES, place & (LANES - 1), BF16)
        chunk_ref[:, four_lanes(k)] = one_hot(CROWS, place >> 8, F32)
        return 0

    lax.fori_loop(0, KLO // 4, body, 0)


def to_places(rows_ref, count, lane_ref, chunk_ref, total_ref, out_ref):
    size = count * CROWS

    def body(k, _):
        chunk = chunk_ref[:, four_lanes(k)]
        left = [[], []]
        for q in range(count):
            for p, part in enumerate(halves(four_rows(rows_ref, q * KLO, k))):
                left[p].append(chunk * part)
        total_ref[0 : 2 * size, :] += lax.dot_general(
            jnp.concatenate(left[0] + left[1], axis=0).astype(BF16),
            lane_ref[:, four_lanes(k)],
            NT,
            preferred_element_type=F32,
        )
        return 0

    total_ref[...] = jnp.zeros_like(total_ref)
    lax.fori_loop(0, KLO // 4, body, 0, unroll=2)
    out_ref[...] = total_ref[0:size, :] + total_ref[size : 2 * size, :]


def from_places(rows_ref, count, lane_ref, chunk_ref, out_ref, starts):
    size = count * CROWS
    both = jnp.concatenate(halves(rows_ref[...]), axis=0).astype(BF16)

    def body(k, _):
        chunk = chunk_ref[:, four_lanes(k)]
        found = jnp.dot(both, lane_ref[:, four_lanes(k)], preferred_element_type=F32)
        for q in range(count):
            at = q * CROWS
            value = found[at : at + CROWS] + found[size + at : size + at + CROWS]
            put_four_rows(
                out_ref, starts[q], k, jnp.sum(value * chunk, axis=0, keepdims=True)
            )
        return 0

    lax.fori_loop(0, KLO // 4, body, 0, unroll=2)


def turn_cells(cells, turned_ref):
    for c in range(3):
        for b in range(BUCKETS):
            block = cells(c, b).T
            high, low = halves(block)
            at = slice(c * CY, (c + 1) * CY)
            turned_ref[b, at, 0:BROWS] = high.astype(BF16)
            turned_ref[b, at, BROWS : 2 * BROWS] = low.astype(BF16)


def two_rows(ref, start, j):
    return jnp.concatenate([ref[pl.ds(start + 2 * j + n, 1), :] for n in range(2)], axis=1)


def chunk_hots(index_ref, j, b):
    index = two_rows(index_ref, 0, j).astype(jnp.int32) - 1
    row = one_hot(BROWS, (index >> 7) - BROWS * b, BF16)
    lane = one_hot(CY, index & 127, F32)
    return row, lane


def gather_chunk(turned, row, lane, out_ref, start, j):
    found = jnp.dot(turned, jnp.concatenate([row, row], axis=0), preferred_element_type=F32)
    for c in range(3):
        value = jnp.sum(found[c * CY : (c + 1) * CY] * lane, axis=0, keepdims=True)
        for n in range(2):
            out_ref[pl.ds(start + c * CROWS + 2 * j + n, 1), :] = value[
                :, LANES * n : LANES * (n + 1)
            ]


def scatter_chunk(values_ref, start, j, row, lane, total_ref, b):
    high, low = [], []
    for c in range(3):
        one, two = halves(two_rows(values_ref, start + c * CROWS, j))
        high.append(lane * one)
        low.append(lane * two)
    part = lax.dot_general(
        jnp.concatenate(high + low, axis=0).astype(BF16), row, NT, preferred_element_type=F32
    )
    total_ref[b] += part[: 3 * CY] + part[3 * CY :]


def each_chunk(starts, act):
    counts = [starts[b + 1] - starts[b] for b in range(BUCKETS)]
    steps = counts[0]
    for count in counts[1:]:
        steps = jnp.maximum(steps, count)

    def body(t, _):
        for b in range(BUCKETS):
            act(b, jnp.where(t < counts[b], starts[b] + t, SPARE))
        return 0

    lax.fori_loop(0, steps, body, 0)


def scattered_cells(total_ref, b, c):
    return total_ref[b, c * CY : (c + 1) * CY, :].T.reshape(NZ // BUCKETS, CX, CY)


def unpack(came, rows_ref, comps):
    for h in range(KHI):
        rows_ref[0 : comps * KLO, ND * h : ND * (h + 1)] = came[:, h, :].T[0 : comps * KLO]


def second_kernel(
    came, diag, adjoint, rest,
    adjoint_out, pulled, index_out, place, starts_out,
    rows, lane_hot, chunk_hot, total, ordered, turned, scattered,
    diag_here, adjoint_here, rest_here, load_sem,
):
    loads = [
        pltpu.make_async_copy(a, b, load_sem.at[n])
        for n, (a, b) in enumerate(
            [(adjoint, adjoint_here), (diag, diag_here), (rest, rest_here)]
        )
    ]
    for load in loads:
        load.start()
    unpack(came, rows, 4)
    index = rows[0:KLO, :].astype(jnp.int32)
    starts = bucket_starts(index)
    place_slots(index, place, starts)
    place_hots(place, lane_hot, chunk_hot)
    to_places(rows, 4, lane_hot, chunk_hot, total, ordered)
    loads[0].wait()
    turn_cells(
        lambda c, b: adjoint_here[c, 8 * b : 8 * b + 8].reshape(BROWS, CY),
        turned,
    )
    scattered[...] = jnp.zeros_like(scattered)
    pulled[...] = jnp.zeros_like(pulled)
    index_rows = ordered.at[pl.ds(0, CROWS)]

    def first(b, j):
        row, lane = chunk_hots(index_rows, j, b)
        gather_chunk(turned[b], row, lane, pulled, 0, j)
        scatter_chunk(ordered, CROWS, j, row, lane, scattered, b)

    each_chunk(starts, first)
    loads[1].wait()
    loads[2].wait()
    for b in range(BUCKETS):
        for c in range(3):
            at = slice(8 * b, 8 * b + 8)
            rest_here[c, at] = rest_here[c, at] - scattered_cells(scattered, b, c)

    def update(z, _):
        step = solve_rows(
            [[diag_here[i, j, z] for j in range(3)] for i in range(3)], cells_at(rest_here, z)
        )
        for c in range(3):
            adjoint_out[c, z] = adjoint_here[c, z] + step[c]
        return 0

    lax.fori_loop(0, NZ, update, 0, unroll=2)
    turn_cells(
        lambda c, b: adjoint_out[c, 8 * b : 8 * b + 8].reshape(BROWS, CY),
        turned,
    )

    def second(b, j):
        row, lane = chunk_hots(index_rows, j, b)
        gather_chunk(turned[b], row, lane, pulled, 3 * CROWS, j)

    each_chunk(starts, second)
    index_out[...] = ordered[0:CROWS, :]
    for b in range(BUCKETS + 1):
        starts_out[b] = starts[b]


def seg_image(adjoint, diag, chain, scattered):
    position = iota((1, SEGS), 1) % SEG_MAX
    own = transposed_rows(seg_matrix(diag), adjoint)
    lower, upper = [
        transposed_rows(
            [[chain[i, j, n : n + 1, :] for j in range(3)] for i in range(3)], adjoint
        )
        for n in range(2)
    ]
    out = []
    for c in range(3):
        total = own[c] + scattered[c]
        total += jnp.where(position == SEG_MAX - 1, 0.0, pltpu.roll(lower[c], SEGS - 1, 1))
        total += jnp.where(position == 0, 0.0, pltpu.roll(upper[c], 1, 1))
        out.append(total)
    return out


def third_kernel(
    pulled, place, grad_cells, adjoint, diag, off,
    grad_segs, adjoint_segs, seg_diag, seg_chain, seg_len, seg_slots, push_blocks, pull_blocks,
    ordered, rest_out, adjoint_segs_out, residual_segs_out,
    place_lane, place_chunk, total, message, pulls_in, push_message, came,
    pulls, terms, lane_hot, table, push, off_here, diag_here, grad_here, adjoint_here, image,
    x_out, x_in, y_out, y_in, column,
    load_sem, send_sem, recv_sem, own_sem, halo_send, halo_recv,
):
    greet()
    loads = [
        pltpu.make_async_copy(a, b, load_sem.at[n])
        for n, (a, b) in enumerate(
            [
                (adjoint, adjoint_here), (diag, diag_here),
                (off, off_here), (grad_cells, grad_here),
            ]
        )
    ]
    for load in loads:
        load.start()
    pull_exchange = Exchange(message, pulls_in, send_sem.at[0], recv_sem.at[0], own_sem.at[0])
    push_exchange = Exchange(
        push_message, came, send_sem.at[1], recv_sem.at[1], own_sem.at[1]
    )
    halo = Halo(x_out, x_in, y_out, y_in, halo_send, halo_recv)
    place_hots(place, place_lane, place_chunk)
    pulls[...] = jnp.zeros_like(pulls)
    from_places(
        pulled, 6, place_lane, place_chunk, pulls,
        [q * KLO + (q // 3) * KLO for q in range(6)],
    )
    for h in range(KHI):
        for n in range(2):
            message[:, 2 * h + n, :] = pulls[ND * n : ND * (n + 1), ND * h : ND * (h + 1)].T
    greeted()
    pull_exchange.start()
    for load in loads[:3]:
        load.wait()
    stencil(lambda z: cells_at(adjoint_here, z), diag_here, off_here, image, halo, column)
    lane_hots(seg_slots, lane_hot)
    active = active_row(seg_len)
    grad = seg_rows(grad_segs)
    matrix = seg_matrix(seg_diag)
    before = seg_rows(adjoint_segs)
    pull_exchange.wait_recv()
    for h in range(KHI):
        for n in range(2):
            pulls[ND * n : ND * (n + 1), ND * h : ND * (h + 1)] = pulls_in[:, 2 * h + n, :].T
    for c, term in enumerate(slot_terms(pull_blocks, pulls, 0)):
        terms[c * KLO : (c + 1) * KLO, :] = term
    scattered = seg_scatter(terms, seg_slots, lane_hot, table)
    seen = seg_image(before, seg_diag, seg_chain, scattered)
    step = solve_rows(matrix, [grad[c] - seen[c] for c in range(3)])
    after = [before[c] + active * step[c] for c in range(3)]
    for c in range(3):
        adjoint_segs_out[c : c + 1, :] = after[c]
    seg_gather(after, seg_slots, lane_hot, table, push)
    packed = jnp.concatenate(
        slot_terms(push_blocks, push, 0) + [jnp.zeros((KLO, WIDE), F32)], axis=0
    )
    for h in range(KHI):
        push_message[:, h, :] = packed[:, ND * h : ND * (h + 1)].T
    push_exchange.start()
    for c, term in enumerate(slot_terms(pull_blocks, pulls, ND)):
        terms[c * KLO : (c + 1) * KLO, :] = term
    scattered = seg_scatter(terms, seg_slots, lane_hot, table)
    seen = seg_image(after, seg_diag, seg_chain, scattered)
    for c in range(3):
        residual_segs_out[c : c + 1, :] = active * (grad[c] - seen[c])
    halo.wait_recv()
    add_rims(image, halo, column)
    loads[3].wait()
    for c in range(3):
        rest_out[c] = grad_here[c] - image[c, 1 : NZ + 1]
    push_exchange.wait_recv()
    unpack(came, pulls, 3)
    to_places(pulls, 3, place_lane, place_chunk, total, ordered)
    pull_exchange.wait_send()
    push_exchange.wait_send()
    halo.wait_send()


def fourth_kernel(
    starts, ordered, rest, index_rows, adjoint_segs, residual_segs,
    residual_out, adjoint_segs_out, residual_segs_out,
    scattered,
):
    adjoint_segs_out[...] = adjoint_segs[...]
    residual_segs_out[...] = residual_segs[...]
    scattered[...] = jnp.zeros_like(scattered)

    def act(b, j):
        row, lane = chunk_hots(index_rows, j, b)
        scatter_chunk(ordered, 0, j, row, lane, scattered, b)

    each_chunk([starts[b] for b in range(BUCKETS + 1)], act)
    for b in range(BUCKETS):
        for c in range(3):
            at = slice(8 * b, 8 * b + 8)
            residual_out[c, at] = rest[c, at] - scattered_cells(scattered, b, c)


def shape(*dims, kind=F32):
    return jax.ShapeDtypeStruct(dims, kind)


def vmem(*dims, kind=F32):
    return pltpu.VMEM(dims, kind)


def rim_scratch():
    return [
        vmem(2, 3, NZ, CY),
        vmem(2, 3, NZ, CY),
        vmem(2, 8, ROWS),
        vmem(2, 8, ROWS),
        vmem(ROWS, CY),
    ]


def call(kernel, outs, ins, scratch, number=None, in_specs=None, out_specs=None):
    params = dict(vmem_limit_bytes=58 << 20)
    if number is not None:
        params.update(collective_id=number, has_side_effects=True)
    return pl.pallas_call(
        kernel,
        out_shape=outs,
        in_specs=in_specs or [VMEM] * len(ins),
        out_specs=out_specs or [VMEM] * len(outs),
        scratch_shapes=scratch,
        compiler_params=pltpu.CompilerParams(**params),
        name=kernel.__name__,
    )(*ins)


def shards(
    grad_cells, grad_segs, cell_diag, cell_off, seg_diag, seg_chain, seg_len,
    perf_device, perf_local, perf_seg, perf_blocks,
):
    dma = pltpu.SemaphoreType.DMA
    smem = pl.BlockSpec(memory_space=pltpu.SMEM)
    lens = seg_len.reshape(1, 32)
    chain = seg_chain.transpose(1, 2, 0, 3)
    cells = shape(3, NZ, CX, CY)
    segs = shape(3, SEGS)
    tile = vmem(3, NZ, CX, CY)
    diag_tile = vmem(3, 3, NZ, CX, CY)
    off_tile = vmem(6, 3, 3, NZ, CX, CY)
    image = vmem(3, NZ + 2, CX, CY)
    came, seg_slots, push_blocks, pull_blocks, adjoint, rest, adjoint_segs = call(
        first_kernel,
        [
            shape(ND, KHI, ND), shape(KLO, WIDE), shape(9 * KLO, WIDE), shape(9 * KLO, WIDE),
            cells, cells, segs,
        ],
        [
            grad_cells, grad_segs, cell_diag, cell_off, seg_diag, lens,
            perf_device.reshape(1, PERFS), perf_local.reshape(1, PERFS),
            perf_seg.reshape(1, PERFS), perf_blocks.transpose(1, 2, 0, 3),
        ],
        [
            vmem(WIDE, PERFS, kind=BF16),
            vmem(KLO, PERFS),
            vmem(22 * KLO, 512, kind=BF16),
            vmem(22 * KLO, WIDE),
            vmem(11 * KLO, WIDE),
            vmem(128, SLOTS, kind=BF16),
            vmem(48, 128),
            vmem(3 * KLO, WIDE),
            vmem(ND, KHI, ND),
            off_tile,
            diag_tile,
            tile,
            image,
        ]
        + rim_scratch()
        + [dma((3,)), dma, dma, dma, dma((4,)), dma((4,))],
        0,
        [ANY, VMEM, ANY, ANY] + [VMEM] * 6,
    )
    adjoint, pulled, index_rows, place, starts = call(
        second_kernel,
        [
            cells, shape(6 * CROWS, LANES), shape(CROWS, LANES),
            shape(KLO, WIDE, kind=jnp.int32), shape(8, kind=jnp.int32),
        ],
        [came, cell_diag, adjoint, rest],
        [
            vmem(4 * KLO, WIDE),
            vmem(LANES, SLOTS, kind=BF16),
            vmem(CROWS, SLOTS),
            vmem(8 * CROWS, LANES),
            vmem(4 * CROWS, LANES),
            vmem(BUCKETS, 3 * CY, 2 * BROWS, kind=BF16),
            vmem(BUCKETS, 3 * CY, BROWS),
            diag_tile,
            tile,
            tile,
            dma((3,)),
        ],
        None,
        [VMEM] + [ANY] * 3,
        [VMEM] * 4 + [smem],
    )
    ordered, rest, adjoint_segs, residual_segs = call(
        third_kernel,
        [shape(3 * CROWS, LANES), cells, segs, segs],
        [
            pulled, place, grad_cells, adjoint, cell_diag, cell_off,
            grad_segs, adjoint_segs, seg_diag, chain, lens, seg_slots, push_blocks, pull_blocks,
        ],
        [
            vmem(LANES, SLOTS, kind=BF16),
            vmem(CROWS, SLOTS),
            vmem(6 * CROWS, LANES),
            vmem(ND, 4, ND),
            vmem(ND, 4, ND),
            vmem(ND, KHI, ND),
            vmem(ND, KHI, ND),
            vmem(8 * KLO, WIDE),
            vmem(3 * KLO, WIDE),
            vmem(128, SLOTS, kind=BF16),
            vmem(48, 128),
            vmem(3 * KLO, WIDE),
            off_tile,
            diag_tile,
            tile,
            tile,
            image,
        ]
        + rim_scratch()
        + [dma((4,)), dma((2,)), dma((2,)), dma((2,)), dma((4,)), dma((4,))],
        1,
        [VMEM] * 2 + [ANY] * 4 + [VMEM] * 8,
    )
    residual, adjoint_segs, residual_segs = call(
        fourth_kernel,
        [cells, segs, segs],
        [starts, ordered, rest, index_rows, adjoint_segs, residual_segs],
        [vmem(BUCKETS, 3 * CY, BROWS)],
        None,
        [smem] + [VMEM] * 5,
    )
    return adjoint, adjoint_segs, residual, residual_segs


def solution(mesh):
    in_specs = (
        P(None, None, "gx", "gy"),
        P(None, ("gx", "gy")),
        P(None, None, None, "gx", "gy"),
        P(None, None, None, None, "gx", "gy"),
        P(None, None, ("gx", "gy")),
        P(None, None, None, ("gx", "gy")),
        P(("gx", "gy")),
        P(("gx", "gy"), None),
        P(("gx", "gy")),
        P(("gx", "gy")),
        P(None, None, None, ("gx", "gy")),
    )
    out_specs = (
        P(None, None, "gx", "gy"),
        P(None, ("gx", "gy")),
        P(None, None, "gx", "gy"),
        P(None, ("gx", "gy")),
    )
    return jax.shard_map(shards, mesh=mesh, in_specs=in_specs, out_specs=out_specs, check_vma=False)
```

```python
import jax
import jax.numpy as jnp
from jax import lax
from jax.experimental import pallas as pl
from jax.experimental.pallas import tpu as pltpu
from jax.sharding import PartitionSpec as P

MESH = pl.DeviceIdType.MESH
F32 = jnp.float32
BF16 = jnp.bfloat16
NT = (((1,), (1,)), ((), ()))
GX = 8
GY = 16
ND = GX * GY
NZ = 32
CX = 16
CY = 128
ROWS = NZ * CX
SEGS = 1024
SEG_MAX = 32
PERFS = 4096
KLO = 32
KHI = 2
WIDE = KHI * ND
SLOTS = KLO * WIDE
BUCKETS = 4
BROWS = ROWS // BUCKETS
HALF = CY // 2
CHUNK = 512
LANES = 256
CROWS = 40
SPARE = CROWS * LANES // CHUNK - 1
VMEM = pl.BlockSpec(memory_space=pltpu.VMEM)
ANY = pl.BlockSpec(memory_space=pl.ANY)


def rounded(x):
    return x.astype(BF16).astype(F32)


def halves(x):
    high = rounded(x)
    return high, x - high


def iota(shape, dim):
    return lax.broadcasted_iota(jnp.int32, shape, dim)


def one_hot(count, row, kind):
    hit = iota((count, row.shape[1]), 0) == row
    return hit.astype(F32).astype(kind)


def inverse_rows(matrix):
    cofactor = [
        [
            matrix[(i + 1) % 3][(j + 1) % 3] * matrix[(i + 2) % 3][(j + 2) % 3]
            - matrix[(i + 1) % 3][(j + 2) % 3] * matrix[(i + 2) % 3][(j + 1) % 3]
            for j in range(3)
        ]
        for i in range(3)
    ]
    determinant = (
        matrix[0][0] * cofactor[0][0]
        + matrix[0][1] * cofactor[0][1]
        + matrix[0][2] * cofactor[0][2]
    )
    return cofactor, 1.0 / determinant


def solve_rows(matrix, vector):
    cofactor, scale = inverse_rows(matrix)
    return [
        (cofactor[i][0] * vector[0] + cofactor[i][1] * vector[1] + cofactor[i][2] * vector[2])
        * scale
        for i in range(3)
    ]


def transposed_rows(matrix, vector):
    return [
        matrix[0][i] * vector[0] + matrix[1][i] * vector[1] + matrix[2][i] * vector[2]
        for i in range(3)
    ]


def seg_rows(ref):
    return [ref[j : j + 1, :] for j in range(3)]


def seg_matrix(ref):
    return [[ref[i, j : j + 1, :] for j in range(3)] for i in range(3)]


def active_row(seg_len_ref):
    square = iota((32, 32), 0) == iota((32, 32), 1)
    lens = jnp.sum(jnp.where(square, seg_len_ref[...].astype(F32), 0.0), axis=1, keepdims=True)
    lanes = iota((32, SEGS), 1)
    mine = (lanes // SEG_MAX) == iota((32, SEGS), 0)
    below = (lanes % SEG_MAX).astype(F32) < lens
    return jnp.sum(jnp.where(mine & below, 1.0, 0.0), axis=0, keepdims=True)


def four_rows(ref, start, k):
    return jnp.concatenate([ref[pl.ds(start + 4 * k + n, 1), :] for n in range(4)], axis=1)


def put_four_rows(ref, start, k, value):
    for n in range(4):
        ref[pl.ds(start + 4 * k + n, 1), :] = value[:, WIDE * n : WIDE * (n + 1)]


def four_lanes(k):
    return pl.ds(pl.multiple_of(k * 4 * WIDE, 4 * WIDE), 4 * WIDE)


def seg_gather(values, seg_slots, lane_hot_ref, table_ref, out_ref):
    for c in range(3):
        for p, part in enumerate(halves(values[c])):
            for h in range(8):
                at = p * 24 + c * 8 + h
                table_ref[at : at + 1, :] = part[:, 128 * h : 128 * (h + 1)]
    table = table_ref[...].astype(BF16)

    def body(k, _):
        found = jnp.dot(table, lane_hot_ref[:, four_lanes(k)], preferred_element_type=F32)
        found = found[:24] + found[24:]
        high = four_rows(seg_slots, 0, k).astype(jnp.int32) >> 7
        pick = (iota((8, 4 * WIDE), 0) == high).astype(F32)
        for c in range(3):
            value = jnp.sum(found[8 * c : 8 * c + 8] * pick, axis=0, keepdims=True)
            put_four_rows(out_ref, c * KLO, k, value)
        return 0

    lax.fori_loop(0, KLO // 4, body, 0, unroll=2)


def seg_scatter(values_ref, seg_slots, lane_hot_ref, table_ref):
    def body(k, total):
        high = four_rows(seg_slots, 0, k).astype(jnp.int32) >> 7
        pick = (iota((8, 4 * WIDE), 0) == high).astype(F32)
        right = []
        for c in range(3):
            right += [pick * part for part in halves(four_rows(values_ref, c * KLO, k))]
        return total + lax.dot_general(
            lane_hot_ref[:, four_lanes(k)],
            jnp.concatenate(right, axis=0).astype(BF16),
            NT,
            preferred_element_type=F32,
        )

    total = lax.fori_loop(0, KLO // 4, body, jnp.zeros((128, 48), F32), unroll=2)
    turned = jnp.concatenate([total, jnp.zeros((128, 80), F32)], axis=1).T
    rows = []
    for c in range(3):
        table_ref[0:8, :] = turned[16 * c : 16 * c + 8] + turned[16 * c + 8 : 16 * c + 16]
        rows.append(jnp.concatenate([table_ref[h : h + 1, :] for h in range(8)], axis=1))
    return rows


def lane_hots(seg_slots, lane_hot_ref):
    def body(k, _):
        low = four_rows(seg_slots, 0, k).astype(jnp.int32) & 127
        lane_hot_ref[:, four_lanes(k)] = one_hot(128, low, BF16)
        return 0

    lax.fori_loop(0, KLO // 4, body, 0)


def slot_terms(blocks, rows_ref, start):
    vector = [rows_ref[start + c * KLO : start + (c + 1) * KLO, :] for c in range(3)]
    out = []
    for i in range(3):
        total = None
        for j in range(3):
            at = (j * 3 + i) * KLO
            term = blocks[at : at + KLO, :] * vector[j]
            total = term if total is None else total + term
        out.append(total)
    return out


def everyone(act):
    gx = lax.axis_index("gx")
    gy = lax.axis_index("gy")
    me = gx * GY + gy

    def body(i, _):
        other = lax.rem(me + i, ND)
        act(other, (other // GY, lax.rem(other, GY)))
        return 0

    lax.fori_loop(1, ND, body, 0)


def greet():
    barrier = pltpu.get_barrier_semaphore()
    everyone(
        lambda other, place: pl.semaphore_signal(
            barrier, inc=1, device_id=place, device_id_type=MESH
        )
    )


def greeted():
    pl.semaphore_wait(pltpu.get_barrier_semaphore(), ND - 1)


class Exchange:
    def __init__(self, source, target, send_sem, recv_sem, own_sem):
        self.source, self.target = source, target
        self.send_sem, self.recv_sem, self.own_sem = send_sem, recv_sem, own_sem
        self.me = lax.axis_index("gx") * GY + lax.axis_index("gy")

    def own(self):
        return pltpu.make_async_copy(
            self.source.at[self.me], self.target.at[self.me], self.own_sem
        )

    def whole(self):
        return pltpu.make_async_remote_copy(
            src_ref=self.source.at[pl.ds(0, ND - 1)],
            dst_ref=self.target.at[pl.ds(0, ND - 1)],
            send_sem=self.send_sem,
            recv_sem=self.recv_sem,
            device_id=(lax.axis_index("gx"), lax.axis_index("gy")),
            device_id_type=MESH,
        )

    def start(self):
        self.own().start()
        everyone(
            lambda other, place: pltpu.make_async_remote_copy(
                src_ref=self.source.at[other],
                dst_ref=self.target.at[self.me],
                send_sem=self.send_sem,
                recv_sem=self.recv_sem,
                device_id=place,
                device_id_type=MESH,
            ).start()
        )

    def wait_recv(self):
        self.own().wait()
        self.whole().wait_recv()

    def wait_send(self):
        self.whole().wait_send()


class Halo:
    def __init__(self, x_out, x_in, y_out, y_in, send_sem, recv_sem):
        gx = lax.axis_index("gx")
        gy = lax.axis_index("gy")
        places = [
            (lax.rem(gx + 1, GX), gy),
            (lax.rem(gx + GX - 1, GX), gy),
            (gx, lax.rem(gy + 1, GY)),
            (gx, lax.rem(gy + GY - 1, GY)),
        ]
        pairs = [(x_out, x_in, 0), (x_out, x_in, 1), (y_out, y_in, 0), (y_out, y_in, 1)]
        self.copies = [
            pltpu.make_async_remote_copy(
                src_ref=a.at[n],
                dst_ref=b.at[n],
                send_sem=send_sem.at[at],
                recv_sem=recv_sem.at[at],
                device_id=place,
                device_id_type=MESH,
            )
            for at, ((a, b, n), place) in enumerate(zip(pairs, places))
        ]
        self.x_out, self.x_in, self.y_out, self.y_in = x_out, x_in, y_out, y_in

    def start(self):
        for copy in self.copies:
            copy.start()

    def wait_recv(self):
        for copy in self.copies:
            copy.wait_recv()

    def wait_send(self):
        for copy in self.copies:
            copy.wait_send()


def stencil_sides(adjoint, off_ref, image_ref, halo, column_ref):
    rows = iota((CX, CY), 0)
    lanes = iota((CX, CY), 1)

    def body(z, _):
        a = adjoint(z)
        moved = [
            transposed_rows([[off_ref[e, j, i, z] for i in range(3)] for j in range(3)], a)
            for e in range(4)
        ]
        at = pl.ds(pl.multiple_of(z * CX, CX), CX)
        for c in range(3):
            halo.x_out[0, c, pl.ds(z, 1), :] = moved[0][c][CX - 1 : CX]
            halo.x_out[1, c, pl.ds(z, 1), :] = moved[1][c][0:1]
            right = pltpu.roll(moved[2][c], 1, 1)
            left = pltpu.roll(moved[3][c], CY - 1, 1)
            column_ref[c, at, :] = jnp.where(lanes < HALF, right, left)
            total = jnp.where(rows == 0, 0.0, pltpu.roll(moved[0][c], 1, 0))
            total += jnp.where(rows == CX - 1, 0.0, pltpu.roll(moved[1][c], CX - 1, 0))
            total += jnp.where(lanes == 0, 0.0, right)
            total += jnp.where(lanes == CY - 1, 0.0, left)
            image_ref[c, z + 1] = total
        return 0

    lax.fori_loop(0, NZ, body, 0, unroll=2)
    for c in range(3):
        turned = column_ref[c].T
        halo.y_out[0, c : c + 1, :] = turned[0:1]
        halo.y_out[1, c : c + 1, :] = turned[CY - 1 : CY]
    halo.start()


def stencil_layers(adjoint, diag_ref, off_ref, image_ref):
    for c in range(3):
        image_ref[c, 0] = jnp.zeros((CX, CY), F32)
        image_ref[c, NZ + 1] = jnp.zeros((CX, CY), F32)

    def body(z, _):
        a = adjoint(z)
        own = transposed_rows([[diag_ref[j, i, z] for i in range(3)] for j in range(3)], a)
        rising, falling = [
            transposed_rows([[off_ref[e, j, i, z] for i in range(3)] for j in range(3)], a)
            for e in (4, 5)
        ]
        for c in range(3):
            image_ref[c, z + 1] += own[c]
            image_ref[c, z + 2] += rising[c]
            image_ref[c, z] += falling[c]
        return 0

    lax.fori_loop(0, NZ, body, 0, unroll=2)


def add_rims(image_ref, halo, column_ref):
    gx = lax.axis_index("gx")
    gy = lax.axis_index("gy")
    first_x = jnp.where(gx > 0, 1.0, 0.0)
    last_x = jnp.where(gx < GX - 1, 1.0, 0.0)
    first_y = jnp.where(gy > 0, 1.0, 0.0)
    last_y = jnp.where(gy < GY - 1, 1.0, 0.0)
    eight = iota((8, ROWS), 0)
    for c in range(3):
        top = jnp.where(eight == 0, halo.y_in[0, c : c + 1, :] * first_y, 0.0)
        bottom = jnp.where(eight == 7, halo.y_in[1, c : c + 1, :] * last_y, 0.0)
        column_ref[c] = jnp.concatenate([top, jnp.zeros((CY - 16, ROWS), F32), bottom], axis=0).T
    rows = iota((CX, CY), 0)

    def body(z, _):
        at = pl.ds(pl.multiple_of(z * CX, CX), CX)
        for c in range(3):
            low = halo.x_in[0, c, pl.ds(z, 1), :] * first_x
            high = halo.x_in[1, c, pl.ds(z, 1), :] * last_x
            total = jnp.where(rows == 0, low, 0.0) + jnp.where(rows == CX - 1, high, 0.0)
            image_ref[c, z + 1] += total + column_ref[c, at, :]
        return 0

    lax.fori_loop(0, NZ, body, 0, unroll=2)


def rank_rows(device_ref, column_ref, row_ref):
    above = (iota((256, 256), 0) < iota((256, 256), 1)).astype(F32).astype(BF16)
    ones = jnp.ones((256, 256), BF16)
    carry = jnp.zeros((ND, 256), F32)
    for j in range(PERFS // 256):
        at = slice(256 * j, 256 * (j + 1))
        target = device_ref[:, at]
        hit = one_hot(ND, target, F32)
        hit16 = hit.astype(BF16)
        before = jnp.dot(hit16, above, preferred_element_type=F32) + carry
        carry = carry + jnp.dot(hit16, ones, preferred_element_type=F32)
        rank = jnp.sum(before * hit, axis=0, keepdims=True).astype(jnp.int32)
        column_ref[:, at] = one_hot(WIDE, target + ND * (rank >> 5), BF16)
        row_ref[:, at] = one_hot(KLO, rank & (KLO - 1), F32)


def place_rows(row, count, column_ref, row_ref, work_ref, total_ref, out_ref):
    size = count * KLO
    for j in range(PERFS // 512):
        at = slice(512 * j, 512 * (j + 1))
        row_hot = row_ref[:, at]
        for q in range(count):
            for p, part in enumerate(halves(row(q, at))):
                put = p * size + q * KLO
                work_ref[put : put + KLO, :] = (row_hot * part).astype(BF16)
        part = lax.dot_general(
            work_ref[0 : 2 * size, :], column_ref[:, at], NT, preferred_element_type=F32
        )
        if j == 0:
            total_ref[0 : 2 * size, :] = part
        else:
            total_ref[0 : 2 * size, :] += part
    out_ref[...] = total_ref[0:size, :] + total_ref[size : 2 * size, :]


def cells_at(ref, z):
    return [ref[c, z] for c in range(3)]


def first_kernel(
    grad_cells, grad_segs, diag, off, seg_diag, seg_len, device, local, seg, blocks,
    came, seg_slots_out, push_out, pull_out, adjoint_out, rest_out, adjoint_segs_out,
    column_hot, row_hot, work, total, slots, pull_blocks, lane_hot, table, push, message,
    off_here, diag_here, grad_here, adjoint, image,
    x_out, x_in, y_out, y_in, column,
    load_sem, store_sem, send_sem, recv_sem, own_sem, halo_send, halo_recv,
):
    loads = [
        pltpu.make_async_copy(a, b, load_sem.at[n])
        for n, (a, b) in enumerate(
            [(diag, diag_here), (grad_cells, grad_here), (off, off_here)]
        )
    ]
    for load in loads:
        load.start()
    greet()
    exchange = Exchange(message, came, send_sem, recv_sem, own_sem)
    halo = Halo(x_out, x_in, y_out, y_in, halo_send, halo_recv)
    rank_rows(device, column_hot, row_hot)

    def first_rows(q, at):
        if q == 0:
            return (local[:, at] + 1).astype(F32)
        if q == 1:
            return seg[:, at].astype(F32)
        return blocks[(q - 2) // 3, (q - 2) % 3, 0:1, at]

    place_rows(first_rows, 11, column_hot, row_hot, work, total, slots)
    active = active_row(seg_len)
    adjoint_segs = [
        active * row for row in solve_rows(seg_matrix(seg_diag), seg_rows(grad_segs))
    ]
    for c in range(3):
        adjoint_segs_out[c : c + 1, :] = adjoint_segs[c]
    seg_slots = slots.at[pl.ds(KLO, KLO)]
    push_blocks = slots.at[pl.ds(2 * KLO, 9 * KLO)]
    stores = [
        pltpu.make_async_copy(a, b, store_sem.at[n])
        for n, (a, b) in enumerate(
            [
                (seg_slots, seg_slots_out), (push_blocks, push_out),
                (adjoint, adjoint_out), (pull_blocks, pull_out), (grad_here, rest_out),
            ]
        )
    ]
    stores[0].start()
    stores[1].start()
    lane_hots(seg_slots, lane_hot)
    seg_gather(adjoint_segs, seg_slots, lane_hot, table, push)
    terms = slot_terms(push_blocks, push, 0)
    packed = jnp.concatenate([slots[0:KLO, :]] + terms, axis=0)
    for h in range(KHI):
        message[:, h, :] = packed[:, ND * h : ND * (h + 1)].T
    loads[0].wait()
    loads[1].wait()

    def begin(z, _):
        a = solve_rows(
            [[diag_here[i, j, z] for j in range(3)] for i in range(3)], cells_at(grad_here, z)
        )
        for c in range(3):
            adjoint[c, z] = a[c]
        return 0

    lax.fori_loop(0, NZ, begin, 0, unroll=2)
    stores[2].start()
    loads[2].wait()
    greeted()
    stencil_sides(lambda z: cells_at(adjoint, z), off_here, image, halo, column)
    exchange.start()
    stencil_layers(lambda z: cells_at(adjoint, z), diag_here, off_here, image)
    place_rows(
        lambda q, at: blocks[q // 3, q % 3, 1:2, at],
        9, column_hot, row_hot, work, total, pull_blocks,
    )
    stores[3].start()
    halo.wait_recv()
    add_rims(image, halo, column)
    for c in range(3):
        grad_here[c] = grad_here[c] - image[c, 1 : NZ + 1]
    stores[4].start()
    exchange.wait_recv()
    for store in stores:
        store.wait()
    exchange.wait_send()
    halo.wait_send()


def place_slots(index, place_ref, starts):
    row = (index - 1) >> 7
    parts = []
    for b in range(BUCKETS):
        parts.append(((index > 0) & ((row // BROWS) == b)).astype(F32))
    hit = jnp.concatenate(parts, axis=0)
    hit16 = hit.astype(BF16)
    above = (iota((WIDE, WIDE), 0) < iota((WIDE, WIDE), 1)).astype(F32).astype(BF16)
    within = jnp.dot(hit16, above, preferred_element_type=F32)
    totals = jnp.dot(hit16, jnp.ones((WIDE, WIDE), BF16), preferred_element_type=F32)
    r0 = iota((BUCKETS * KLO, BUCKETS * KLO), 0)
    r1 = iota((BUCKETS * KLO, BUCKETS * KLO), 1)
    lower = ((r1 < r0) & ((r1 // KLO) == (r0 // KLO))).astype(F32).astype(BF16)
    earlier = jnp.dot(lower, totals.astype(BF16), preferred_element_type=F32)
    before = within + earlier
    place = jnp.full((KLO, WIDE), -1.0, F32)
    for b in range(BUCKETS):
        at = slice(b * KLO, (b + 1) * KLO)
        base = (starts[b] * CHUNK).astype(F32)
        place = jnp.where(hit[at] > 0, before[at] + base, place)
    place_ref[...] = place.astype(jnp.int32)


def bucket_starts(index):
    row = (index - 1) >> 7
    starts = [jnp.int32(0)]
    for b in range(BUCKETS):
        held = ((index > 0) & ((row // BROWS) == b)).astype(jnp.int32)
        count = jnp.sum(held)
        starts.append(starts[-1] + (count + CHUNK - 1) // CHUNK)
    return starts


def place_hots(place_ref, lane_ref, chunk_ref):
    def body(k, _):
        place = four_rows(place_ref, 0, k)
        lane_ref[:, four_lanes(k)] = one_hot(LANES, place & (LANES - 1), BF16)
        chunk_ref[:, four_lanes(k)] = one_hot(CROWS, place >> 8, F32)
        return 0

    lax.fori_loop(0, KLO // 4, body, 0)


def to_places(rows_ref, count, lane_ref, chunk_ref, total_ref, out_ref):
    size = count * CROWS

    def body(k, _):
        chunk = chunk_ref[:, four_lanes(k)]
        left = [[], []]
        for q in range(count):
            for p, part in enumerate(halves(four_rows(rows_ref, q * KLO, k))):
                left[p].append(chunk * part)
        total_ref[0 : 2 * size, :] += lax.dot_general(
            jnp.concatenate(left[0] + left[1], axis=0).astype(BF16),
            lane_ref[:, four_lanes(k)],
            NT,
            preferred_element_type=F32,
        )
        return 0

    total_ref[...] = jnp.zeros_like(total_ref)
    lax.fori_loop(0, KLO // 4, body, 0, unroll=2)
    out_ref[...] = total_ref[0:size, :] + total_ref[size : 2 * size, :]


def from_places(rows_ref, count, lane_ref, chunk_ref, out_ref, starts):
    size = count * CROWS
    both = jnp.concatenate(halves(rows_ref[...]), axis=0).astype(BF16)

    def body(k, _):
        chunk = chunk_ref[:, four_lanes(k)]
        found = jnp.dot(both, lane_ref[:, four_lanes(k)], preferred_element_type=F32)
        for q in range(count):
            at = q * CROWS
            value = found[at : at + CROWS] + found[size + at : size + at + CROWS]
            put_four_rows(
                out_ref, starts[q], k, jnp.sum(value * chunk, axis=0, keepdims=True)
            )
        return 0

    lax.fori_loop(0, KLO // 4, body, 0, unroll=2)


def turn_cells(cells, turned_ref):
    for c in range(3):
        for b in range(BUCKETS):
            for p, part in enumerate(halves(cells(c, b).T)):
                at = (3 * p + c) * HALF
                turned_ref[b, at : at + HALF, 0:BROWS] = part[:HALF].astype(BF16)
                turned_ref[b, at : at + HALF, BROWS : 2 * BROWS] = part[HALF:].astype(BF16)


def chunk_row(ref, start, j):
    rows = CHUNK // LANES
    if rows == 1:
        return ref[pl.ds(start + j, 1), :]
    return jnp.concatenate([ref[pl.ds(start + rows * j + n, 1), :] for n in range(rows)], axis=1)


def chunk_hots(index_ref, j, b):
    index = chunk_row(index_ref, 0, j).astype(jnp.int32) - 1
    row = (index >> 7) - BROWS * b + ((index >> 6) & 1) * BROWS
    row = one_hot(2 * BROWS, jnp.where(index >= 0, row, -1), BF16)
    lane = one_hot(HALF, index & (HALF - 1), F32)
    return row, lane


def gather_chunk(turned, row, lane, out_ref, start, j):
    found = jnp.dot(turned, row, preferred_element_type=F32)
    found = found[: 3 * HALF] + found[3 * HALF :]
    for c in range(3):
        value = jnp.sum(found[c * HALF : (c + 1) * HALF] * lane, axis=0, keepdims=True)
        rows = CHUNK // LANES
        for n in range(rows):
            out_ref[pl.ds(start + c * CROWS + rows * j + n, 1), :] = value[
                :, LANES * n : LANES * (n + 1)
            ]


def scatter_chunk(values_ref, start, j, row, lane, total_ref, b):
    high, low = [], []
    for c in range(3):
        one, two = halves(chunk_row(values_ref, start + c * CROWS, j))
        high.append(lane * one)
        low.append(lane * two)
    part = lax.dot_general(
        jnp.concatenate(high + low, axis=0).astype(BF16), row, NT, preferred_element_type=F32
    )
    total_ref[b] += part[: 3 * HALF] + part[3 * HALF :]


def each_chunk(starts, act):
    counts = [starts[b + 1] - starts[b] for b in range(BUCKETS)]
    steps = counts[0]
    for count in counts[1:]:
        steps = jnp.maximum(steps, count)

    def body(t, _):
        for b in range(BUCKETS):
            act(b, jnp.where(t < counts[b], starts[b] + t, SPARE))
        return 0

    lax.fori_loop(0, steps, body, 0)


def scattered_cells(total_ref, b, c):
    part = total_ref[b, c * HALF : (c + 1) * HALF, :]
    whole = jnp.concatenate([part[:, :BROWS], part[:, BROWS:]], axis=0)
    return whole.T.reshape(NZ // BUCKETS, CX, CY)


def unpack(came, rows_ref, comps):
    for h in range(KHI):
        rows_ref[0 : comps * KLO, ND * h : ND * (h + 1)] = came[:, h, :].T[0 : comps * KLO]


def second_kernel(
    came, diag, adjoint, rest,
    adjoint_out, pulled, index_out, place, starts_out,
    rows, lane_hot, chunk_hot, total, ordered, turned, scattered,
    diag_here, adjoint_here, rest_here, load_sem, store_sem,
):
    loads = [
        pltpu.make_async_copy(a, b, load_sem.at[n])
        for n, (a, b) in enumerate(
            [(adjoint, adjoint_here), (diag, diag_here), (rest, rest_here)]
        )
    ]
    for load in loads:
        load.start()
    unpack(came, rows, 4)
    index = rows[0:KLO, :].astype(jnp.int32)
    starts = bucket_starts(index)
    place_slots(index, place, starts)
    place_hots(place, lane_hot, chunk_hot)
    to_places(rows, 4, lane_hot, chunk_hot, total, ordered)
    loads[0].wait()
    turn_cells(
        lambda c, b: adjoint_here[c, 8 * b : 8 * b + 8].reshape(BROWS, CY),
        turned,
    )
    scattered[...] = jnp.zeros_like(scattered)
    pulled[...] = jnp.zeros_like(pulled)
    index_rows = ordered.at[pl.ds(0, CROWS)]

    def first(b, j):
        row, lane = chunk_hots(index_rows, j, b)
        gather_chunk(turned[b], row, lane, pulled, 0, j)
        scatter_chunk(ordered, CROWS, j, row, lane, scattered, b)

    each_chunk(starts, first)
    loads[1].wait()
    loads[2].wait()
    for b in range(BUCKETS):
        for c in range(3):
            at = slice(8 * b, 8 * b + 8)
            rest_here[c, at] = rest_here[c, at] - scattered_cells(scattered, b, c)

    def update(z, _):
        step = solve_rows(
            [[diag_here[i, j, z] for j in range(3)] for i in range(3)], cells_at(rest_here, z)
        )
        for c in range(3):
            adjoint_here[c, z] += step[c]
        return 0

    lax.fori_loop(0, NZ, update, 0, unroll=2)
    store = pltpu.make_async_copy(adjoint_here, adjoint_out, store_sem)
    store.start()
    turn_cells(
        lambda c, b: adjoint_here[c, 8 * b : 8 * b + 8].reshape(BROWS, CY),
        turned,
    )

    def second(b, j):
        row, lane = chunk_hots(index_rows, j, b)
        gather_chunk(turned[b], row, lane, pulled, 3 * CROWS, j)

    each_chunk(starts, second)
    index_out[...] = ordered[0:CROWS, :]
    for b in range(BUCKETS + 1):
        starts_out[b] = starts[b]
    store.wait()


def seg_image(adjoint, diag, chain, scattered):
    position = iota((1, SEGS), 1) % SEG_MAX
    own = transposed_rows(seg_matrix(diag), adjoint)
    lower, upper = [
        transposed_rows(
            [[chain[i, j, n : n + 1, :] for j in range(3)] for i in range(3)], adjoint
        )
        for n in range(2)
    ]
    out = []
    for c in range(3):
        total = own[c] + scattered[c]
        total += jnp.where(position == SEG_MAX - 1, 0.0, pltpu.roll(lower[c], SEGS - 1, 1))
        total += jnp.where(position == 0, 0.0, pltpu.roll(upper[c], 1, 1))
        out.append(total)
    return out


def third_kernel(
    pulled, place, grad_cells, adjoint, diag, off,
    grad_segs, adjoint_segs, seg_diag, seg_chain, seg_len, seg_slots, push_blocks, pull_blocks,
    ordered, rest_out, adjoint_segs_out, residual_segs_out,
    place_lane, place_chunk, total, message, pulls_in, late_message, late_in, push_message, came,
    pulls, terms, lane_hot, table, push, off_here, diag_here, grad_here, adjoint_here, image,
    x_out, x_in, y_out, y_in, column,
    load_sem, store_sem, send_sem, recv_sem, own_sem, halo_send, halo_recv,
):
    greet()
    loads = [
        pltpu.make_async_copy(a, b, load_sem.at[n])
        for n, (a, b) in enumerate(
            [
                (adjoint, adjoint_here), (diag, diag_here),
                (off, off_here), (grad_cells, grad_here),
            ]
        )
    ]
    for load in loads:
        load.start()
    pull_exchange = Exchange(message, pulls_in, send_sem.at[0], recv_sem.at[0], own_sem.at[0])
    push_exchange = Exchange(
        push_message, came, send_sem.at[1], recv_sem.at[1], own_sem.at[1]
    )
    late_exchange = Exchange(
        late_message, late_in, send_sem.at[2], recv_sem.at[2], own_sem.at[2]
    )
    halo = Halo(x_out, x_in, y_out, y_in, halo_send, halo_recv)
    place_hots(place, place_lane, place_chunk)
    pulls[...] = jnp.zeros_like(pulls)
    from_places(
        pulled.at[pl.ds(0, 3 * CROWS)], 3, place_lane, place_chunk, pulls, [0, KLO, 2 * KLO]
    )
    for h in range(KHI):
        message[:, h, :] = pulls[0:ND, ND * h : ND * (h + 1)].T
    lane_hots(seg_slots, lane_hot)
    greeted()
    pull_exchange.start()
    from_places(
        pulled.at[pl.ds(3 * CROWS, 3 * CROWS)], 3, place_lane, place_chunk, pulls,
        [ND, ND + KLO, ND + 2 * KLO],
    )
    for h in range(KHI):
        late_message[:, h, :] = pulls[ND : 2 * ND, ND * h : ND * (h + 1)].T
    late_exchange.start()
    for load in loads[:3]:
        load.wait()
    stencil_sides(lambda z: cells_at(adjoint_here, z), off_here, image, halo, column)
    active = active_row(seg_len)
    grad = seg_rows(grad_segs)
    matrix = seg_matrix(seg_diag)
    before = seg_rows(adjoint_segs)
    pull_exchange.wait_recv()
    unpack(pulls_in, pulls, 3)
    for c, term in enumerate(slot_terms(pull_blocks, pulls, 0)):
        terms[c * KLO : (c + 1) * KLO, :] = term
    scattered = seg_scatter(terms, seg_slots, lane_hot, table)
    seen = seg_image(before, seg_diag, seg_chain, scattered)
    step = solve_rows(matrix, [grad[c] - seen[c] for c in range(3)])
    after = [before[c] + active * step[c] for c in range(3)]
    for c in range(3):
        adjoint_segs_out[c : c + 1, :] = after[c]
    seg_gather(after, seg_slots, lane_hot, table, push)
    packed = jnp.concatenate(
        slot_terms(push_blocks, push, 0) + [jnp.zeros((KLO, WIDE), F32)], axis=0
    )
    for h in range(KHI):
        push_message[:, h, :] = packed[:, ND * h : ND * (h + 1)].T
    push_exchange.start()
    stencil_layers(lambda z: cells_at(adjoint_here, z), diag_here, off_here, image)
    late_exchange.wait_recv()
    unpack(late_in, pulls, 3)
    for c, term in enumerate(slot_terms(pull_blocks, pulls, 0)):
        terms[c * KLO : (c + 1) * KLO, :] = term
    scattered = seg_scatter(terms, seg_slots, lane_hot, table)
    seen = seg_image(after, seg_diag, seg_chain, scattered)
    for c in range(3):
        residual_segs_out[c : c + 1, :] = active * (grad[c] - seen[c])
    halo.wait_recv()
    add_rims(image, halo, column)
    loads[3].wait()
    for c in range(3):
        grad_here[c] = grad_here[c] - image[c, 1 : NZ + 1]
    store = pltpu.make_async_copy(grad_here, rest_out, store_sem)
    store.start()
    push_exchange.wait_recv()
    unpack(came, pulls, 3)
    to_places(pulls, 3, place_lane, place_chunk, total, ordered)
    store.wait()
    late_exchange.wait_send()
    pull_exchange.wait_send()
    push_exchange.wait_send()
    halo.wait_send()


def fourth_kernel(
    starts, ordered, rest, index_rows, adjoint_segs, residual_segs,
    residual_out, adjoint_segs_out, residual_segs_out,
    scattered,
):
    adjoint_segs_out[...] = adjoint_segs[...]
    residual_segs_out[...] = residual_segs[...]
    scattered[...] = jnp.zeros_like(scattered)

    def act(b, j):
        row, lane = chunk_hots(index_rows, j, b)
        scatter_chunk(ordered, 0, j, row, lane, scattered, b)

    each_chunk([starts[b] for b in range(BUCKETS + 1)], act)
    for b in range(BUCKETS):
        for c in range(3):
            at = slice(8 * b, 8 * b + 8)
            residual_out[c, at] = rest[c, at] - scattered_cells(scattered, b, c)


def shape(*dims, kind=F32):
    return jax.ShapeDtypeStruct(dims, kind)


def vmem(*dims, kind=F32):
    return pltpu.VMEM(dims, kind)


def rim_scratch():
    return [
        vmem(2, 3, NZ, CY),
        vmem(2, 3, NZ, CY),
        vmem(2, 3, ROWS),
        vmem(2, 3, ROWS),
        vmem(3, ROWS, CY),
    ]


def call(kernel, outs, ins, scratch, number=None, in_specs=None, out_specs=None):
    params = dict(vmem_limit_bytes=58 << 20)
    if number is not None:
        params.update(collective_id=number, has_side_effects=True)
    return pl.pallas_call(
        kernel,
        out_shape=outs,
        in_specs=in_specs or [VMEM] * len(ins),
        out_specs=out_specs or [VMEM] * len(outs),
        scratch_shapes=scratch,
        compiler_params=pltpu.CompilerParams(**params),
        name=kernel.__name__,
    )(*ins)


def shards(
    grad_cells, grad_segs, cell_diag, cell_off, seg_diag, seg_chain, seg_len,
    perf_device, perf_local, perf_seg, perf_blocks,
):
    dma = pltpu.SemaphoreType.DMA
    smem = pl.BlockSpec(memory_space=pltpu.SMEM)
    lens = seg_len.reshape(1, 32)
    chain = seg_chain.transpose(1, 2, 0, 3)
    cells = shape(3, NZ, CX, CY)
    segs = shape(3, SEGS)
    tile = vmem(3, NZ, CX, CY)
    diag_tile = vmem(3, 3, NZ, CX, CY)
    off_tile = vmem(6, 3, 3, NZ, CX, CY)
    image = vmem(3, NZ + 2, CX, CY)
    came, seg_slots, push_blocks, pull_blocks, adjoint, rest, adjoint_segs = call(
        first_kernel,
        [
            shape(ND, KHI, ND), shape(KLO, WIDE), shape(9 * KLO, WIDE), shape(9 * KLO, WIDE),
            cells, cells, segs,
        ],
        [
            grad_cells, grad_segs, cell_diag, cell_off, seg_diag, lens,
            perf_device.reshape(1, PERFS), perf_local.reshape(1, PERFS),
            perf_seg.reshape(1, PERFS), perf_blocks.transpose(1, 2, 0, 3),
        ],
        [
            vmem(WIDE, PERFS, kind=BF16),
            vmem(KLO, PERFS),
            vmem(22 * KLO, 512, kind=BF16),
            vmem(22 * KLO, WIDE),
            vmem(11 * KLO, WIDE),
            vmem(9 * KLO, WIDE),
            vmem(128, SLOTS, kind=BF16),
            vmem(48, 128),
            vmem(3 * KLO, WIDE),
            vmem(ND, KHI, ND),
            off_tile,
            diag_tile,
            tile,
            tile,
            image,
        ]
        + rim_scratch()
        + [dma((3,)), dma((5,)), dma, dma, dma, dma((4,)), dma((4,))],
        0,
        [ANY, VMEM, ANY, ANY] + [VMEM] * 6,
        [VMEM] + [ANY] * 5 + [VMEM],
    )
    adjoint, pulled, index_rows, place, starts = call(
        second_kernel,
        [
            cells, shape(6 * CROWS, LANES), shape(CROWS, LANES),
            shape(KLO, WIDE, kind=jnp.int32), shape(8, kind=jnp.int32),
        ],
        [came, cell_diag, adjoint, rest],
        [
            vmem(4 * KLO, WIDE),
            vmem(LANES, SLOTS, kind=BF16),
            vmem(CROWS, SLOTS),
            vmem(8 * CROWS, LANES),
            vmem(4 * CROWS, LANES),
            vmem(BUCKETS, 6 * HALF, 2 * BROWS, kind=BF16),
            vmem(BUCKETS, 3 * HALF, 2 * BROWS),
            diag_tile,
            tile,
            tile,
            dma((3,)),
            dma,
        ],
        None,
        [VMEM] + [ANY] * 3,
        [ANY] + [VMEM] * 3 + [smem],
    )
    ordered, rest, adjoint_segs, residual_segs = call(
        third_kernel,
        [shape(3 * CROWS, LANES), cells, segs, segs],
        [
            pulled, place, grad_cells, adjoint, cell_diag, cell_off,
            grad_segs, adjoint_segs, seg_diag, chain, lens, seg_slots, push_blocks, pull_blocks,
        ],
        [
            vmem(LANES, SLOTS, kind=BF16),
            vmem(CROWS, SLOTS),
            vmem(6 * CROWS, LANES),
            vmem(ND, KHI, ND),
            vmem(ND, KHI, ND),
            vmem(ND, KHI, ND),
            vmem(ND, KHI, ND),
            vmem(ND, KHI, ND),
            vmem(ND, KHI, ND),
            vmem(8 * KLO, WIDE),
            vmem(3 * KLO, WIDE),
            vmem(128, SLOTS, kind=BF16),
            vmem(48, 128),
            vmem(3 * KLO, WIDE),
            off_tile,
            diag_tile,
            tile,
            tile,
            image,
        ]
        + rim_scratch()
        + [dma((4,)), dma, dma((3,)), dma((3,)), dma((3,)), dma((4,)), dma((4,))],
        1,
        [VMEM] * 2 + [ANY] * 4 + [VMEM] * 8,
        [VMEM, ANY, VMEM, VMEM],
    )
    residual, adjoint_segs, residual_segs = call(
        fourth_kernel,
        [cells, segs, segs],
        [starts, ordered, rest, index_rows, adjoint_segs, residual_segs],
        [vmem(BUCKETS, 3 * HALF, 2 * BROWS)],
        None,
        [smem] + [VMEM] * 5,
    )
    return adjoint, adjoint_segs, residual, residual_segs


def solution(mesh):
    in_specs = (
        P(None, None, "gx", "gy"),
        P(None, ("gx", "gy")),
        P(None, None, None, "gx", "gy"),
        P(None, None, None, None, "gx", "gy"),
        P(None, None, ("gx", "gy")),
        P(None, None, None, ("gx", "gy")),
        P(("gx", "gy")),
        P(("gx", "gy"), None),
        P(("gx", "gy")),
        P(("gx", "gy")),
        P(None, None, None, ("gx", "gy")),
    )
    out_specs = (
        P(None, None, "gx", "gy"),
        P(None, ("gx", "gy")),
        P(None, None, "gx", "gy"),
        P(None, ("gx", "gy")),
    )
    return jax.shard_map(shards, mesh=mesh, in_specs=in_specs, out_specs=out_specs, check_vma=False)
```

```python
import jax
import jax.numpy as jnp
from jax import lax
from jax.experimental import pallas as pl
from jax.experimental.pallas import tpu as pltpu
from jax.sharding import PartitionSpec as P

MESH = pl.DeviceIdType.MESH
F32 = jnp.float32
BF16 = jnp.bfloat16
NT = (((1,), (1,)), ((), ()))
GX = 8
GY = 16
ND = GX * GY
NZ = 32
CX = 16
CY = 128
ROWS = NZ * CX
SEGS = 1024
SEG_MAX = 32
PERFS = 4096
KLO = 32
KHI = 2
WIDE = KHI * ND
SLOTS = KLO * WIDE
BUCKETS = 4
BROWS = ROWS // BUCKETS
HALF = CY // 2
CHUNK = 512
LANES = 256
CROWS = 40
SPARE = CROWS * LANES // CHUNK - 1
VMEM = pl.BlockSpec(memory_space=pltpu.VMEM)
ANY = pl.BlockSpec(memory_space=pl.ANY)


def rounded(x):
    return x.astype(BF16).astype(F32)


def halves(x):
    high = rounded(x)
    return high, x - high


def iota(shape, dim):
    return lax.broadcasted_iota(jnp.int32, shape, dim)


def one_hot(count, row, kind):
    hit = iota((count, row.shape[1]), 0) == row
    return hit.astype(F32).astype(kind)


def inverse_rows(matrix):
    cofactor = [
        [
            matrix[(i + 1) % 3][(j + 1) % 3] * matrix[(i + 2) % 3][(j + 2) % 3]
            - matrix[(i + 1) % 3][(j + 2) % 3] * matrix[(i + 2) % 3][(j + 1) % 3]
            for j in range(3)
        ]
        for i in range(3)
    ]
    determinant = (
        matrix[0][0] * cofactor[0][0]
        + matrix[0][1] * cofactor[0][1]
        + matrix[0][2] * cofactor[0][2]
    )
    return cofactor, 1.0 / determinant


def solve_rows(matrix, vector):
    cofactor, scale = inverse_rows(matrix)
    return [
        (cofactor[i][0] * vector[0] + cofactor[i][1] * vector[1] + cofactor[i][2] * vector[2])
        * scale
        for i in range(3)
    ]


def transposed_rows(matrix, vector):
    return [
        matrix[0][i] * vector[0] + matrix[1][i] * vector[1] + matrix[2][i] * vector[2]
        for i in range(3)
    ]


def seg_rows(ref):
    return [ref[j : j + 1, :] for j in range(3)]


def seg_matrix(ref):
    return [[ref[i, j : j + 1, :] for j in range(3)] for i in range(3)]


def active_row(seg_len_ref):
    square = iota((32, 32), 0) == iota((32, 32), 1)
    lens = jnp.sum(jnp.where(square, seg_len_ref[...].astype(F32), 0.0), axis=1, keepdims=True)
    lanes = iota((32, SEGS), 1)
    mine = (lanes // SEG_MAX) == iota((32, SEGS), 0)
    below = (lanes % SEG_MAX).astype(F32) < lens
    return jnp.sum(jnp.where(mine & below, 1.0, 0.0), axis=0, keepdims=True)


def four_rows(ref, start, k):
    return jnp.concatenate([ref[pl.ds(start + 4 * k + n, 1), :] for n in range(4)], axis=1)


def put_four_rows(ref, start, k, value):
    for n in range(4):
        ref[pl.ds(start + 4 * k + n, 1), :] = value[:, WIDE * n : WIDE * (n + 1)]


def four_lanes(k):
    return pl.ds(pl.multiple_of(k * 4 * WIDE, 4 * WIDE), 4 * WIDE)


def seg_gather(values, seg_slots, lane_hot_ref, table_ref, out_ref):
    for c in range(3):
        for p, part in enumerate(halves(values[c])):
            for h in range(8):
                at = p * 24 + c * 8 + h
                table_ref[at : at + 1, :] = part[:, 128 * h : 128 * (h + 1)]
    table = table_ref[...].astype(BF16)

    def body(k, _):
        found = jnp.dot(table, lane_hot_ref[:, four_lanes(k)], preferred_element_type=F32)
        found = found[:24] + found[24:]
        high = four_rows(seg_slots, 0, k).astype(jnp.int32) >> 7
        pick = (iota((8, 4 * WIDE), 0) == high).astype(F32)
        for c in range(3):
            value = jnp.sum(found[8 * c : 8 * c + 8] * pick, axis=0, keepdims=True)
            put_four_rows(out_ref, c * KLO, k, value)
        return 0

    lax.fori_loop(0, KLO // 4, body, 0, unroll=2)


def seg_scatter(values_ref, seg_slots, lane_hot_ref, table_ref):
    def body(k, total):
        high = four_rows(seg_slots, 0, k).astype(jnp.int32) >> 7
        pick = (iota((8, 4 * WIDE), 0) == high).astype(F32)
        right = []
        for c in range(3):
            right += [pick * part for part in halves(four_rows(values_ref, c * KLO, k))]
        return total + lax.dot_general(
            lane_hot_ref[:, four_lanes(k)],
            jnp.concatenate(right, axis=0).astype(BF16),
            NT,
            preferred_element_type=F32,
        )

    total = lax.fori_loop(0, KLO // 4, body, jnp.zeros((128, 48), F32), unroll=2)
    turned = jnp.concatenate([total, jnp.zeros((128, 80), F32)], axis=1).T
    rows = []
    for c in range(3):
        table_ref[0:8, :] = turned[16 * c : 16 * c + 8] + turned[16 * c + 8 : 16 * c + 16]
        rows.append(jnp.concatenate([table_ref[h : h + 1, :] for h in range(8)], axis=1))
    return rows


def lane_hots(seg_slots, lane_hot_ref):
    def body(k, _):
        low = four_rows(seg_slots, 0, k).astype(jnp.int32) & 127
        lane_hot_ref[:, four_lanes(k)] = one_hot(128, low, BF16)
        return 0

    lax.fori_loop(0, KLO // 4, body, 0)


def slot_terms(blocks, rows_ref, start):
    vector = [rows_ref[start + c * KLO : start + (c + 1) * KLO, :] for c in range(3)]
    out = []
    for i in range(3):
        total = None
        for j in range(3):
            at = (j * 3 + i) * KLO
            term = blocks[at : at + KLO, :] * vector[j]
            total = term if total is None else total + term
        out.append(total)
    return out


def everyone(act):
    gx = lax.axis_index("gx")
    gy = lax.axis_index("gy")
    columns = [lax.rem(gy + j, GY) for j in range(GY)]

    def visit(row, distances):
        for j in distances:
            act(row * GY + columns[j], (row, columns[j]))

    visit(gx, range(1, GY))

    def body(i, _):
        visit(lax.rem(gx + i, GX), range(GY))
        return 0

    lax.fori_loop(1, GX, body, 0)


def greet():
    barrier = pltpu.get_barrier_semaphore()
    everyone(
        lambda other, place: pl.semaphore_signal(
            barrier, inc=1, device_id=place, device_id_type=MESH
        )
    )


def greeted():
    pl.semaphore_wait(pltpu.get_barrier_semaphore(), ND - 1)


class Exchange:
    def __init__(self, source, target, send_sem, recv_sem, own_sem):
        self.source, self.target = source, target
        self.send_sem, self.recv_sem, self.own_sem = send_sem, recv_sem, own_sem
        self.me = lax.axis_index("gx") * GY + lax.axis_index("gy")

    def own(self):
        return pltpu.make_async_copy(
            self.source.at[self.me], self.target.at[self.me], self.own_sem
        )

    def whole(self):
        return pltpu.make_async_remote_copy(
            src_ref=self.source.at[pl.ds(0, ND - 1)],
            dst_ref=self.target.at[pl.ds(0, ND - 1)],
            send_sem=self.send_sem,
            recv_sem=self.recv_sem,
            device_id=(lax.axis_index("gx"), lax.axis_index("gy")),
            device_id_type=MESH,
        )

    def start(self):
        self.own().start()
        everyone(
            lambda other, place: pltpu.make_async_remote_copy(
                src_ref=self.source.at[other],
                dst_ref=self.target.at[self.me],
                send_sem=self.send_sem,
                recv_sem=self.recv_sem,
                device_id=place,
                device_id_type=MESH,
            ).start()
        )

    def wait_recv(self):
        self.own().wait()
        self.whole().wait_recv()

    def wait_send(self):
        self.whole().wait_send()


class Halo:
    def __init__(self, x_out, x_in, y_out, y_in, send_sem, recv_sem):
        gx = lax.axis_index("gx")
        gy = lax.axis_index("gy")
        places = [
            (lax.rem(gx + 1, GX), gy),
            (lax.rem(gx + GX - 1, GX), gy),
            (gx, lax.rem(gy + 1, GY)),
            (gx, lax.rem(gy + GY - 1, GY)),
        ]
        pairs = [(x_out, x_in, 0), (x_out, x_in, 1), (y_out, y_in, 0), (y_out, y_in, 1)]
        self.copies = [
            pltpu.make_async_remote_copy(
                src_ref=a.at[n],
                dst_ref=b.at[n],
                send_sem=send_sem.at[at],
                recv_sem=recv_sem.at[at],
                device_id=place,
                device_id_type=MESH,
            )
            for at, ((a, b, n), place) in enumerate(zip(pairs, places))
        ]
        self.x_out, self.x_in, self.y_out, self.y_in = x_out, x_in, y_out, y_in

    def start(self):
        for copy in self.copies:
            copy.start()

    def wait_recv(self):
        for copy in self.copies:
            copy.wait_recv()

    def wait_send(self):
        for copy in self.copies:
            copy.wait_send()


def stencil_sides(adjoint, off_ref, image_ref, halo, column_ref):
    rows = iota((CX, CY), 0)
    lanes = iota((CX, CY), 1)

    def body(z, _):
        a = adjoint(z)
        moved = [
            transposed_rows([[off_ref[e, j, i, z] for i in range(3)] for j in range(3)], a)
            for e in range(4)
        ]
        at = pl.ds(pl.multiple_of(z * CX, CX), CX)
        for c in range(3):
            halo.x_out[0, c, pl.ds(z, 1), :] = moved[0][c][CX - 1 : CX]
            halo.x_out[1, c, pl.ds(z, 1), :] = moved[1][c][0:1]
            right = pltpu.roll(moved[2][c], 1, 1)
            left = pltpu.roll(moved[3][c], CY - 1, 1)
            column_ref[c, at, :] = jnp.where(lanes < HALF, right, left)
            total = jnp.where(rows == 0, 0.0, pltpu.roll(moved[0][c], 1, 0))
            total += jnp.where(rows == CX - 1, 0.0, pltpu.roll(moved[1][c], CX - 1, 0))
            total += jnp.where(lanes == 0, 0.0, right)
            total += jnp.where(lanes == CY - 1, 0.0, left)
            image_ref[c, z + 1] = total
        return 0

    lax.fori_loop(0, NZ, body, 0, unroll=2)
    for c in range(3):
        turned = column_ref[c].T
        halo.y_out[0, c : c + 1, :] = turned[0:1]
        halo.y_out[1, c : c + 1, :] = turned[CY - 1 : CY]
    halo.start()


def stencil_layers(adjoint, diag_ref, off_ref, image_ref):
    for c in range(3):
        image_ref[c, 0] = jnp.zeros((CX, CY), F32)
        image_ref[c, NZ + 1] = jnp.zeros((CX, CY), F32)

    def body(z, _):
        a = adjoint(z)
        own = transposed_rows([[diag_ref[j, i, z] for i in range(3)] for j in range(3)], a)
        rising, falling = [
            transposed_rows([[off_ref[e, j, i, z] for i in range(3)] for j in range(3)], a)
            for e in (4, 5)
        ]
        for c in range(3):
            image_ref[c, z + 1] += own[c]
            image_ref[c, z + 2] += rising[c]
            image_ref[c, z] += falling[c]
        return 0

    lax.fori_loop(0, NZ, body, 0, unroll=2)


def add_rims(image_ref, halo, column_ref):
    gx = lax.axis_index("gx")
    gy = lax.axis_index("gy")
    first_x = jnp.where(gx > 0, 1.0, 0.0)
    last_x = jnp.where(gx < GX - 1, 1.0, 0.0)
    first_y = jnp.where(gy > 0, 1.0, 0.0)
    last_y = jnp.where(gy < GY - 1, 1.0, 0.0)
    eight = iota((8, ROWS), 0)
    for c in range(3):
        top = jnp.where(eight == 0, halo.y_in[0, c : c + 1, :] * first_y, 0.0)
        bottom = jnp.where(eight == 7, halo.y_in[1, c : c + 1, :] * last_y, 0.0)
        column_ref[c] = jnp.concatenate([top, jnp.zeros((CY - 16, ROWS), F32), bottom], axis=0).T
    rows = iota((CX, CY), 0)

    def body(z, _):
        at = pl.ds(pl.multiple_of(z * CX, CX), CX)
        for c in range(3):
            low = halo.x_in[0, c, pl.ds(z, 1), :] * first_x
            high = halo.x_in[1, c, pl.ds(z, 1), :] * last_x
            total = jnp.where(rows == 0, low, 0.0) + jnp.where(rows == CX - 1, high, 0.0)
            image_ref[c, z + 1] += total + column_ref[c, at, :]
        return 0

    lax.fori_loop(0, NZ, body, 0, unroll=2)


def rank_rows(device_ref, column_ref, row_ref):
    above = (iota((256, 256), 0) < iota((256, 256), 1)).astype(F32).astype(BF16)
    ones = jnp.ones((256, 256), BF16)
    carry = jnp.zeros((ND, 256), F32)
    for j in range(PERFS // 256):
        at = slice(256 * j, 256 * (j + 1))
        target = device_ref[:, at]
        hit = one_hot(ND, target, F32)
        hit16 = hit.astype(BF16)
        before = jnp.dot(hit16, above, preferred_element_type=F32) + carry
        carry = carry + jnp.dot(hit16, ones, preferred_element_type=F32)
        rank = jnp.sum(before * hit, axis=0, keepdims=True).astype(jnp.int32)
        column_ref[:, at] = one_hot(WIDE, target + ND * (rank >> 5), BF16)
        row_ref[:, at] = one_hot(KLO, rank & (KLO - 1), F32)


def place_rows(row, count, column_ref, row_ref, work_ref, total_ref, out_ref):
    size = count * KLO
    for j in range(PERFS // 512):
        at = slice(512 * j, 512 * (j + 1))
        row_hot = row_ref[:, at]
        for q in range(count):
            for p, part in enumerate(halves(row(q, at))):
                put = p * size + q * KLO
                work_ref[put : put + KLO, :] = (row_hot * part).astype(BF16)
        part = lax.dot_general(
            work_ref[0 : 2 * size, :], column_ref[:, at], NT, preferred_element_type=F32
        )
        if j == 0:
            total_ref[0 : 2 * size, :] = part
        else:
            total_ref[0 : 2 * size, :] += part
    out_ref[...] = total_ref[0:size, :] + total_ref[size : 2 * size, :]


def cells_at(ref, z):
    return [ref[c, z] for c in range(3)]


def first_kernel(
    grad_cells, grad_segs, diag, off, seg_diag, seg_len, device, local, seg, blocks,
    came, seg_slots_out, push_out, pull_out, adjoint_out, rest_out, adjoint_segs_out,
    column_hot, row_hot, work, total, slots, pull_blocks, lane_hot, table, push, message,
    off_here, diag_here, grad_here, adjoint, image,
    x_out, x_in, y_out, y_in, column,
    load_sem, store_sem, send_sem, recv_sem, own_sem, halo_send, halo_recv,
):
    loads = [
        pltpu.make_async_copy(a, b, load_sem.at[n])
        for n, (a, b) in enumerate(
            [(diag, diag_here), (grad_cells, grad_here), (off, off_here)]
        )
    ]
    for load in loads:
        load.start()
    greet()
    exchange = Exchange(message, came, send_sem, recv_sem, own_sem)
    halo = Halo(x_out, x_in, y_out, y_in, halo_send, halo_recv)
    rank_rows(device, column_hot, row_hot)

    def first_rows(q, at):
        if q == 0:
            return (local[:, at] + 1).astype(F32)
        if q == 1:
            return seg[:, at].astype(F32)
        return blocks[(q - 2) // 3, (q - 2) % 3, 0:1, at]

    place_rows(first_rows, 11, column_hot, row_hot, work, total, slots)
    active = active_row(seg_len)
    adjoint_segs = [
        active * row for row in solve_rows(seg_matrix(seg_diag), seg_rows(grad_segs))
    ]
    for c in range(3):
        adjoint_segs_out[c : c + 1, :] = adjoint_segs[c]
    seg_slots = slots.at[pl.ds(KLO, KLO)]
    push_blocks = slots.at[pl.ds(2 * KLO, 9 * KLO)]
    stores = [
        pltpu.make_async_copy(a, b, store_sem.at[n])
        for n, (a, b) in enumerate(
            [
                (seg_slots, seg_slots_out), (push_blocks, push_out),
                (adjoint, adjoint_out), (pull_blocks, pull_out), (grad_here, rest_out),
            ]
        )
    ]
    stores[0].start()
    stores[1].start()
    lane_hots(seg_slots, lane_hot)
    seg_gather(adjoint_segs, seg_slots, lane_hot, table, push)
    terms = slot_terms(push_blocks, push, 0)
    packed = jnp.concatenate([slots[0:KLO, :]] + terms, axis=0)
    for h in range(KHI):
        message[:, h, :] = packed[:, ND * h : ND * (h + 1)].T
    loads[0].wait()
    loads[1].wait()

    def begin(z, _):
        a = solve_rows(
            [[diag_here[i, j, z] for j in range(3)] for i in range(3)], cells_at(grad_here, z)
        )
        for c in range(3):
            adjoint[c, z] = a[c]
        return 0

    lax.fori_loop(0, NZ, begin, 0, unroll=2)
    stores[2].start()
    loads[2].wait()
    greeted()
    stencil_sides(lambda z: cells_at(adjoint, z), off_here, image, halo, column)
    exchange.start()
    stencil_layers(lambda z: cells_at(adjoint, z), diag_here, off_here, image)
    place_rows(
        lambda q, at: blocks[q // 3, q % 3, 1:2, at],
        9, column_hot, row_hot, work, total, pull_blocks,
    )
    stores[3].start()
    halo.wait_recv()
    add_rims(image, halo, column)
    for c in range(3):
        grad_here[c] = grad_here[c] - image[c, 1 : NZ + 1]
    stores[4].start()
    exchange.wait_recv()
    for store in stores:
        store.wait()
    exchange.wait_send()
    halo.wait_send()


def place_slots(index, place_ref, starts):
    row = (index - 1) >> 7
    parts = []
    for b in range(BUCKETS):
        parts.append(((index > 0) & ((row // BROWS) == b)).astype(F32))
    hit = jnp.concatenate(parts, axis=0)
    hit16 = hit.astype(BF16)
    above = (iota((WIDE, WIDE), 0) < iota((WIDE, WIDE), 1)).astype(F32).astype(BF16)
    within = jnp.dot(hit16, above, preferred_element_type=F32)
    totals = jnp.dot(hit16, jnp.ones((WIDE, WIDE), BF16), preferred_element_type=F32)
    r0 = iota((BUCKETS * KLO, BUCKETS * KLO), 0)
    r1 = iota((BUCKETS * KLO, BUCKETS * KLO), 1)
    lower = ((r1 < r0) & ((r1 // KLO) == (r0 // KLO))).astype(F32).astype(BF16)
    earlier = jnp.dot(lower, totals.astype(BF16), preferred_element_type=F32)
    before = within + earlier
    place = jnp.full((KLO, WIDE), -1.0, F32)
    for b in range(BUCKETS):
        at = slice(b * KLO, (b + 1) * KLO)
        base = (starts[b] * CHUNK).astype(F32)
        place = jnp.where(hit[at] > 0, before[at] + base, place)
    place_ref[...] = place.astype(jnp.int32)


def bucket_starts(index):
    row = (index - 1) >> 7
    starts = [jnp.int32(0)]
    for b in range(BUCKETS):
        held = ((index > 0) & ((row // BROWS) == b)).astype(jnp.int32)
        count = jnp.sum(held)
        starts.append(starts[-1] + (count + CHUNK - 1) // CHUNK)
    return starts


def built_hots(place_ref, k):
    place = four_rows(place_ref, 0, k)
    return one_hot(LANES, place & (LANES - 1), BF16), one_hot(CROWS, place >> 8, F32)


def kept_hots(place_ref, lane_ref, chunk_ref, k):
    lane, chunk = built_hots(place_ref, k)
    lane_ref[:, four_lanes(k)] = lane
    chunk_ref[:, four_lanes(k)] = chunk
    return lane, chunk


def to_places(rows_ref, count, hots, total_ref, out_ref):
    size = count * CROWS

    def body(k, _):
        lane, chunk = hots(k)
        left = [[], []]
        for q in range(count):
            for p, part in enumerate(halves(four_rows(rows_ref, q * KLO, k))):
                left[p].append(chunk * part)
        total_ref[0 : 2 * size, :] += lax.dot_general(
            jnp.concatenate(left[0] + left[1], axis=0).astype(BF16),
            lane,
            NT,
            preferred_element_type=F32,
        )
        return 0

    total_ref[...] = jnp.zeros_like(total_ref)
    lax.fori_loop(0, KLO // 4, body, 0, unroll=2)
    out_ref[...] = total_ref[0:size, :] + total_ref[size : 2 * size, :]


def from_places(rows_ref, count, hots, out_ref, starts):
    size = count * CROWS
    both = jnp.concatenate(halves(rows_ref[...]), axis=0).astype(BF16)

    def body(k, _):
        lane, chunk = hots(k)
        found = jnp.dot(both, lane, preferred_element_type=F32)
        for q in range(count):
            at = q * CROWS
            value = found[at : at + CROWS] + found[size + at : size + at + CROWS]
            put_four_rows(
                out_ref, starts[q], k, jnp.sum(value * chunk, axis=0, keepdims=True)
            )
        return 0

    lax.fori_loop(0, KLO // 4, body, 0, unroll=2)


def turn_cells(cells, turned_ref):
    for c in range(3):
        for b in range(BUCKETS):
            for p, part in enumerate(halves(cells(c, b).T)):
                at = (3 * p + c) * HALF
                turned_ref[b, at : at + HALF, 0:BROWS] = part[:HALF].astype(BF16)
                turned_ref[b, at : at + HALF, BROWS : 2 * BROWS] = part[HALF:].astype(BF16)


def chunk_row(ref, start, j):
    rows = CHUNK // LANES
    if rows == 1:
        return ref[pl.ds(start + j, 1), :]
    return jnp.concatenate([ref[pl.ds(start + rows * j + n, 1), :] for n in range(rows)], axis=1)


def chunk_hots(index_ref, j, b):
    index = chunk_row(index_ref, 0, j).astype(jnp.int32) - 1
    row = (index >> 7) - BROWS * b + ((index >> 6) & 1) * BROWS
    row = one_hot(2 * BROWS, jnp.where(index >= 0, row, -1), BF16)
    lane = one_hot(HALF, index & (HALF - 1), F32)
    return row, lane


def gather_chunk(turned, row, lane, out_ref, start, j):
    found = jnp.dot(turned, row, preferred_element_type=F32)
    found = found[: 3 * HALF] + found[3 * HALF :]
    for c in range(3):
        value = jnp.sum(found[c * HALF : (c + 1) * HALF] * lane, axis=0, keepdims=True)
        rows = CHUNK // LANES
        for n in range(rows):
            out_ref[pl.ds(start + c * CROWS + rows * j + n, 1), :] = value[
                :, LANES * n : LANES * (n + 1)
            ]


def scatter_chunk(values_ref, start, j, row, lane, total_ref, b):
    high, low = [], []
    for c in range(3):
        one, two = halves(chunk_row(values_ref, start + c * CROWS, j))
        high.append(lane * one)
        low.append(lane * two)
    part = lax.dot_general(
        jnp.concatenate(high + low, axis=0).astype(BF16), row, NT, preferred_element_type=F32
    )
    total_ref[b] += part[: 3 * HALF] + part[3 * HALF :]


def each_chunk(starts, act):
    counts = [starts[b + 1] - starts[b] for b in range(BUCKETS)]
    steps = counts[0]
    for count in counts[1:]:
        steps = jnp.maximum(steps, count)

    def body(t, _):
        for b in range(BUCKETS):
            act(b, jnp.where(t < counts[b], starts[b] + t, SPARE))
        return 0

    lax.fori_loop(0, steps, body, 0)


def scattered_cells(total_ref, b, c):
    part = total_ref[b, c * HALF : (c + 1) * HALF, :]
    whole = jnp.concatenate([part[:, :BROWS], part[:, BROWS:]], axis=0)
    return whole.T.reshape(NZ // BUCKETS, CX, CY)


def unpack(came, rows_ref, comps):
    for h in range(KHI):
        rows_ref[0 : comps * KLO, ND * h : ND * (h + 1)] = came[:, h, :].T[0 : comps * KLO]


def second_kernel(
    came, diag, adjoint, rest,
    adjoint_out, pulled, index_out, place, starts_out,
    rows, total, ordered, turned, scattered,
    diag_here, adjoint_here, rest_here, load_sem, store_sem,
):
    loads = [
        pltpu.make_async_copy(a, b, load_sem.at[n])
        for n, (a, b) in enumerate(
            [(adjoint, adjoint_here), (diag, diag_here), (rest, rest_here)]
        )
    ]
    for load in loads:
        load.start()
    unpack(came, rows, 4)
    index = rows[0:KLO, :].astype(jnp.int32)
    starts = bucket_starts(index)
    place_slots(index, place, starts)
    to_places(rows, 4, lambda k: built_hots(place, k), total, ordered)
    loads[0].wait()
    turn_cells(
        lambda c, b: adjoint_here[c, 8 * b : 8 * b + 8].reshape(BROWS, CY),
        turned,
    )
    scattered[...] = jnp.zeros_like(scattered)
    pulled[...] = jnp.zeros_like(pulled)
    index_rows = ordered.at[pl.ds(0, CROWS)]

    def first(b, j):
        row, lane = chunk_hots(index_rows, j, b)
        gather_chunk(turned[b], row, lane, pulled, 0, j)
        scatter_chunk(ordered, CROWS, j, row, lane, scattered, b)

    each_chunk(starts, first)
    loads[1].wait()
    loads[2].wait()
    for b in range(BUCKETS):
        for c in range(3):
            at = slice(8 * b, 8 * b + 8)
            rest_here[c, at] = rest_here[c, at] - scattered_cells(scattered, b, c)

    def update(z, _):
        step = solve_rows(
            [[diag_here[i, j, z] for j in range(3)] for i in range(3)], cells_at(rest_here, z)
        )
        for c in range(3):
            adjoint_here[c, z] += step[c]
        return 0

    lax.fori_loop(0, NZ, update, 0, unroll=2)
    store = pltpu.make_async_copy(adjoint_here, adjoint_out, store_sem)
    store.start()
    turn_cells(
        lambda c, b: adjoint_here[c, 8 * b : 8 * b + 8].reshape(BROWS, CY),
        turned,
    )

    def second(b, j):
        row, lane = chunk_hots(index_rows, j, b)
        gather_chunk(turned[b], row, lane, pulled, 3 * CROWS, j)

    each_chunk(starts, second)
    index_out[...] = ordered[0:CROWS, :]
    for b in range(BUCKETS + 1):
        starts_out[b] = starts[b]
    store.wait()


def seg_image(adjoint, diag, chain, scattered):
    position = iota((1, SEGS), 1) % SEG_MAX
    own = transposed_rows(seg_matrix(diag), adjoint)
    lower, upper = [
        transposed_rows(
            [[chain[i, j, n : n + 1, :] for j in range(3)] for i in range(3)], adjoint
        )
        for n in range(2)
    ]
    out = []
    for c in range(3):
        total = own[c] + scattered[c]
        total += jnp.where(position == SEG_MAX - 1, 0.0, pltpu.roll(lower[c], SEGS - 1, 1))
        total += jnp.where(position == 0, 0.0, pltpu.roll(upper[c], 1, 1))
        out.append(total)
    return out


def third_kernel(
    pulled, place, grad_cells, adjoint, diag, off,
    grad_segs, adjoint_segs, seg_diag, seg_chain, seg_len, seg_slots, push_blocks, pull_blocks,
    ordered, rest_out, adjoint_segs_out, residual_segs_out,
    place_lane, place_chunk, total, message, pulls_in, late_message, late_in, push_message, came,
    pulls, terms, lane_hot, table, push, off_here, diag_here, grad_here, adjoint_here, image,
    x_out, x_in, y_out, y_in, column,
    load_sem, store_sem, send_sem, recv_sem, own_sem, halo_send, halo_recv,
):
    greet()
    loads = [
        pltpu.make_async_copy(a, b, load_sem.at[n])
        for n, (a, b) in enumerate(
            [
                (adjoint, adjoint_here), (diag, diag_here),
                (off, off_here), (grad_cells, grad_here),
            ]
        )
    ]
    for load in loads:
        load.start()
    pull_exchange = Exchange(message, pulls_in, send_sem.at[0], recv_sem.at[0], own_sem.at[0])
    push_exchange = Exchange(
        push_message, came, send_sem.at[1], recv_sem.at[1], own_sem.at[1]
    )
    late_exchange = Exchange(
        late_message, late_in, send_sem.at[2], recv_sem.at[2], own_sem.at[2]
    )
    halo = Halo(x_out, x_in, y_out, y_in, halo_send, halo_recv)
    pulls[...] = jnp.zeros_like(pulls)
    from_places(
        pulled.at[pl.ds(0, 3 * CROWS)], 3,
        lambda k: kept_hots(place, place_lane, place_chunk, k), pulls, [0, KLO, 2 * KLO],
    )

    def hots(k):
        return place_lane[:, four_lanes(k)], place_chunk[:, four_lanes(k)]

    for h in range(KHI):
        message[:, h, :] = pulls[0:ND, ND * h : ND * (h + 1)].T
    lane_hots(seg_slots, lane_hot)
    greeted()
    pull_exchange.start()
    from_places(
        pulled.at[pl.ds(3 * CROWS, 3 * CROWS)], 3, hots, pulls,
        [ND, ND + KLO, ND + 2 * KLO],
    )
    for h in range(KHI):
        late_message[:, h, :] = pulls[ND : 2 * ND, ND * h : ND * (h + 1)].T
    late_exchange.start()
    for load in loads[:3]:
        load.wait()
    stencil_sides(lambda z: cells_at(adjoint_here, z), off_here, image, halo, column)
    active = active_row(seg_len)
    grad = seg_rows(grad_segs)
    matrix = seg_matrix(seg_diag)
    before = seg_rows(adjoint_segs)
    pull_exchange.wait_recv()
    unpack(pulls_in, pulls, 3)
    for c, term in enumerate(slot_terms(pull_blocks, pulls, 0)):
        terms[c * KLO : (c + 1) * KLO, :] = term
    scattered = seg_scatter(terms, seg_slots, lane_hot, table)
    seen = seg_image(before, seg_diag, seg_chain, scattered)
    step = solve_rows(matrix, [grad[c] - seen[c] for c in range(3)])
    after = [before[c] + active * step[c] for c in range(3)]
    for c in range(3):
        adjoint_segs_out[c : c + 1, :] = after[c]
    seg_gather(after, seg_slots, lane_hot, table, push)
    packed = jnp.concatenate(
        slot_terms(push_blocks, push, 0) + [jnp.zeros((KLO, WIDE), F32)], axis=0
    )
    for h in range(KHI):
        push_message[:, h, :] = packed[:, ND * h : ND * (h + 1)].T
    push_exchange.start()
    stencil_layers(lambda z: cells_at(adjoint_here, z), diag_here, off_here, image)
    late_exchange.wait_recv()
    unpack(late_in, pulls, 3)
    for c, term in enumerate(slot_terms(pull_blocks, pulls, 0)):
        terms[c * KLO : (c + 1) * KLO, :] = term
    scattered = seg_scatter(terms, seg_slots, lane_hot, table)
    seen = seg_image(after, seg_diag, seg_chain, scattered)
    for c in range(3):
        residual_segs_out[c : c + 1, :] = active * (grad[c] - seen[c])
    halo.wait_recv()
    add_rims(image, halo, column)
    loads[3].wait()
    for c in range(3):
        grad_here[c] = grad_here[c] - image[c, 1 : NZ + 1]
    store = pltpu.make_async_copy(grad_here, rest_out, store_sem)
    store.start()
    push_exchange.wait_recv()
    unpack(came, pulls, 3)
    to_places(pulls, 3, hots, total, ordered)
    store.wait()
    late_exchange.wait_send()
    pull_exchange.wait_send()
    push_exchange.wait_send()
    halo.wait_send()


def fourth_kernel(
    starts, ordered, rest, index_rows, adjoint_segs, residual_segs,
    residual_out, adjoint_segs_out, residual_segs_out,
    scattered,
):
    adjoint_segs_out[...] = adjoint_segs[...]
    residual_segs_out[...] = residual_segs[...]
    scattered[...] = jnp.zeros_like(scattered)

    def act(b, j):
        row, lane = chunk_hots(index_rows, j, b)
        scatter_chunk(ordered, 0, j, row, lane, scattered, b)

    each_chunk([starts[b] for b in range(BUCKETS + 1)], act)
    for b in range(BUCKETS):
        for c in range(3):
            at = slice(8 * b, 8 * b + 8)
            residual_out[c, at] = rest[c, at] - scattered_cells(scattered, b, c)


def shape(*dims, kind=F32):
    return jax.ShapeDtypeStruct(dims, kind)


def vmem(*dims, kind=F32):
    return pltpu.VMEM(dims, kind)


def rim_scratch():
    return [
        vmem(2, 3, NZ, CY),
        vmem(2, 3, NZ, CY),
        vmem(2, 3, ROWS),
        vmem(2, 3, ROWS),
        vmem(3, ROWS, CY),
    ]


def call(kernel, outs, ins, scratch, number=None, in_specs=None, out_specs=None):
    params = dict(vmem_limit_bytes=58 << 20)
    if number is not None:
        params.update(collective_id=number, has_side_effects=True)
    return pl.pallas_call(
        kernel,
        out_shape=outs,
        in_specs=in_specs or [VMEM] * len(ins),
        out_specs=out_specs or [VMEM] * len(outs),
        scratch_shapes=scratch,
        compiler_params=pltpu.CompilerParams(**params),
        name=kernel.__name__,
    )(*ins)


def shards(
    grad_cells, grad_segs, cell_diag, cell_off, seg_diag, seg_chain, seg_len,
    perf_device, perf_local, perf_seg, perf_blocks,
):
    dma = pltpu.SemaphoreType.DMA
    smem = pl.BlockSpec(memory_space=pltpu.SMEM)
    lens = seg_len.reshape(1, 32)
    chain = seg_chain.transpose(1, 2, 0, 3)
    cells = shape(3, NZ, CX, CY)
    segs = shape(3, SEGS)
    tile = vmem(3, NZ, CX, CY)
    diag_tile = vmem(3, 3, NZ, CX, CY)
    off_tile = vmem(6, 3, 3, NZ, CX, CY)
    image = vmem(3, NZ + 2, CX, CY)
    came, seg_slots, push_blocks, pull_blocks, adjoint, rest, adjoint_segs = call(
        first_kernel,
        [
            shape(ND, KHI, ND), shape(KLO, WIDE), shape(9 * KLO, WIDE), shape(9 * KLO, WIDE),
            cells, cells, segs,
        ],
        [
            grad_cells, grad_segs, cell_diag, cell_off, seg_diag, lens,
            perf_device.reshape(1, PERFS), perf_local.reshape(1, PERFS),
            perf_seg.reshape(1, PERFS), perf_blocks.transpose(1, 2, 0, 3),
        ],
        [
            vmem(WIDE, PERFS, kind=BF16),
            vmem(KLO, PERFS),
            vmem(22 * KLO, 512, kind=BF16),
            vmem(22 * KLO, WIDE),
            vmem(11 * KLO, WIDE),
            vmem(9 * KLO, WIDE),
            vmem(128, SLOTS, kind=BF16),
            vmem(48, 128),
            vmem(3 * KLO, WIDE),
            vmem(ND, KHI, ND),
            off_tile,
            diag_tile,
            tile,
            tile,
            image,
        ]
        + rim_scratch()
        + [dma((3,)), dma((5,)), dma, dma, dma, dma((4,)), dma((4,))],
        0,
        [ANY, VMEM, ANY, ANY] + [VMEM] * 6,
        [VMEM] + [ANY] * 5 + [VMEM],
    )
    adjoint, pulled, index_rows, place, starts = call(
        second_kernel,
        [
            cells, shape(6 * CROWS, LANES), shape(CROWS, LANES),
            shape(KLO, WIDE, kind=jnp.int32), shape(8, kind=jnp.int32),
        ],
        [came, cell_diag, adjoint, rest],
        [
            vmem(4 * KLO, WIDE),
            vmem(8 * CROWS, LANES),
            vmem(4 * CROWS, LANES),
            vmem(BUCKETS, 6 * HALF, 2 * BROWS, kind=BF16),
            vmem(BUCKETS, 3 * HALF, 2 * BROWS),
            diag_tile,
            tile,
            tile,
            dma((3,)),
            dma,
        ],
        None,
        [VMEM] + [ANY] * 3,
        [ANY] + [VMEM] * 3 + [smem],
    )
    ordered, rest, adjoint_segs, residual_segs = call(
        third_kernel,
        [shape(3 * CROWS, LANES), cells, segs, segs],
        [
            pulled, place, grad_cells, adjoint, cell_diag, cell_off,
            grad_segs, adjoint_segs, seg_diag, chain, lens, seg_slots, push_blocks, pull_blocks,
        ],
        [
            vmem(LANES, SLOTS, kind=BF16),
            vmem(CROWS, SLOTS),
            vmem(6 * CROWS, LANES),
            vmem(ND, KHI, ND),
            vmem(ND, KHI, ND),
            vmem(ND, KHI, ND),
            vmem(ND, KHI, ND),
            vmem(ND, KHI, ND),
            vmem(ND, KHI, ND),
            vmem(8 * KLO, WIDE),
            vmem(3 * KLO, WIDE),
            vmem(128, SLOTS, kind=BF16),
            vmem(48, 128),
            vmem(3 * KLO, WIDE),
            off_tile,
            diag_tile,
            tile,
            tile,
            image,
        ]
        + rim_scratch()
        + [dma((4,)), dma, dma((3,)), dma((3,)), dma((3,)), dma((4,)), dma((4,))],
        1,
        [VMEM] * 2 + [ANY] * 4 + [VMEM] * 8,
        [VMEM, ANY, VMEM, VMEM],
    )
    residual, adjoint_segs, residual_segs = call(
        fourth_kernel,
        [cells, segs, segs],
        [starts, ordered, rest, index_rows, adjoint_segs, residual_segs],
        [vmem(BUCKETS, 3 * HALF, 2 * BROWS)],
        None,
        [smem] + [VMEM] * 5,
    )
    return adjoint, adjoint_segs, residual, residual_segs


def solution(mesh):
    in_specs = (
        P(None, None, "gx", "gy"),
        P(None, ("gx", "gy")),
        P(None, None, None, "gx", "gy"),
        P(None, None, None, None, "gx", "gy"),
        P(None, None, ("gx", "gy")),
        P(None, None, None, ("gx", "gy")),
        P(("gx", "gy")),
        P(("gx", "gy"), None),
        P(("gx", "gy")),
        P(("gx", "gy")),
        P(None, None, None, ("gx", "gy")),
    )
    out_specs = (
        P(None, None, "gx", "gy"),
        P(None, ("gx", "gy")),
        P(None, None, "gx", "gy"),
        P(None, ("gx", "gy")),
    )
    return jax.shard_map(shards, mesh=mesh, in_specs=in_specs, out_specs=out_specs, check_vma=False)
```

```python
import jax
import jax.numpy as jnp
from jax import lax
from jax.experimental import pallas as pl
from jax.experimental.pallas import tpu as pltpu
from jax.sharding import PartitionSpec as P

MESH = pl.DeviceIdType.MESH
F32 = jnp.float32
BF16 = jnp.bfloat16
NT = (((1,), (1,)), ((), ()))
GX = 8
GY = 16
ND = GX * GY
NZ = 32
CX = 16
CY = 128
ROWS = NZ * CX
SEGS = 1024
SEG_MAX = 32
PERFS = 4096
KLO = 32
KHI = 2
WIDE = KHI * ND
SLOTS = KLO * WIDE
BUCKETS = 4
BROWS = ROWS // BUCKETS
HALF = CY // 2
CHUNK = 512
LANES = 256
CROWS = 40
SPARE = CROWS * LANES // CHUNK - 1
VMEM = pl.BlockSpec(memory_space=pltpu.VMEM)
ANY = pl.BlockSpec(memory_space=pl.ANY)


def rounded(x):
    return x.astype(BF16).astype(F32)


def halves(x):
    high = rounded(x)
    return high, x - high


def iota(shape, dim):
    return lax.broadcasted_iota(jnp.int32, shape, dim)


def one_hot(count, row, kind):
    hit = iota((count, row.shape[1]), 0) == row
    return hit.astype(F32).astype(kind)


def inverse_rows(matrix):
    cofactor = [
        [
            matrix[(i + 1) % 3][(j + 1) % 3] * matrix[(i + 2) % 3][(j + 2) % 3]
            - matrix[(i + 1) % 3][(j + 2) % 3] * matrix[(i + 2) % 3][(j + 1) % 3]
            for j in range(3)
        ]
        for i in range(3)
    ]
    determinant = (
        matrix[0][0] * cofactor[0][0]
        + matrix[0][1] * cofactor[0][1]
        + matrix[0][2] * cofactor[0][2]
    )
    return cofactor, 1.0 / determinant


def solve_rows(matrix, vector):
    cofactor, scale = inverse_rows(matrix)
    return [
        (cofactor[i][0] * vector[0] + cofactor[i][1] * vector[1] + cofactor[i][2] * vector[2])
        * scale
        for i in range(3)
    ]


def transposed_rows(matrix, vector):
    return [
        matrix[0][i] * vector[0] + matrix[1][i] * vector[1] + matrix[2][i] * vector[2]
        for i in range(3)
    ]


def seg_rows(ref):
    return [ref[j : j + 1, :] for j in range(3)]


def seg_matrix(ref):
    return [[ref[i, j : j + 1, :] for j in range(3)] for i in range(3)]


def active_row(seg_len_ref):
    square = iota((32, 32), 0) == iota((32, 32), 1)
    lens = jnp.sum(jnp.where(square, seg_len_ref[...].astype(F32), 0.0), axis=1, keepdims=True)
    lanes = iota((32, SEGS), 1)
    mine = (lanes // SEG_MAX) == iota((32, SEGS), 0)
    below = (lanes % SEG_MAX).astype(F32) < lens
    return jnp.sum(jnp.where(mine & below, 1.0, 0.0), axis=0, keepdims=True)


def four_rows(ref, start, k):
    return jnp.concatenate([ref[pl.ds(start + 4 * k + n, 1), :] for n in range(4)], axis=1)


def put_four_rows(ref, start, k, value):
    for n in range(4):
        ref[pl.ds(start + 4 * k + n, 1), :] = value[:, WIDE * n : WIDE * (n + 1)]


def four_lanes(k):
    return pl.ds(pl.multiple_of(k * 4 * WIDE, 4 * WIDE), 4 * WIDE)


def seg_gather(values, seg_slots, lane_hot_ref, table_ref, out_ref):
    for c in range(3):
        for p, part in enumerate(halves(values[c])):
            for h in range(8):
                at = p * 24 + c * 8 + h
                table_ref[at : at + 1, :] = part[:, 128 * h : 128 * (h + 1)]
    table = table_ref[...].astype(BF16)

    def body(k, _):
        found = jnp.dot(table, lane_hot_ref[:, four_lanes(k)], preferred_element_type=F32)
        found = found[:24] + found[24:]
        high = four_rows(seg_slots, 0, k).astype(jnp.int32) >> 7
        pick = (iota((8, 4 * WIDE), 0) == high).astype(F32)
        for c in range(3):
            value = jnp.sum(found[8 * c : 8 * c + 8] * pick, axis=0, keepdims=True)
            put_four_rows(out_ref, c * KLO, k, value)
        return 0

    lax.fori_loop(0, KLO // 4, body, 0, unroll=2)


def seg_scatter(values_ref, seg_slots, lane_hot_ref, table_ref):
    def body(k, total):
        high = four_rows(seg_slots, 0, k).astype(jnp.int32) >> 7
        pick = (iota((8, 4 * WIDE), 0) == high).astype(F32)
        right = []
        for c in range(3):
            right += [pick * part for part in halves(four_rows(values_ref, c * KLO, k))]
        return total + lax.dot_general(
            lane_hot_ref[:, four_lanes(k)],
            jnp.concatenate(right, axis=0).astype(BF16),
            NT,
            preferred_element_type=F32,
        )

    total = lax.fori_loop(0, KLO // 4, body, jnp.zeros((128, 48), F32), unroll=2)
    turned = jnp.concatenate([total, jnp.zeros((128, 80), F32)], axis=1).T
    rows = []
    for c in range(3):
        table_ref[0:8, :] = turned[16 * c : 16 * c + 8] + turned[16 * c + 8 : 16 * c + 16]
        rows.append(jnp.concatenate([table_ref[h : h + 1, :] for h in range(8)], axis=1))
    return rows


def lane_hots(seg_slots, lane_hot_ref):
    def body(k, _):
        low = four_rows(seg_slots, 0, k).astype(jnp.int32) & 127
        lane_hot_ref[:, four_lanes(k)] = one_hot(128, low, BF16)
        return 0

    lax.fori_loop(0, KLO // 4, body, 0)


def slot_terms(blocks, rows_ref, start):
    vector = [rows_ref[start + c * KLO : start + (c + 1) * KLO, :] for c in range(3)]
    out = []
    for i in range(3):
        total = None
        for j in range(3):
            at = (j * 3 + i) * KLO
            term = blocks[at : at + KLO, :] * vector[j]
            total = term if total is None else total + term
        out.append(total)
    return out


def everyone(act):
    gx = lax.axis_index("gx")
    gy = lax.axis_index("gy")
    columns = [lax.rem(gy + j, GY) for j in range(GY)]

    def visit(row, distances):
        for j in distances:
            act(row * GY + columns[j], (row, columns[j]))

    visit(gx, range(1, GY))

    def body(i, _):
        visit(lax.rem(gx + i, GX), range(GY))
        return 0

    lax.fori_loop(1, GX, body, 0)


def greet():
    barrier = pltpu.get_barrier_semaphore()
    everyone(
        lambda other, place: pl.semaphore_signal(
            barrier, inc=1, device_id=place, device_id_type=MESH
        )
    )


def greeted():
    pl.semaphore_wait(pltpu.get_barrier_semaphore(), ND - 1)


class Exchange:
    def __init__(self, source, target, send_sem, recv_sem, own_sem):
        self.source, self.target = source, target
        self.send_sem, self.recv_sem, self.own_sem = send_sem, recv_sem, own_sem
        self.me = lax.axis_index("gx") * GY + lax.axis_index("gy")

    def own(self):
        return pltpu.make_async_copy(
            self.source.at[self.me], self.target.at[self.me], self.own_sem
        )

    def whole(self):
        return pltpu.make_async_remote_copy(
            src_ref=self.source.at[pl.ds(0, ND - 1)],
            dst_ref=self.target.at[pl.ds(0, ND - 1)],
            send_sem=self.send_sem,
            recv_sem=self.recv_sem,
            device_id=(lax.axis_index("gx"), lax.axis_index("gy")),
            device_id_type=MESH,
        )

    def start(self):
        self.own().start()
        everyone(
            lambda other, place: pltpu.make_async_remote_copy(
                src_ref=self.source.at[other],
                dst_ref=self.target.at[self.me],
                send_sem=self.send_sem,
                recv_sem=self.recv_sem,
                device_id=place,
                device_id_type=MESH,
            ).start()
        )

    def wait_recv(self):
        self.own().wait()
        self.whole().wait_recv()

    def wait_send(self):
        self.whole().wait_send()


class Halo:
    def __init__(self, x_out, x_in, y_out, y_in, send_sem, recv_sem):
        gx = lax.axis_index("gx")
        gy = lax.axis_index("gy")
        places = [
            (lax.rem(gx + 1, GX), gy),
            (lax.rem(gx + GX - 1, GX), gy),
            (gx, lax.rem(gy + 1, GY)),
            (gx, lax.rem(gy + GY - 1, GY)),
        ]
        pairs = [(x_out, x_in, 0), (x_out, x_in, 1), (y_out, y_in, 0), (y_out, y_in, 1)]
        self.copies = [
            pltpu.make_async_remote_copy(
                src_ref=a.at[n],
                dst_ref=b.at[n],
                send_sem=send_sem.at[at],
                recv_sem=recv_sem.at[at],
                device_id=place,
                device_id_type=MESH,
            )
            for at, ((a, b, n), place) in enumerate(zip(pairs, places))
        ]
        self.x_out, self.x_in, self.y_out, self.y_in = x_out, x_in, y_out, y_in

    def start(self):
        for copy in self.copies:
            copy.start()

    def wait_recv(self):
        for copy in self.copies:
            copy.wait_recv()

    def wait_send(self):
        for copy in self.copies:
            copy.wait_send()


def stencil_sides(adjoint, off_ref, image_ref, halo, column_ref):
    rows = iota((CX, CY), 0)
    lanes = iota((CX, CY), 1)

    def body(z, _):
        a = adjoint(z)
        moved = [
            transposed_rows([[off_ref[e, j, i, z] for i in range(3)] for j in range(3)], a)
            for e in range(4)
        ]
        at = pl.ds(pl.multiple_of(z * CX, CX), CX)
        for c in range(3):
            halo.x_out[0, c, pl.ds(z, 1), :] = moved[0][c][CX - 1 : CX]
            halo.x_out[1, c, pl.ds(z, 1), :] = moved[1][c][0:1]
            right = pltpu.roll(moved[2][c], 1, 1)
            left = pltpu.roll(moved[3][c], CY - 1, 1)
            column_ref[c, at, :] = jnp.where(lanes < HALF, right, left)
            total = jnp.where(rows == 0, 0.0, pltpu.roll(moved[0][c], 1, 0))
            total += jnp.where(rows == CX - 1, 0.0, pltpu.roll(moved[1][c], CX - 1, 0))
            total += jnp.where(lanes == 0, 0.0, right)
            total += jnp.where(lanes == CY - 1, 0.0, left)
            image_ref[c, z + 1] = total
        return 0

    lax.fori_loop(0, NZ, body, 0, unroll=2)
    for c in range(3):
        turned = column_ref[c].T
        halo.y_out[0, c : c + 1, :] = turned[0:1]
        halo.y_out[1, c : c + 1, :] = turned[CY - 1 : CY]
    halo.start()


def stencil_layers(adjoint, diag_ref, off_ref, image_ref):
    for c in range(3):
        image_ref[c, 0] = jnp.zeros((CX, CY), F32)
        image_ref[c, NZ + 1] = jnp.zeros((CX, CY), F32)

    def body(z, _):
        a = adjoint(z)
        own = transposed_rows([[diag_ref[j, i, z] for i in range(3)] for j in range(3)], a)
        rising, falling = [
            transposed_rows([[off_ref[e, j, i, z] for i in range(3)] for j in range(3)], a)
            for e in (4, 5)
        ]
        for c in range(3):
            image_ref[c, z + 1] += own[c]
            image_ref[c, z + 2] += rising[c]
            image_ref[c, z] += falling[c]
        return 0

    lax.fori_loop(0, NZ, body, 0, unroll=2)


def add_rims(image_ref, halo, column_ref):
    gx = lax.axis_index("gx")
    gy = lax.axis_index("gy")
    first_x = jnp.where(gx > 0, 1.0, 0.0)
    last_x = jnp.where(gx < GX - 1, 1.0, 0.0)
    first_y = jnp.where(gy > 0, 1.0, 0.0)
    last_y = jnp.where(gy < GY - 1, 1.0, 0.0)
    eight = iota((8, ROWS), 0)
    for c in range(3):
        top = jnp.where(eight == 0, halo.y_in[0, c : c + 1, :] * first_y, 0.0)
        bottom = jnp.where(eight == 7, halo.y_in[1, c : c + 1, :] * last_y, 0.0)
        column_ref[c] = jnp.concatenate([top, jnp.zeros((CY - 16, ROWS), F32), bottom], axis=0).T
    rows = iota((CX, CY), 0)

    def body(z, _):
        at = pl.ds(pl.multiple_of(z * CX, CX), CX)
        for c in range(3):
            low = halo.x_in[0, c, pl.ds(z, 1), :] * first_x
            high = halo.x_in[1, c, pl.ds(z, 1), :] * last_x
            total = jnp.where(rows == 0, low, 0.0) + jnp.where(rows == CX - 1, high, 0.0)
            image_ref[c, z + 1] += total + column_ref[c, at, :]
        return 0

    lax.fori_loop(0, NZ, body, 0, unroll=2)


def rank_rows(device_ref, column_ref, row_ref):
    above = (iota((256, 256), 0) < iota((256, 256), 1)).astype(F32).astype(BF16)
    ones = jnp.ones((256, 256), BF16)
    carry = jnp.zeros((ND, 256), F32)
    for j in range(PERFS // 256):
        at = slice(256 * j, 256 * (j + 1))
        target = device_ref[:, at]
        hit = one_hot(ND, target, F32)
        hit16 = hit.astype(BF16)
        before = jnp.dot(hit16, above, preferred_element_type=F32) + carry
        carry = carry + jnp.dot(hit16, ones, preferred_element_type=F32)
        rank = jnp.sum(before * hit, axis=0, keepdims=True).astype(jnp.int32)
        column_ref[:, at] = one_hot(WIDE, target + ND * (rank >> 5), BF16)
        row_ref[:, at] = one_hot(KLO, rank & (KLO - 1), F32)


def place_rows(row, count, column_ref, row_ref, work_ref, total_ref, out_ref):
    size = count * KLO
    for j in range(PERFS // 512):
        at = slice(512 * j, 512 * (j + 1))
        row_hot = row_ref[:, at]
        for q in range(count):
            for p, part in enumerate(halves(row(q, at))):
                put = p * size + q * KLO
                work_ref[put : put + KLO, :] = (row_hot * part).astype(BF16)
        part = lax.dot_general(
            work_ref[0 : 2 * size, :], column_ref[:, at], NT, preferred_element_type=F32
        )
        if j == 0:
            total_ref[0 : 2 * size, :] = part
        else:
            total_ref[0 : 2 * size, :] += part
    out_ref[...] = total_ref[0:size, :] + total_ref[size : 2 * size, :]


def cells_at(ref, z):
    return [ref[c, z] for c in range(3)]


def first_kernel(
    grad_cells, grad_segs, diag, off, seg_diag, seg_len, device, local, seg, blocks,
    came, seg_slots_out, push_out, pull_out, adjoint_out, rest_out, adjoint_segs_out,
    column_hot, row_hot, work, total, slots, pull_blocks, lane_hot, table, push, message,
    off_here, diag_here, grad_here, adjoint, image,
    x_out, x_in, y_out, y_in, column,
    load_sem, store_sem, send_sem, recv_sem, own_sem, halo_send, halo_recv,
):
    loads = [
        pltpu.make_async_copy(a, b, load_sem.at[n])
        for n, (a, b) in enumerate(
            [(diag, diag_here), (grad_cells, grad_here), (off, off_here)]
        )
    ]
    for load in loads:
        load.start()
    greet()
    exchange = Exchange(message, came, send_sem, recv_sem, own_sem)
    halo = Halo(x_out, x_in, y_out, y_in, halo_send, halo_recv)
    rank_rows(device, column_hot, row_hot)

    def first_rows(q, at):
        if q == 0:
            return (local[:, at] + 1).astype(F32)
        if q == 1:
            return seg[:, at].astype(F32)
        return blocks[(q - 2) // 3, (q - 2) % 3, 0:1, at]

    place_rows(first_rows, 11, column_hot, row_hot, work, total, slots)
    active = active_row(seg_len)
    adjoint_segs = [
        active * row for row in solve_rows(seg_matrix(seg_diag), seg_rows(grad_segs))
    ]
    for c in range(3):
        adjoint_segs_out[c : c + 1, :] = adjoint_segs[c]
    seg_slots = slots.at[pl.ds(KLO, KLO)]
    push_blocks = slots.at[pl.ds(2 * KLO, 9 * KLO)]
    stores = [
        pltpu.make_async_copy(a, b, store_sem.at[n])
        for n, (a, b) in enumerate(
            [
                (seg_slots, seg_slots_out), (push_blocks, push_out),
                (adjoint, adjoint_out), (pull_blocks, pull_out), (grad_here, rest_out),
            ]
        )
    ]
    stores[0].start()
    stores[1].start()
    lane_hots(seg_slots, lane_hot)
    seg_gather(adjoint_segs, seg_slots, lane_hot, table, push)
    terms = slot_terms(push_blocks, push, 0)
    packed = jnp.concatenate([slots[0:KLO, :]] + terms, axis=0)
    for h in range(KHI):
        message[:, h, :] = packed[:, ND * h : ND * (h + 1)].T
    loads[0].wait()
    loads[1].wait()

    def begin(z, _):
        a = solve_rows(
            [[diag_here[i, j, z] for j in range(3)] for i in range(3)], cells_at(grad_here, z)
        )
        for c in range(3):
            adjoint[c, z] = a[c]
        return 0

    lax.fori_loop(0, NZ, begin, 0, unroll=2)
    stores[2].start()
    loads[2].wait()
    greeted()
    stencil_sides(lambda z: cells_at(adjoint, z), off_here, image, halo, column)
    exchange.start()
    stencil_layers(lambda z: cells_at(adjoint, z), diag_here, off_here, image)
    place_rows(
        lambda q, at: blocks[q // 3, q % 3, 1:2, at],
        9, column_hot, row_hot, work, total, pull_blocks,
    )
    stores[3].start()
    halo.wait_recv()
    add_rims(image, halo, column)
    for c in range(3):
        grad_here[c] = grad_here[c] - image[c, 1 : NZ + 1]
    stores[4].start()
    exchange.wait_recv()
    for store in stores:
        store.wait()
    exchange.wait_send()
    halo.wait_send()


def place_slots(index, place_ref, starts):
    row = (index - 1) >> 7
    parts = []
    for b in range(BUCKETS):
        parts.append(((index > 0) & ((row // BROWS) == b)).astype(F32))
    hit = jnp.concatenate(parts, axis=0)
    hit16 = hit.astype(BF16)
    above = (iota((WIDE, WIDE), 0) < iota((WIDE, WIDE), 1)).astype(F32).astype(BF16)
    within = jnp.dot(hit16, above, preferred_element_type=F32)
    totals = jnp.dot(hit16, jnp.ones((WIDE, WIDE), BF16), preferred_element_type=F32)
    r0 = iota((BUCKETS * KLO, BUCKETS * KLO), 0)
    r1 = iota((BUCKETS * KLO, BUCKETS * KLO), 1)
    lower = ((r1 < r0) & ((r1 // KLO) == (r0 // KLO))).astype(F32).astype(BF16)
    earlier = jnp.dot(lower, totals.astype(BF16), preferred_element_type=F32)
    before = within + earlier
    place = jnp.full((KLO, WIDE), -1.0, F32)
    for b in range(BUCKETS):
        at = slice(b * KLO, (b + 1) * KLO)
        base = (starts[b] * CHUNK).astype(F32)
        place = jnp.where(hit[at] > 0, before[at] + base, place)
    place_ref[...] = place.astype(jnp.int32)


def bucket_starts(index):
    row = (index - 1) >> 7
    starts = [jnp.int32(0)]
    most = jnp.int32(0)
    for b in range(BUCKETS):
        held = ((index > 0) & ((row // BROWS) == b)).astype(jnp.int32)
        count = jnp.sum(held)
        starts.append(starts[-1] + (count + CHUNK - 1) // CHUNK)
        most = jnp.maximum(most, (count + LANES - 1) // LANES)
    return starts + [most]


def built_hots(place_ref, k):
    place = four_rows(place_ref, 0, k)
    return one_hot(LANES, place & (LANES - 1), BF16), one_hot(CROWS, place >> 8, F32)


def kept_hots(place_ref, lane_ref, chunk_ref, k):
    lane, chunk = built_hots(place_ref, k)
    lane_ref[:, four_lanes(k)] = lane
    chunk_ref[:, four_lanes(k)] = chunk
    return lane, chunk


def to_places(rows_ref, count, hots, total_ref, out_ref):
    size = count * CROWS

    def body(k, _):
        lane, chunk = hots(k)
        left = [[], []]
        for q in range(count):
            for p, part in enumerate(halves(four_rows(rows_ref, q * KLO, k))):
                left[p].append(chunk * part)
        total_ref[0 : 2 * size, :] += lax.dot_general(
            jnp.concatenate(left[0] + left[1], axis=0).astype(BF16),
            lane,
            NT,
            preferred_element_type=F32,
        )
        return 0

    total_ref[...] = jnp.zeros_like(total_ref)
    lax.fori_loop(0, KLO // 4, body, 0, unroll=2)
    out_ref[...] = total_ref[0:size, :] + total_ref[size : 2 * size, :]


def from_places(rows_ref, count, hots, out_ref, starts):
    size = count * CROWS
    both = jnp.concatenate(halves(rows_ref[...]), axis=0).astype(BF16)

    def body(k, _):
        lane, chunk = hots(k)
        found = jnp.dot(both, lane, preferred_element_type=F32)
        for q in range(count):
            at = q * CROWS
            value = found[at : at + CROWS] + found[size + at : size + at + CROWS]
            put_four_rows(
                out_ref, starts[q], k, jnp.sum(value * chunk, axis=0, keepdims=True)
            )
        return 0

    lax.fori_loop(0, KLO // 4, body, 0, unroll=2)


def turn_cells(cells, turned_ref):
    for c in range(3):
        for b in range(BUCKETS):
            for p, part in enumerate(halves(cells(c, b).T)):
                at = (3 * p + c) * HALF
                turned_ref[b, at : at + HALF, 0:BROWS] = part[:HALF].astype(BF16)
                turned_ref[b, at : at + HALF, BROWS : 2 * BROWS] = part[HALF:].astype(BF16)


def chunk_row(ref, row, rows):
    return jnp.concatenate([ref[pl.ds(row + n, 1), :] for n in range(rows)], axis=1)


def chunk_hots(index_ref, j, rows, b):
    index = chunk_row(index_ref, j, rows).astype(jnp.int32) - 1
    row = (index >> 7) - BROWS * b + ((index >> 6) & 1) * BROWS
    row = one_hot(2 * BROWS, jnp.where(index >= 0, row, -1), BF16)
    lane = one_hot(HALF, index & (HALF - 1), F32)
    return row, lane


def gather_chunk(turned, row, lane, out_ref, start, j, rows):
    found = jnp.dot(turned, row, preferred_element_type=F32)
    found = found[: 3 * HALF] + found[3 * HALF :]
    for c in range(3):
        value = jnp.sum(found[c * HALF : (c + 1) * HALF] * lane, axis=0, keepdims=True)
        for n in range(rows):
            out_ref[pl.ds(start + c * CROWS + j + n, 1), :] = value[
                :, LANES * n : LANES * (n + 1)
            ]


def scatter_chunk(values_ref, start, j, rows, row, lane, total_ref, b):
    high, low = [], []
    for c in range(3):
        one, two = halves(chunk_row(values_ref, start + c * CROWS + j, rows))
        high.append(lane * one)
        low.append(lane * two)
    part = lax.dot_general(
        jnp.concatenate(high + low, axis=0).astype(BF16), row, NT, preferred_element_type=F32
    )
    total_ref[b] += part[: 3 * HALF] + part[3 * HALF :]


def each_chunk(starts, act):
    counts = [starts[b + 1] - starts[b] for b in range(BUCKETS)]
    steps = starts[BUCKETS + 1] // 2

    def step(rows):
        def body(t, _):
            for b in range(BUCKETS):
                act(b, 2 * jnp.where(t < counts[b], starts[b] + t, SPARE), rows)
            return 0

        return body

    lax.fori_loop(0, steps, step(2), 0)
    lax.fori_loop(steps, starts[BUCKETS + 1] - steps, step(1), 0)


def scattered_cells(total_ref, b, c):
    part = total_ref[b, c * HALF : (c + 1) * HALF, :]
    whole = jnp.concatenate([part[:, :BROWS], part[:, BROWS:]], axis=0)
    return whole.T.reshape(NZ // BUCKETS, CX, CY)


def unpack(came, rows_ref, comps):
    for h in range(KHI):
        rows_ref[0 : comps * KLO, ND * h : ND * (h + 1)] = came[:, h, :].T[0 : comps * KLO]


def second_kernel(
    came, diag, adjoint, rest,
    adjoint_out, pulled, index_out, place, starts_out,
    rows, total, ordered, turned, scattered,
    diag_here, adjoint_here, rest_here, load_sem, store_sem,
):
    loads = [
        pltpu.make_async_copy(a, b, load_sem.at[n])
        for n, (a, b) in enumerate(
            [(adjoint, adjoint_here), (diag, diag_here), (rest, rest_here)]
        )
    ]
    for load in loads:
        load.start()
    unpack(came, rows, 4)
    index = rows[0:KLO, :].astype(jnp.int32)
    starts = bucket_starts(index)
    place_slots(index, place, starts)
    to_places(rows, 4, lambda k: built_hots(place, k), total, ordered)
    loads[0].wait()
    turn_cells(
        lambda c, b: adjoint_here[c, 8 * b : 8 * b + 8].reshape(BROWS, CY),
        turned,
    )
    scattered[...] = jnp.zeros_like(scattered)
    pulled[...] = jnp.zeros_like(pulled)
    index_rows = ordered.at[pl.ds(0, CROWS)]

    def first(b, j, n):
        row, lane = chunk_hots(index_rows, j, n, b)
        gather_chunk(turned[b], row, lane, pulled, 0, j, n)
        scatter_chunk(ordered, CROWS, j, n, row, lane, scattered, b)

    each_chunk(starts, first)
    loads[1].wait()
    loads[2].wait()
    for b in range(BUCKETS):
        for c in range(3):
            at = slice(8 * b, 8 * b + 8)
            rest_here[c, at] = rest_here[c, at] - scattered_cells(scattered, b, c)

    def update(z, _):
        step = solve_rows(
            [[diag_here[i, j, z] for j in range(3)] for i in range(3)], cells_at(rest_here, z)
        )
        for c in range(3):
            adjoint_here[c, z] += step[c]
        return 0

    lax.fori_loop(0, NZ, update, 0, unroll=2)
    store = pltpu.make_async_copy(adjoint_here, adjoint_out, store_sem)
    store.start()
    turn_cells(
        lambda c, b: adjoint_here[c, 8 * b : 8 * b + 8].reshape(BROWS, CY),
        turned,
    )

    def second(b, j, n):
        row, lane = chunk_hots(index_rows, j, n, b)
        gather_chunk(turned[b], row, lane, pulled, 3 * CROWS, j, n)

    each_chunk(starts, second)
    index_out[...] = ordered[0:CROWS, :]
    for b in range(BUCKETS + 2):
        starts_out[b] = starts[b]
    store.wait()


def seg_image(adjoint, diag, chain, scattered):
    position = iota((1, SEGS), 1) % SEG_MAX
    own = transposed_rows(seg_matrix(diag), adjoint)
    lower, upper = [
        transposed_rows(
            [[chain[i, j, n : n + 1, :] for j in range(3)] for i in range(3)], adjoint
        )
        for n in range(2)
    ]
    out = []
    for c in range(3):
        total = own[c] + scattered[c]
        total += jnp.where(position == SEG_MAX - 1, 0.0, pltpu.roll(lower[c], SEGS - 1, 1))
        total += jnp.where(position == 0, 0.0, pltpu.roll(upper[c], 1, 1))
        out.append(total)
    return out


def third_kernel(
    pulled, place, grad_cells, adjoint, diag, off,
    grad_segs, adjoint_segs, seg_diag, seg_chain, seg_len, seg_slots, push_blocks, pull_blocks,
    ordered, rest_out, adjoint_segs_out, residual_segs_out,
    place_lane, place_chunk, total, message, pulls_in, late_message, late_in, push_message, came,
    pulls, terms, lane_hot, table, push, off_here, diag_here, grad_here, adjoint_here, image,
    x_out, x_in, y_out, y_in, column,
    load_sem, store_sem, send_sem, recv_sem, own_sem, halo_send, halo_recv,
):
    greet()
    loads = [
        pltpu.make_async_copy(a, b, load_sem.at[n])
        for n, (a, b) in enumerate(
            [
                (adjoint, adjoint_here), (diag, diag_here),
                (off, off_here), (grad_cells, grad_here),
            ]
        )
    ]
    for load in loads:
        load.start()
    pull_exchange = Exchange(message, pulls_in, send_sem.at[0], recv_sem.at[0], own_sem.at[0])
    push_exchange = Exchange(
        push_message, came, send_sem.at[1], recv_sem.at[1], own_sem.at[1]
    )
    late_exchange = Exchange(
        late_message, late_in, send_sem.at[2], recv_sem.at[2], own_sem.at[2]
    )
    halo = Halo(x_out, x_in, y_out, y_in, halo_send, halo_recv)
    pulls[...] = jnp.zeros_like(pulls)
    from_places(
        pulled.at[pl.ds(0, 3 * CROWS)], 3,
        lambda k: kept_hots(place, place_lane, place_chunk, k), pulls, [0, KLO, 2 * KLO],
    )

    def hots(k):
        return place_lane[:, four_lanes(k)], place_chunk[:, four_lanes(k)]

    for h in range(KHI):
        message[:, h, :] = pulls[0:ND, ND * h : ND * (h + 1)].T
    lane_hots(seg_slots, lane_hot)
    greeted()
    pull_exchange.start()
    from_places(
        pulled.at[pl.ds(3 * CROWS, 3 * CROWS)], 3, hots, pulls,
        [ND, ND + KLO, ND + 2 * KLO],
    )
    for h in range(KHI):
        late_message[:, h, :] = pulls[ND : 2 * ND, ND * h : ND * (h + 1)].T
    late_exchange.start()
    for load in loads[:3]:
        load.wait()
    stencil_sides(lambda z: cells_at(adjoint_here, z), off_here, image, halo, column)
    active = active_row(seg_len)
    grad = seg_rows(grad_segs)
    matrix = seg_matrix(seg_diag)
    before = seg_rows(adjoint_segs)
    pull_exchange.wait_recv()
    unpack(pulls_in, pulls, 3)
    for c, term in enumerate(slot_terms(pull_blocks, pulls, 0)):
        terms[c * KLO : (c + 1) * KLO, :] = term
    scattered = seg_scatter(terms, seg_slots, lane_hot, table)
    seen = seg_image(before, seg_diag, seg_chain, scattered)
    step = solve_rows(matrix, [grad[c] - seen[c] for c in range(3)])
    after = [before[c] + active * step[c] for c in range(3)]
    for c in range(3):
        adjoint_segs_out[c : c + 1, :] = after[c]
    seg_gather(after, seg_slots, lane_hot, table, push)
    packed = jnp.concatenate(
        slot_terms(push_blocks, push, 0) + [jnp.zeros((KLO, WIDE), F32)], axis=0
    )
    for h in range(KHI):
        push_message[:, h, :] = packed[:, ND * h : ND * (h + 1)].T
    push_exchange.start()
    stencil_layers(lambda z: cells_at(adjoint_here, z), diag_here, off_here, image)
    late_exchange.wait_recv()
    unpack(late_in, pulls, 3)
    for c, term in enumerate(slot_terms(pull_blocks, pulls, 0)):
        terms[c * KLO : (c + 1) * KLO, :] = term
    scattered = seg_scatter(terms, seg_slots, lane_hot, table)
    seen = seg_image(after, seg_diag, seg_chain, scattered)
    for c in range(3):
        residual_segs_out[c : c + 1, :] = active * (grad[c] - seen[c])
    halo.wait_recv()
    add_rims(image, halo, column)
    loads[3].wait()
    for c in range(3):
        grad_here[c] = grad_here[c] - image[c, 1 : NZ + 1]
    store = pltpu.make_async_copy(grad_here, rest_out, store_sem)
    store.start()
    push_exchange.wait_recv()
    unpack(came, pulls, 3)
    to_places(pulls, 3, hots, total, ordered)
    store.wait()
    late_exchange.wait_send()
    pull_exchange.wait_send()
    push_exchange.wait_send()
    halo.wait_send()


def fourth_kernel(
    starts, ordered, rest, index_rows, adjoint_segs, residual_segs,
    residual_out, adjoint_segs_out, residual_segs_out,
    scattered,
):
    adjoint_segs_out[...] = adjoint_segs[...]
    residual_segs_out[...] = residual_segs[...]
    scattered[...] = jnp.zeros_like(scattered)

    def act(b, j, n):
        row, lane = chunk_hots(index_rows, j, n, b)
        scatter_chunk(ordered, 0, j, n, row, lane, scattered, b)

    each_chunk([starts[b] for b in range(BUCKETS + 2)], act)
    for b in range(BUCKETS):
        for c in range(3):
            at = slice(8 * b, 8 * b + 8)
            residual_out[c, at] = rest[c, at] - scattered_cells(scattered, b, c)


def shape(*dims, kind=F32):
    return jax.ShapeDtypeStruct(dims, kind)


def vmem(*dims, kind=F32):
    return pltpu.VMEM(dims, kind)


def rim_scratch():
    return [
        vmem(2, 3, NZ, CY),
        vmem(2, 3, NZ, CY),
        vmem(2, 3, ROWS),
        vmem(2, 3, ROWS),
        vmem(3, ROWS, CY),
    ]


def call(kernel, outs, ins, scratch, number=None, in_specs=None, out_specs=None):
    params = dict(vmem_limit_bytes=58 << 20)
    if number is not None:
        params.update(collective_id=number, has_side_effects=True)
    return pl.pallas_call(
        kernel,
        out_shape=outs,
        in_specs=in_specs or [VMEM] * len(ins),
        out_specs=out_specs or [VMEM] * len(outs),
        scratch_shapes=scratch,
        compiler_params=pltpu.CompilerParams(**params),
        name=kernel.__name__,
    )(*ins)


def shards(
    grad_cells, grad_segs, cell_diag, cell_off, seg_diag, seg_chain, seg_len,
    perf_device, perf_local, perf_seg, perf_blocks,
):
    dma = pltpu.SemaphoreType.DMA
    smem = pl.BlockSpec(memory_space=pltpu.SMEM)
    lens = seg_len.reshape(1, 32)
    chain = seg_chain.transpose(1, 2, 0, 3)
    cells = shape(3, NZ, CX, CY)
    segs = shape(3, SEGS)
    tile = vmem(3, NZ, CX, CY)
    diag_tile = vmem(3, 3, NZ, CX, CY)
    off_tile = vmem(6, 3, 3, NZ, CX, CY)
    image = vmem(3, NZ + 2, CX, CY)
    came, seg_slots, push_blocks, pull_blocks, adjoint, rest, adjoint_segs = call(
        first_kernel,
        [
            shape(ND, KHI, ND), shape(KLO, WIDE), shape(9 * KLO, WIDE), shape(9 * KLO, WIDE),
            cells, cells, segs,
        ],
        [
            grad_cells, grad_segs, cell_diag, cell_off, seg_diag, lens,
            perf_device.reshape(1, PERFS), perf_local.reshape(1, PERFS),
            perf_seg.reshape(1, PERFS), perf_blocks.transpose(1, 2, 0, 3),
        ],
        [
            vmem(WIDE, PERFS, kind=BF16),
            vmem(KLO, PERFS),
            vmem(22 * KLO, 512, kind=BF16),
            vmem(22 * KLO, WIDE),
            vmem(11 * KLO, WIDE),
            vmem(9 * KLO, WIDE),
            vmem(128, SLOTS, kind=BF16),
            vmem(48, 128),
            vmem(3 * KLO, WIDE),
            vmem(ND, KHI, ND),
            off_tile,
            diag_tile,
            tile,
            tile,
            image,
        ]
        + rim_scratch()
        + [dma((3,)), dma((5,)), dma, dma, dma, dma((4,)), dma((4,))],
        0,
        [ANY, VMEM, ANY, ANY] + [VMEM] * 6,
        [VMEM] + [ANY] * 5 + [VMEM],
    )
    adjoint, pulled, index_rows, place, starts = call(
        second_kernel,
        [
            cells, shape(6 * CROWS, LANES), shape(CROWS, LANES),
            shape(KLO, WIDE, kind=jnp.int32), shape(8, kind=jnp.int32),
        ],
        [came, cell_diag, adjoint, rest],
        [
            vmem(4 * KLO, WIDE),
            vmem(8 * CROWS, LANES),
            vmem(4 * CROWS, LANES),
            vmem(BUCKETS, 6 * HALF, 2 * BROWS, kind=BF16),
            vmem(BUCKETS, 3 * HALF, 2 * BROWS),
            diag_tile,
            tile,
            tile,
            dma((3,)),
            dma,
        ],
        None,
        [VMEM] + [ANY] * 3,
        [ANY] + [VMEM] * 3 + [smem],
    )
    ordered, rest, adjoint_segs, residual_segs = call(
        third_kernel,
        [shape(3 * CROWS, LANES), cells, segs, segs],
        [
            pulled, place, grad_cells, adjoint, cell_diag, cell_off,
            grad_segs, adjoint_segs, seg_diag, chain, lens, seg_slots, push_blocks, pull_blocks,
        ],
        [
            vmem(LANES, SLOTS, kind=BF16),
            vmem(CROWS, SLOTS),
            vmem(6 * CROWS, LANES),
            vmem(ND, KHI, ND),
            vmem(ND, KHI, ND),
            vmem(ND, KHI, ND),
            vmem(ND, KHI, ND),
            vmem(ND, KHI, ND),
            vmem(ND, KHI, ND),
            vmem(8 * KLO, WIDE),
            vmem(3 * KLO, WIDE),
            vmem(128, SLOTS, kind=BF16),
            vmem(48, 128),
            vmem(3 * KLO, WIDE),
            off_tile,
            diag_tile,
            tile,
            tile,
            image,
        ]
        + rim_scratch()
        + [dma((4,)), dma, dma((3,)), dma((3,)), dma((3,)), dma((4,)), dma((4,))],
        1,
        [VMEM] * 2 + [ANY] * 4 + [VMEM] * 8,
        [VMEM, ANY, VMEM, VMEM],
    )
    residual, adjoint_segs, residual_segs = call(
        fourth_kernel,
        [cells, segs, segs],
        [starts, ordered, rest, index_rows, adjoint_segs, residual_segs],
        [vmem(BUCKETS, 3 * HALF, 2 * BROWS)],
        None,
        [smem] + [VMEM] * 5,
    )
    return adjoint, adjoint_segs, residual, residual_segs


def solution(mesh):
    in_specs = (
        P(None, None, "gx", "gy"),
        P(None, ("gx", "gy")),
        P(None, None, None, "gx", "gy"),
        P(None, None, None, None, "gx", "gy"),
        P(None, None, ("gx", "gy")),
        P(None, None, None, ("gx", "gy")),
        P(("gx", "gy")),
        P(("gx", "gy"), None),
        P(("gx", "gy")),
        P(("gx", "gy")),
        P(None, None, None, ("gx", "gy")),
    )
    out_specs = (
        P(None, None, "gx", "gy"),
        P(None, ("gx", "gy")),
        P(None, None, "gx", "gy"),
        P(None, ("gx", "gy")),
    )
    return jax.shard_map(shards, mesh=mesh, in_specs=in_specs, out_specs=out_specs, check_vma=False)
```
